128 devices in a mesh: ctx: 32 (over y, z, core), head: 4 (over x).
Axes of the slice: x: 4, y: 4, z: 4, core: 2. Of those that a mesh axis runs over, the one named last changes fastest.
Arguments:
- query_latent: bfloat16 [4096, 128, 576], P('ctx', 'head'), may hold values from -80 to 80
- d_out: bfloat16 [4096, 128, 512], P('ctx', 'head'), may hold values from -6 to 6
- latent: bfloat16 [65536, 576], P('ctx'), may hold values from -20 to 20
- index_query: bfloat16 [4096, 64, 128], P('ctx', 'head'), may hold values from -8 to 8
- index_weight: float32 [4096, 64], P('ctx', 'head'), may hold values from -3 to 3
- index_key: bfloat16 [65536, 128], P('ctx'), may hold values from -6 to 6
- kl_scale: float32 [4096], P('ctx'), may hold values from 16 to 64
- history: int32 [64, 14], P('ctx'), may hold values from 32 to 959, as said below
- diag_block: int32 [64], P('ctx'), may hold values from 960 to 1023, as said below
Outputs:
- d_query: bfloat16 [4096, 128, 576], P('ctx', 'head')
- d_latent: bfloat16 [65536, 576], P('ctx')
- d_index_query: bfloat16 [4096, 64, 128], P('ctx', 'head')
- d_index_weight: float32 [4096, 64], P('ctx', 'head')
- d_index_key: bfloat16 [65536, 128], P('ctx')
The draws below stay inside these ranges and needn't reach their ends.
Inputs may be any that keep to these rules, and one draw needn't show every extreme that they name: `history`: only blocks of ctx shards 1 to 29. Within the lists of one ctx shard's 2 query blocks no block appears twice and no ctx shard's blocks appear more than 2 times; some shard's appear exactly 2 times. `diag_block`: all query blocks together name each of the last 64 blocks once.
All inputs are finite; a program needn't handle non-finite values.
Results may differ from the reference program's by a relative error of at most 0.0051.
Values may be sent and summed in bfloat16 or wider, within the bound.
A program may use at most 192 MiB of HBM per device.

```python
import math
import jax
import jax.numpy as jnp
from jax import lax

H = 128
KVR = 512
ROPE = 64
IH = 64
ID = 128
BS = 64
SEL = 16
BLK_DEV = 32
DL = 576
QB_DEV = 2
QUERIES = 4096
QBLOCKS = 64
NBLK = 1024
CONTEXT = 65536
O_HIST = 30
HCAP = 2


def slab_order(key):
    inner_key = jax.random.fold_in(key, 101)
    return (NBLK - QBLOCKS + jax.random.permutation(inner_key, QBLOCKS)).astype(jnp.int32)


def draw_diag_block(key, part):
    own_blocks = slab_order(key)
    return own_blocks


def draw_history(key, part):
    key = jax.random.fold_in(key, 7)
    shard_total = NBLK // BLK_DEV
    pick_total = QB_DEV * (SEL - 2)

    def per_shard(shard_key):
        key_order, key_full, key_mix = jax.random.split(shard_key, 3)
        owner_order = (jax.random.permutation(key_order, O_HIST - 1) + 1).astype(jnp.int32)
        deck = jnp.arange(pick_total)
        owners = owner_order[deck // HCAP]
        slot_ranks = deck % HCAP
        mixing = jax.random.permutation(key_mix, pick_total)
        owners = owners[mixing]
        slot_ranks = slot_ranks[mixing]

        def full_perm(perm_key):
            return jax.random.permutation(perm_key, BLK_DEV)
        perm_full = jax.vmap(full_perm)(jax.random.split(key_full, O_HIST))
        local_ids = perm_full[owners, slot_ranks]
        return (owners * BLK_DEV + local_ids).reshape(QB_DEV, SEL - 2)
    shard_keys = jax.random.split(key, shard_total)
    return jax.vmap(per_shard)(shard_keys).reshape(QBLOCKS, SEL - 2).astype(jnp.int32)


def draw_query_latent(key, part):
    key = jax.random.fold_in(key, 11)
    key_base = jax.random.fold_in(key, 0)
    values = jnp.clip(jax.random.normal(key_base, (QUERIES, H, DL), jnp.float32), -6.0, 6.0) * 0.87
    return values.astype(jnp.bfloat16)


def draw_latent(key, part):
    key = jax.random.fold_in(key, 13)
    key_base = jax.random.fold_in(key, 0)
    values = jnp.clip(jax.random.normal(key_base, (CONTEXT, DL), jnp.float32), -6.0, 6.0)
    return values.astype(jnp.bfloat16)


def draw_index_key(key, part):
    key = jax.random.fold_in(key, 17)
    values = jnp.clip(jax.random.normal(key, (CONTEXT, ID), jnp.float32), -6.0, 6.0)
    return values.astype(jnp.bfloat16)


def draw_index_query(key, part):
    key = jax.random.fold_in(key, 19)
    values = jnp.clip(jax.random.normal(key, (QUERIES, IH, ID), jnp.float32), -6.0, 6.0)
    return values.astype(jnp.bfloat16)


def draw_index_weight(key, part):
    key = jax.random.fold_in(key, 23)
    values = jnp.clip(jax.random.normal(key, (QUERIES, IH), jnp.float32), -6.0, 6.0) * 0.5
    return values


def levels(rng, extent, cuts, low, largest):
    def one(position, shards_of):
        steps = jax.random.uniform(jax.random.fold_in(jax.random.fold_in(rng, 6), position), (shards_of,), jnp.float32, low / len(cuts), largest / len(cuts))
        return jnp.repeat(jnp.exp(steps), extent[position] // shards_of).reshape((-1,) + (1,) * (len(extent) - position - 1))

    loudness = one(*cuts[0])
    for cut in cuts[1:]:
        loudness = loudness * one(*cut)
    return loudness


def gaussian(rng, dims, width, most, cuts=(), held_as=jnp.bfloat16):
    entries = width * jax.random.normal(rng, dims, jnp.float32)
    if cuts:
        entries = entries * levels(rng, dims, cuts, -0.22, 0.18)
    return jnp.clip(entries, -most, most).astype(held_as)


def setup_inputs(seed: int = 0) -> dict:
    splits = jax.random.split(jax.random.key(seed), 10)
    return {
        "query_latent": draw_query_latent(jax.random.fold_in(splits[9], 71), 0),
        "d_out": gaussian(splits[1], (QUERIES, H, KVR), 1.0, 6.0, ((0, 32), (1, 4))),
        "latent": draw_latent(jax.random.fold_in(splits[9], 71), 0),
        "index_query": draw_index_query(jax.random.fold_in(splits[9], 71), 0),
        "index_weight": draw_index_weight(jax.random.fold_in(splits[9], 71), 0),
        "index_key": draw_index_key(jax.random.fold_in(splits[9], 71), 0),
        "kl_scale": jnp.clip(jnp.exp(math.log(64.0) - 1.3862944 * jax.random.uniform(splits[6], (QUERIES,), jnp.float32) ** levels(splits[6], (QUERIES,), ((0, 32),), -0.2, 0.2)), 16.0, 64.0),
        "history": draw_history(jax.random.fold_in(splits[9], 71), 0),
        "diag_block": draw_diag_block(jax.random.fold_in(splits[9], 71), 0),
    }


score_scale = 192.0 ** -0.5


def silu_slope(values):
    sig_vals = jax.nn.sigmoid(values)
    return sig_vals * (1.0 + values * (1.0 - sig_vals))


def attend_block(query_rows, grad_rows, lat_keys, idx_rows, idx_weights, idx_keys, loss_rows):
    key_count = lat_keys.shape[0]
    head_total = query_rows.shape[1]
    idx_total = idx_rows.shape[1]
    q_flat = query_rows.reshape(BS * head_total, DL)
    g_flat = grad_rows.reshape(BS * head_total, KVR)
    query_pos = jnp.arange(BS * head_total) // head_total
    key_pos = jnp.arange(key_count) - (key_count - BS)
    visible = key_pos[None, :] <= query_pos[:, None]
    scores = jnp.dot(q_flat, lat_keys.T, preferred_element_type=jnp.float32) * score_scale
    scores = jnp.where(visible, scores, -jnp.inf)
    row_top = jnp.max(scores, axis=1, keepdims=True)
    row_exp = jnp.exp(scores - row_top)
    prob_rows = row_exp / jnp.sum(row_exp, axis=1, keepdims=True)
    probs_low = prob_rows.astype(jnp.bfloat16)
    d_probs = jnp.dot(g_flat, lat_keys[:, :KVR].T, preferred_element_type=jnp.float32)
    row_delta = jnp.sum(prob_rows * d_probs, axis=1, keepdims=True)
    d_scores = (prob_rows * (d_probs - row_delta) * score_scale).astype(jnp.bfloat16)
    d_query = jnp.dot(d_scores, lat_keys, preferred_element_type=jnp.float32).astype(jnp.bfloat16)
    key_grad = jnp.dot(d_scores.T, q_flat, preferred_element_type=jnp.float32)
    value_grad = jnp.dot(probs_low.T, g_flat, preferred_element_type=jnp.float32)
    key_grad = key_grad + jnp.pad(value_grad, ((0, 0), (0, ROPE)))
    target = jnp.sum(prob_rows.reshape(BS, head_total, key_count), axis=1) / head_total
    iq_flat = idx_rows.reshape(BS * idx_total, ID)
    logits = jnp.dot(iq_flat, idx_keys.T, preferred_element_type=jnp.float32) * (ID ** -0.5)
    logit_cube = logits.reshape(BS, idx_total, key_count)
    gated_vals = jax.nn.silu(logit_cube)
    index_score = jnp.sum(idx_weights[:, :, None] * gated_vals, axis=1)
    near_mask = visible[::head_total]
    index_score = jnp.where(near_mask, index_score, -jnp.inf)
    row_peak = jnp.max(index_score, axis=1, keepdims=True)
    index_exp = jnp.exp(index_score - row_peak)
    index_prob = index_exp / jnp.sum(index_exp, axis=1, keepdims=True)
    d_score = loss_rows[:, None] * (index_prob - target)
    d_weight = jnp.sum(d_score[:, None, :] * gated_vals, axis=2)
    d_logit = (d_score[:, None, :] * idx_weights[:, :, None] * silu_slope(logit_cube) * (ID ** -0.5)).astype(jnp.bfloat16)
    d_logit = d_logit.reshape(BS * idx_total, key_count)
    d_iq = jnp.dot(d_logit, idx_keys, preferred_element_type=jnp.float32).astype(jnp.bfloat16)
    ikey_grad = jnp.dot(d_logit.T, iq_flat, preferred_element_type=jnp.float32)
    return d_query.reshape(BS, head_total, DL), key_grad, d_iq.reshape(BS, idx_total, ID), d_weight, ikey_grad


def reference(query_latent, d_out, latent, index_query, index_weight, index_key, kl_scale, history, diag_block):
    n_blocks = CONTEXT // BS
    lat_blocks = latent.reshape(n_blocks, BS, DL)
    key_blocks = index_key.reshape(n_blocks, BS, ID)
    sink_col = jnp.zeros((QBLOCKS, 1), jnp.int32)
    key_lists = jnp.concatenate([sink_col, history.astype(jnp.int32), diag_block.astype(jnp.int32)[:, None]], axis=1)

    def per_block(block_items):
        q_rows, g_rows, iq_rows, iw_rows, loss_rows, picks = block_items
        lat_keys = jnp.take(lat_blocks, picks, axis=0).reshape(SEL * BS, DL)
        idx_keys = jnp.take(key_blocks, picks, axis=0).reshape(SEL * BS, ID)
        return attend_block(q_rows, g_rows, lat_keys, iq_rows, iw_rows, idx_keys, loss_rows)

    stacked = (query_latent.reshape(QBLOCKS, BS, H, DL), d_out.reshape(QBLOCKS, BS, H, KVR),
               index_query.reshape(QBLOCKS, BS, IH, ID), index_weight.reshape(QBLOCKS, BS, IH),
               kl_scale.reshape(QBLOCKS, BS), key_lists)
    d_query, key_grads, d_iq, d_weight, ikey_grads = lax.map(per_block, stacked)
    flat_ids = key_lists.reshape(-1)
    lat_total = jnp.zeros((n_blocks, BS, DL), jnp.float32).at[flat_ids].add(key_grads.reshape(QBLOCKS * SEL, BS, DL))
    key_total = jnp.zeros((n_blocks, BS, ID), jnp.float32).at[flat_ids].add(ikey_grads.reshape(QBLOCKS * SEL, BS, ID))
    return (d_query.reshape(QUERIES, H, DL), lat_total.reshape(CONTEXT, DL).astype(jnp.bfloat16),
            d_iq.reshape(QUERIES, IH, ID), d_weight.reshape(QUERIES, IH),
            key_total.reshape(CONTEXT, ID).astype(jnp.bfloat16))
```

```python
from functools import partial

import jax
import jax.numpy as jnp
from jax import lax
from jax.experimental import pallas as pl
from jax.experimental.pallas import tpu as pltpu
from jax.sharding import PartitionSpec as P

MESH = pl.DeviceIdType.MESH
f32, bf16, i32 = jnp.float32, jnp.bfloat16, jnp.int32

SCORE_SCALE = 192.0 ** (-0.5)
LOG2E = 1.4426950408889634
BLOCK = 64
SLOTS = 2
LANES = 128


def iota(shape, dim):
    return lax.broadcasted_iota(i32, shape, dim)


def one_hot(index_rows, width):
    wide = jnp.concatenate([index_rows] * (width // LANES), axis=1)
    hit = wide == iota(wide.shape, 1)
    return jnp.where(hit, 1.0, 0.0).astype(bf16)


def slot_rows(ids, sel, n_ctx, quarter):
    @pl.loop(0, n_ctx)
    def _(r):
        for s in range(SLOTS):
            row = jnp.broadcast_to(ids[r, s : s + 1, :], (quarter, LANES))
            start = pl.multiple_of((r * SLOTS + s) * quarter, quarter)
            sel[pl.ds(start, quarter), :] = row * quarter + iota((quarter, LANES), 0)


def greet(n_ctx, n_head, with_ctx):
    me, col = lax.axis_index("ctx"), lax.axis_index("head")
    barrier = pltpu.get_barrier_semaphore()
    count = 0
    if with_ctx:

        @pl.loop(1, n_ctx)
        def _(d):
            pl.semaphore_signal(
                barrier, inc=1, device_id=(lax.rem(me + d, n_ctx), col), device_id_type=MESH
            )

        count += n_ctx - 1
    for d in range(1, n_head):
        pl.semaphore_signal(
            barrier, inc=1, device_id=(me, lax.rem(col + d, n_head)), device_id_type=MESH
        )
    pl.semaphore_wait(barrier, count + n_head - 1)


def ctx_copy(src, dst, send_sem, recv_sem, d, n_ctx):
    me, col = lax.axis_index("ctx"), lax.axis_index("head")
    to = lax.rem(me + d, n_ctx)
    return pltpu.make_async_remote_copy(
        src_ref=src.at[to],
        dst_ref=dst.at[me],
        send_sem=send_sem.at[d],
        recv_sem=recv_sem.at[d],
        device_id=(to, col),
        device_id_type=MESH,
    )


def ctx_arrival(src, dst, send_sem, recv_sem, d, n_ctx):
    me, col = lax.axis_index("ctx"), lax.axis_index("head")
    to = lax.rem(me + d, n_ctx)
    come = lax.rem(me - d + n_ctx, n_ctx)
    return pltpu.make_async_remote_copy(
        src_ref=src.at[to],
        dst_ref=dst.at[come],
        send_sem=send_sem.at[d],
        recv_sem=recv_sem.at[d],
        device_id=(to, col),
        device_id_type=MESH,
    )


def exchange_ctx(src, dst, send_sem, recv_sem, n_ctx):
    @pl.loop(1, n_ctx)
    def _(d):
        ctx_copy(src, dst, send_sem, recv_sem, d, n_ctx).start()


def finish_ctx(src, dst, send_sem, recv_sem, n_ctx):
    @pl.loop(1, n_ctx)
    def _(d):
        arrival = ctx_arrival(src, dst, send_sem, recv_sem, d, n_ctx)
        arrival.wait_recv()
        arrival.wait_send()


def head_copy(src, dst, send_sem, recv_sem, d, n_head):
    me, col = lax.axis_index("ctx"), lax.axis_index("head")
    return pltpu.make_async_remote_copy(
        src_ref=src,
        dst_ref=dst,
        send_sem=send_sem,
        recv_sem=recv_sem,
        device_id=(me, lax.rem(col + d, n_head)),
        device_id_type=MESH,
    )


def gather_kernel(
    n_ctx, n_head, ask, want, lat, key, k_out, ids,
    latq, keyq, sel, send, recv, comp,
    load_sem, ask_send, ask_recv, a_send, a_recv, x_send, x_recv,
):
    me, col = lax.axis_index("ctx"), lax.axis_index("head")
    blocks, quarter, lat_width = latq.shape
    entries = comp.shape[0]
    mine = pl.ds(pl.multiple_of(col * quarter, quarter), quarter)
    load_lat = pltpu.make_async_copy(lat.at[:, mine], latq, load_sem.at[0])
    load_key = pltpu.make_async_copy(key.at[:, mine], keyq, load_sem.at[1])
    load_lat.start()
    load_key.start()
    greet(n_ctx, n_head, True)

    exchange_ctx(ask, ids, ask_send, ask_recv, n_ctx)
    ids[me] = ask[me]
    load_lat.wait()
    load_key.wait()
    finish_ctx(ask, ids, ask_send, ask_recv, n_ctx)
    slot_rows(ids, sel, n_ctx, quarter)

    per = 256 // (SLOTS * quarter)

    @pl.loop(0, n_ctx // per)
    def _(i):
        start = pl.multiple_of(i * 256, 256)
        pick = one_hot(sel[pl.ds(start, 256), :], blocks * quarter)
        lat_rows = jnp.dot(
            pick, latq[...].reshape(blocks * quarter, lat_width), preferred_element_type=f32
        )
        key_rows = jnp.dot(
            pick, keyq[...].reshape(blocks * quarter, LANES), preferred_element_type=f32
        )
        pad = jnp.zeros((256, 640 - lat_width), f32)
        rows = jnp.concatenate([lat_rows, pad, key_rows], axis=1).astype(bf16)
        send[pl.ds(i * per, per)] = rows.reshape(per, SLOTS * quarter, 768)

    exchange_ctx(send, recv, a_send, a_recv, n_ctx)
    recv[me] = send[me]
    finish_ctx(send, recv, a_send, a_recv, n_ctx)

    @pl.loop(0, entries * quarter // 256)
    def _(i):
        start = pl.multiple_of(i * 256, 256)
        pick = one_hot(want[pl.ds(start, 256), :], n_ctx * SLOTS * quarter)
        rows = jnp.dot(
            pick, recv[...].reshape(n_ctx * SLOTS * quarter, 768), preferred_element_type=f32
        ).astype(bf16)
        comp[pl.ds(i * (256 // quarter), 256 // quarter)] = rows.reshape(256 // quarter, quarter, 768)

    def place(d):
        return head_copy(comp, k_out.at[:, col], x_send.at[d], x_recv.at[d], d, n_head)

    for d in range(1, n_head):
        place(d).start()
    k_out[:, col] = comp[...]
    for d in range(1, n_head):
        come = lax.rem(col - d + n_head, n_head)
        arrival = head_copy(comp, k_out.at[:, come], x_send.at[d], x_recv.at[d], d, n_head)
        arrival.wait_recv()
        arrival.wait_send()


def main_kernel(
    n_head, head_total, q_hbm, g_hbm, keys, iq, iw, kl, dq_hbm, diq, dw, tq,
    qbuf, gbuf, dqbuf, kt, acc, ik_acc, logit, ex, exr, dsb, ktb, rsr, ikb, ikr,
    q_sem, g_sem, dq_sem, ex_send, ex_recv, ds_send, ds_recv, rs_send, rs_recv, ik_send, ik_recv,
):
    me, col = lax.axis_index("ctx"), lax.axis_index("head")
    groups, key_count, _ = keys.shape
    lat_width, val_width = qbuf.shape[1], gbuf.shape[1]
    heads = qbuf.shape[0] // (groups * BLOCK)
    idx_heads = iq.shape[0] // (groups * BLOCK)
    span = BLOCK // n_head
    chunk = span * heads
    sub = 256
    idx_scale = LANES ** (-0.5)
    exp_scale = SCORE_SCALE * LOG2E

    def q_load(n):
        rows = pl.ds(pl.multiple_of(n * chunk, chunk), chunk)
        return pltpu.make_async_copy(q_hbm.at[rows], qbuf.at[rows], q_sem.at[n])

    def g_load(n):
        rows = pl.ds(pl.multiple_of(n * chunk, chunk), chunk)
        return pltpu.make_async_copy(g_hbm.at[rows], gbuf.at[rows], g_sem.at[n])

    def dq_store(n):
        rows = pl.ds(pl.multiple_of(n * chunk, chunk), chunk)
        return pltpu.make_async_copy(dqbuf.at[rows], dq_hbm.at[rows], dq_sem.at[n])

    for n in range(groups * n_head):
        q_load(n).start()
        g_load(n).start()
    greet(1, n_head, False)

    @pl.loop(0, groups)
    def _(g):
        kt[...] = keys[g].T
        acc[...] = jnp.zeros_like(acc)

        @pl.loop(0, n_head)
        def _(c):
            n = g * n_head + c
            q_load(n).wait()
            g_load(n).wait()
            for half in range(chunk // sub):
                start = pl.multiple_of(n * chunk + half * sub, sub)
                rows = pl.ds(start, sub)
                qc, gc = qbuf[rows, :], gbuf[rows, :]
                s = jnp.dot(qc, kt[:lat_width, :], preferred_element_type=f32)
                edge = key_count - LANES
                first = c * span + half * (sub // heads)
                q_pos = first + iota((sub, LANES), 0) // heads
                k_pos = iota((sub, LANES), 1) - (LANES - BLOCK)
                tail = jnp.where(k_pos <= q_pos, s[:, edge:], -jnp.inf)
                s = jnp.concatenate([s[:, :edge], tail], axis=1)
                top = jnp.max(s, axis=1, keepdims=True)
                e = jnp.exp2((s - top) * exp_scale)
                p = e * (1.0 / jnp.sum(e, axis=1, keepdims=True))
                p_low = p.astype(bf16)
                dp = jnp.dot(gc, kt[:val_width, :], preferred_element_type=f32)
                delta = jnp.sum(p * dp, axis=1, keepdims=True)
                ds = (p * (dp - delta) * SCORE_SCALE).astype(bf16)
                dq = jnp.dot(ds, keys[g, :, :lat_width], preferred_element_type=f32)
                dqbuf[rows, :] = dq.astype(bf16)
                both = jnp.concatenate([ds, p_low], axis=0)
                q_t, g_t = qc.T, gc.T
                lhs = jnp.concatenate([q_t[:val_width], g_t], axis=1)
                acc[:val_width, :] += jnp.dot(lhs, both, preferred_element_type=f32)
                acc[val_width:lat_width, :] += jnp.dot(
                    q_t[val_width:], ds, preferred_element_type=f32
                )
                per = sub // heads
                ex[g, c, 0, half * per : (half + 1) * per, :] = jnp.sum(
                    p.reshape(per, heads, key_count), axis=1
                )
            dq_store(n).start()

        @pl.loop(0, BLOCK * idx_heads // sub)
        def _(c):
            start = pl.multiple_of((g * BLOCK * idx_heads) + c * sub, sub)
            rows = pl.ds(start, sub)
            v = jnp.dot(iq[rows, :], kt[640:, :], preferred_element_type=f32) * idx_scale
            logit[rows, :] = v
            silu = v / (1.0 + jnp.exp(-v))
            part = silu * iw[rows, 0:1]
            ex[g, c, 1] = jnp.sum(part.reshape(sub // idx_heads, idx_heads, key_count), axis=1)

        for d in range(1, n_head):
            to = lax.rem(col + d, n_head)
            head_copy(
                ex.at[g, to], exr.at[g, d - 1], ex_send.at[g, d - 1], ex_recv.at[g, d - 1], d, n_head
            ).start()

        for j in range(key_count // LANES):
            part = acc[:, j * LANES : (j + 1) * LANES].astype(bf16).T
            ktb[g, 2 * j : 2 * j + 2] = part.reshape(2, n_head, span, 640)
        for d in range(1, n_head):
            to = lax.rem(col + d, n_head)
            head_copy(
                ktb.at[g, :, to], rsr.at[g, d - 1], rs_send.at[g, d - 1], rs_recv.at[g, d - 1], d, n_head
            ).start()

    @pl.loop(0, groups)
    def _(g):
        for d in range(1, n_head):
            to = lax.rem(col + d, n_head)
            arrival = head_copy(
                ex.at[g, to], exr.at[g, d - 1], ex_send.at[g, d - 1], ex_recv.at[g, d - 1], d, n_head
            )
            arrival.wait_recv()
            arrival.wait_send()
        total = ex[g, col]
        for d in range(1, n_head):
            total = total + exr[g, d - 1]
        target = total[0] * (1.0 / head_total)
        q_pos = col * span + iota((span, key_count), 0)
        k_pos = iota((span, key_count), 1) - (key_count - BLOCK)
        score = jnp.where(k_pos <= q_pos, total[1], -jnp.inf)
        e = jnp.exp(score - jnp.max(score, axis=1, keepdims=True))
        prob = e / jnp.sum(e, axis=1, keepdims=True)
        k_rows = pl.ds(pl.multiple_of(g * BLOCK + col * span, span), span)
        dsb[g, col] = kl[k_rows, 0:1] * (prob - target)
        for d in range(1, n_head):
            head_copy(
                dsb.at[g, col], dsb.at[g, col], ds_send.at[g, d - 1], ds_recv.at[g, d - 1], d, n_head
            ).start()

    @pl.loop(0, groups)
    def _(g):
        for d in range(1, n_head):
            come = lax.rem(col - d + n_head, n_head)
            arrival = head_copy(
                dsb.at[g, col], dsb.at[g, come], ds_send.at[g, d - 1], ds_recv.at[g, d - 1], d, n_head
            )
            arrival.wait_recv()
            arrival.wait_send()
        ik_acc[...] = jnp.zeros_like(ik_acc)

        @pl.loop(0, BLOCK * idx_heads // sub)
        def _(c):
            start = pl.multiple_of((g * BLOCK * idx_heads) + c * sub, sub)
            rows = pl.ds(start, sub)
            v = logit[rows, :]
            sig = 1.0 / (1.0 + jnp.exp(-v))
            d_score = dsb[g, c]
            d_wide = jnp.broadcast_to(
                d_score[:, None, :], (sub // idx_heads, idx_heads, key_count)
            ).reshape(sub, key_count)
            silu = v * sig
            dw[rows, :] = jnp.sum(d_wide * silu, axis=1, keepdims=True)
            slope = sig + silu * (1.0 - sig)
            grad = (d_wide * (iw[rows, 0:1] * idx_scale) * slope).astype(bf16)
            iqc = iq[rows, :]
            diq[rows, :] = jnp.dot(grad, keys[g, :, 640:], preferred_element_type=f32).astype(bf16)
            ik_acc[...] += jnp.dot(iqc.T, grad, preferred_element_type=f32)

        for j in range(key_count // LANES):
            part = ik_acc[:, j * LANES : (j + 1) * LANES].astype(bf16).T
            ikb[g, 2 * j : 2 * j + 2] = part.reshape(2, n_head, span, LANES)
        for d in range(1, n_head):
            to = lax.rem(col + d, n_head)
            head_copy(
                ikb.at[g, :, to], ikr.at[g, d - 1], ik_send.at[g, d - 1], ik_recv.at[g, d - 1], d, n_head
            ).start()

    picks = key_count // BLOCK

    @pl.loop(0, groups)
    def _(g):
        for d in range(1, n_head):
            to = lax.rem(col + d, n_head)
            for arrival in (
                head_copy(
                    ktb.at[g, :, to], rsr.at[g, d - 1], rs_send.at[g, d - 1], rs_recv.at[g, d - 1], d, n_head
                ),
                head_copy(
                    ikb.at[g, :, to], ikr.at[g, d - 1], ik_send.at[g, d - 1], ik_recv.at[g, d - 1], d, n_head
                ),
            ):
                arrival.wait_recv()
                arrival.wait_send()
        lat_sum = ktb[g, :, col].astype(f32)
        key_sum = ikb[g, :, col].astype(f32)
        for d in range(1, n_head):
            lat_sum = lat_sum + rsr[g, d - 1].astype(f32)
            key_sum = key_sum + ikr[g, d - 1].astype(f32)
        tq[g, :, :640] = lat_sum.astype(bf16).reshape(picks * span, 640)
        tq[g, :, 640:] = key_sum.astype(bf16).reshape(picks * span, LANES)

    for n in range(groups * n_head):
        dq_store(n).wait()


def return_kernel(
    n_ctx, n_head, tq, have, ids, out,
    sel, slots, recv, own, a_send, a_recv, x_send, x_recv,
):
    me, col = lax.axis_index("ctx"), lax.axis_index("head")
    blocks, _, quarter, width = out.shape
    rows_in = tq.shape[0]
    per = 256 // (SLOTS * quarter)
    greet(n_ctx, n_head, True)

    @pl.loop(0, n_ctx // per)
    def _(i):
        start = pl.multiple_of(i * 256, 256)
        pick = one_hot(have[pl.ds(start, 256), :], rows_in)
        rows = jnp.dot(pick, tq[...], preferred_element_type=f32).astype(bf16)
        slots[pl.ds(i * per, per)] = rows.reshape(per, SLOTS * quarter, width)

    exchange_ctx(slots, recv, a_send, a_recv, n_ctx)
    recv[me] = slots[me]
    slot_rows(ids, sel, n_ctx, quarter)
    finish_ctx(slots, recv, a_send, a_recv, n_ctx)

    pick = one_hot(sel[...], blocks * quarter)
    total = lax.dot_general(
        pick,
        recv[...].reshape(n_ctx * SLOTS * quarter, width),
        (((0,), (0,)), ((), ())),
        preferred_element_type=f32,
    )
    own[...] = total.astype(bf16).reshape(blocks, quarter, width)

    for d in range(1, n_head):
        head_copy(own, out.at[:, col], x_send.at[d], x_recv.at[d], d, n_head).start()
    out[:, col] = own[...]
    for d in range(1, n_head):
        come = lax.rem(col - d + n_head, n_head)
        arrival = head_copy(own, out.at[:, come], x_send.at[d], x_recv.at[d], d, n_head)
        arrival.wait_recv()
        arrival.wait_send()


VM = pl.BlockSpec(memory_space=pltpu.VMEM)
HB = pl.BlockSpec(memory_space=pl.ANY)
DMA = pltpu.SemaphoreType.DMA


def call(kernel, name, cid, ins, outs, scratch, flops=0):
    return pl.pallas_call(
        kernel,
        name=name,
        in_specs=[spec for spec, _ in ins],
        out_specs=[spec for spec, _ in outs],
        out_shape=[shape for _, shape in outs],
        scratch_shapes=scratch,
        compiler_params=pltpu.CompilerParams(
            collective_id=cid, has_side_effects=True, vmem_limit_bytes=60 * 2**20
        ),
    )(*[value for _, value in ins])


def shards(
    n_ctx, n_head,
    query_latent, d_out, latent, index_query, index_weight, index_key, kl_scale, history, diag_block,
):
    q_dev, heads, lat_width = query_latent.shape
    val_width = d_out.shape[2]
    idx_heads, idx_width = index_query.shape[1:]
    groups, hist = history.shape
    picks = hist + 2
    entries = groups * picks
    key_count = picks * BLOCK
    blk_dev = latent.shape[0] // BLOCK
    quarter = BLOCK // n_head
    slot_total = n_ctx * SLOTS
    width = 768
    shape = jax.ShapeDtypeStruct

    sink = jnp.zeros((groups, 1), i32)
    lists = jnp.concatenate([sink, history, diag_block[:, None]], axis=1).reshape(-1)
    owner, local = lists // blk_dev, lists % blk_dev
    order = jnp.arange(entries)
    earlier = (order[None, :] < order[:, None]) & (owner[None, :] == owner[:, None])
    slot = owner * SLOTS + jnp.sum(earlier.astype(i32), axis=1)
    hits = slot[None, :] == jnp.arange(slot_total)[:, None]
    ask = jnp.sum(jnp.where(hits, local[None, :] + 1, 0), axis=1) - 1
    entry = jnp.sum(jnp.where(hits, order[None, :] + 1, 0), axis=1) - 1
    ask = jnp.pad(ask.reshape(n_ctx, SLOTS), ((0, 0), (0, 8 - SLOTS)), constant_values=-1)
    ask = jnp.broadcast_to(ask[:, :, None], (n_ctx, 8, LANES))

    def lane_rows(ids):
        rows = ids[:, None] * quarter + jnp.arange(quarter)[None, :]
        return jnp.broadcast_to(rows.reshape(-1, 1), (ids.shape[0] * quarter, LANES))

    want, have = lane_rows(slot), lane_rows(entry)

    k_all, ids = call(
        partial(gather_kernel, n_ctx, n_head), "gather_keys", 0,
        [
            (VM, ask), (VM, want),
            (HB, latent.reshape(blk_dev, BLOCK, lat_width)),
            (HB, index_key.reshape(blk_dev, BLOCK, idx_width)),
        ],
        [(VM, shape((entries, n_head, quarter, width), bf16)), (VM, shape((n_ctx, 8, LANES), i32))],
        [
            pltpu.VMEM((blk_dev, quarter, lat_width), bf16),
            pltpu.VMEM((blk_dev, quarter, idx_width), bf16),
            pltpu.VMEM((slot_total * quarter, LANES), i32),
            pltpu.VMEM((n_ctx, SLOTS * quarter, width), bf16),
            pltpu.VMEM((n_ctx, SLOTS * quarter, width), bf16),
            pltpu.VMEM((entries, quarter, width), bf16),
            DMA((2,)), DMA((n_ctx,)), DMA((n_ctx,)), DMA((n_ctx,)), DMA((n_ctx,)),
            DMA((n_head,)), DMA((n_head,)),
        ],
    )

    q_rows, i_rows = q_dev * heads, q_dev * idx_heads
    loads = groups * n_head
    iw = jnp.broadcast_to(index_weight.reshape(i_rows, 1), (i_rows, LANES))
    kl = jnp.broadcast_to(kl_scale[:, None], (q_dev, LANES))
    d_query, d_iq, d_weight, terms = call(
        partial(main_kernel, n_head, heads * n_head), "attend", 1,
        [
            (HB, query_latent.reshape(q_rows, lat_width)),
            (HB, d_out.reshape(q_rows, val_width)),
            (VM, k_all.reshape(groups, key_count, width)),
            (VM, index_query.reshape(i_rows, idx_width)),
            (VM, iw), (VM, kl),
        ],
        [
            (HB, shape((q_rows, lat_width), bf16)),
            (VM, shape((i_rows, idx_width), bf16)),
            (VM, shape((i_rows, 1), f32)),
            (VM, shape((groups, picks * quarter, width), bf16)),
        ],
        [
            pltpu.VMEM((q_rows, lat_width), bf16),
            pltpu.VMEM((q_rows, val_width), bf16),
            pltpu.VMEM((q_rows, lat_width), bf16),
            pltpu.VMEM((width, key_count), bf16),
            pltpu.VMEM((640, key_count), f32),
            pltpu.VMEM((idx_width, key_count), f32),
            pltpu.VMEM((i_rows, key_count), f32),
            pltpu.VMEM((groups, n_head, 2, quarter, key_count), f32),
            pltpu.VMEM((groups, n_head - 1, 2, quarter, key_count), f32),
            pltpu.VMEM((groups, n_head, quarter, key_count), f32),
            pltpu.VMEM((groups, picks, n_head, quarter, 640), bf16),
            pltpu.VMEM((groups, n_head - 1, picks, quarter, 640), bf16),
            pltpu.VMEM((groups, picks, n_head, quarter, idx_width), bf16),
            pltpu.VMEM((groups, n_head - 1, picks, quarter, idx_width), bf16),
            DMA((loads,)), DMA((loads,)), DMA((loads,)),
            DMA((groups, n_head - 1)), DMA((groups, n_head - 1)),
            DMA((groups, n_head - 1)), DMA((groups, n_head - 1)),
            DMA((groups, n_head - 1)), DMA((groups, n_head - 1)),
            DMA((groups, n_head - 1)), DMA((groups, n_head - 1)),
        ],
    )

    (back,) = call(
        partial(return_kernel, n_ctx, n_head), "return_terms", 2,
        [(VM, terms.reshape(entries * quarter, width)), (VM, have), (VM, ids)],
        [(VM, shape((blk_dev, n_head, quarter, width), bf16))],
        [
            pltpu.VMEM((slot_total * quarter, LANES), i32),
            pltpu.VMEM((n_ctx, SLOTS * quarter, width), bf16),
            pltpu.VMEM((n_ctx, SLOTS * quarter, width), bf16),
            pltpu.VMEM((blk_dev, quarter, width), bf16),
            DMA((n_ctx,)), DMA((n_ctx,)), DMA((n_head,)), DMA((n_head,)),
        ],
    )
    back = back.reshape(blk_dev * BLOCK, width)
    return (
        d_query.reshape(q_dev, heads, lat_width),
        back[:, :lat_width],
        d_iq.reshape(q_dev, idx_heads, idx_width),
        d_weight.reshape(q_dev, idx_heads),
        back[:, 640:],
    )


def solution(mesh):
    in_specs = (
        P("ctx", "head", None),
        P("ctx", "head", None),
        P("ctx", None),
        P("ctx", "head", None),
        P("ctx", "head"),
        P("ctx", None),
        P("ctx"),
        P("ctx", None),
        P("ctx"),
    )
    out_specs = (
        P("ctx", "head", None),
        P("ctx", None),
        P("ctx", "head", None),
        P("ctx", "head"),
        P("ctx", None),
    )
    body = partial(shards, mesh.shape["ctx"], mesh.shape["head"])
    return jax.shard_map(body, mesh=mesh, in_specs=in_specs, out_specs=out_specs, check_vma=False)
```

```python
from functools import partial

import jax
import jax.numpy as jnp
from jax import lax
from jax.experimental import pallas as pl
from jax.experimental.pallas import tpu as pltpu
from jax.sharding import PartitionSpec as P

MESH = pl.DeviceIdType.MESH
f32, bf16, i32 = jnp.float32, jnp.bfloat16, jnp.int32

SCORE_SCALE = 192.0 ** (-0.5)
EXP_SCALE = SCORE_SCALE * 1.4426950408889634
BLOCK = 64
SLOTS = 2
LANES = 128
IDX = slice(0, 128)
LAT = slice(128, 704)
VAL = slice(128, 640)
WIDTH = 768
COLS = (slice(0, 384), slice(384, 768))
NH = 4
QT = BLOCK // NH
HC = 8
R = HC * BLOCK
TT = 32


def nn(a, b):
    return jnp.dot(a, b, preferred_element_type=f32)


def nt(a, b):
    return lax.dot_general(a, b, (((1,), (1,)), ((), ())), preferred_element_type=f32)


def tn(a, b):
    return lax.dot_general(a, b, (((0,), (0,)), ((), ())), preferred_element_type=f32)


def iota(shape, dim):
    return lax.broadcasted_iota(i32, shape, dim)


def fold(x, op):
    rows, cols = x.shape
    return op(x.reshape(rows // 8, 8, cols), axis=0)


def row_picks(ids, out, n_ctx, width):
    @pl.loop(0, n_ctx)
    def _(r):
        for s in range(SLOTS):
            row = jnp.broadcast_to(ids[r, s : s + 1, :], (QT, LANES)) * QT + iota((QT, LANES), 0)
            wide = jnp.concatenate([row] * (width // LANES), axis=1)
            hit = jnp.where(wide == iota((QT, width), 1), 1.0, 0.0).astype(bf16)
            out[pl.ds(pl.multiple_of((r * SLOTS + s) * QT, QT), QT), :] = hit


def remote(src, dst, sems, index, to):
    send, recv = sems
    return pltpu.make_async_remote_copy(
        src_ref=src,
        dst_ref=dst,
        send_sem=send.at[index],
        recv_sem=recv.at[index],
        device_id=to,
        device_id_type=MESH,
    )


class CtxExchange:
    def __init__(self, n_ctx, src, dst, sems, group=None):
        self.n, self.src, self.dst, self.sems, self.group = n_ctx, src, dst, sems, group

    def copy(self, d, arrival):
        me, col = lax.axis_index("ctx"), lax.axis_index("head")
        to = lax.rem(me + d, self.n)
        place = lax.rem(me - d + self.n, self.n) if arrival else me
        if self.group is None:
            return remote(self.src.at[to], self.dst.at[place], self.sems, d, (to, col))
        cols = pl.ds(self.group * 384, 384)
        return remote(
            self.src.at[to, :, cols], self.dst.at[place, :, cols], self.sems, (self.group, d), (to, col)
        )

    def start(self):
        @pl.loop(1, self.n)
        def _(d):
            self.copy(d, False).start()

    def finish(self):
        @pl.loop(1, self.n)
        def _(d):
            copy = self.copy(d, True)
            copy.wait_recv()
            copy.wait_send()


class HeadGather:
    def __init__(self, src, dst, sems, index):
        self.src, self.dst, self.sems, self.index = src, dst, sems, index
        me, col = lax.axis_index("ctx"), lax.axis_index("head")
        self.me, self.col = me, col
        self.right, self.left, self.far = (lax.rem(col + d, NH) for d in (1, 3, 2))
        half = src.shape[0] // 2
        self.low, self.high = pl.ds(0, half), pl.ds(half, half)

    def copy(self, kind, member):
        to = (self.me, (self.right, self.left)[kind % 2])
        if kind < 2:
            return remote(self.src, self.dst.at[:, member], self.sems, self.index + (kind,), to)
        part = (self.low, self.high)[kind - 2]
        ref = self.dst.at[part, member]
        return remote(ref, ref, self.sems, self.index + (kind,), to)

    def start(self):
        self.copy(0, self.col).start()
        self.copy(1, self.col).start()

    def forward(self):
        self.copy(0, self.left).wait_recv()
        self.copy(2, self.left).start()
        self.copy(1, self.right).wait_recv()
        self.copy(3, self.right).start()

    def finish(self):
        self.copy(2, self.far).wait_recv()
        self.copy(3, self.far).wait_recv()
        self.copy(0, self.col).wait_send()
        self.copy(1, self.col).wait_send()
        self.copy(2, self.left).wait_send()
        self.copy(3, self.right).wait_send()


def greet(n_ctx):
    me, col = lax.axis_index("ctx"), lax.axis_index("head")
    barrier = pltpu.get_barrier_semaphore()

    @pl.loop(1, n_ctx)
    def _(d):
        pl.semaphore_signal(
            barrier, inc=1, device_id=(lax.rem(me + d, n_ctx), col), device_id_type=MESH
        )

    for d in range(1, NH):
        pl.semaphore_signal(barrier, inc=1, device_id=(me, lax.rem(col + d, NH)), device_id_type=MESH)
    pl.semaphore_wait(barrier, n_ctx + NH - 2)


def whole_kernel(
    n_ctx, head_total,
    ask, entry, q_hbm, g_hbm, lat_hbm, key_hbm, iq, iw, kl,
    dq_hbm, dlat, dkey, diq, dw,
    ids, latr, latq, keyq, pick_own, pick_entry, send, recv, back, comp, keys,
    qp, dqp, gbuf, kt, acc, pacc, s_a, dp_a, ds_a, pl_a, s_b, dp_b, ds_b, pl_b,
    istage, iqr, ex, exr, dsb, dst, ktb, opp_in, merged, fin, ikb, ikr, ik_acc,
    lat_sem, key_sem, q_sem, g_sem, dq_sem,
    ask_send, ask_recv, a_send, a_recv, r_send, r_recv, ag_send, ag_recv, og_send, og_recv,
    ex_send, ex_recv, d_send, d_recv, rs_send, rs_recv, ik_send, ik_recv,
):
    me, col = lax.axis_index("ctx"), lax.axis_index("head")
    right, left, far = (lax.rem(col + d, NH) for d in (1, 3, 2))
    blocks = latq.shape[0]
    lat_width = latq.shape[2]
    groups, picks = keys.shape[0], keys.shape[1]
    key_count = picks * BLOCK
    pairs = qp.shape[1]
    heads = 2 * pairs
    idx_heads = iw.shape[0]
    idx_scale = LANES ** (-0.5)
    slot_rows = n_ctx * SLOTS * QT

    lat_loads = [
        pltpu.make_async_copy(
            lat_hbm.at[:, pl.ds(n * LANES, LANES)], dqp.at[0, n], lat_sem.at[n]
        )
        for n in range(blocks // 2)
    ]
    mine = pl.ds(pl.multiple_of(col * QT, QT), QT)
    key_load = pltpu.make_async_copy(key_hbm.at[:, mine], keyq, key_sem.at[0])
    stages = (ds_a, pl_a, ds_b, pl_b)
    g_loads = [
        pltpu.make_async_copy(
            g_hbm.at[pl.ds(n * key_count, key_count)], stages[n], g_sem.at[n]
        )
        for n in range(4)
    ]
    for copy in lat_loads + [key_load] + g_loads:
        copy.start()
    greet(n_ctx)
    asks = CtxExchange(n_ctx, ask, ids, (ask_send, ask_recv))
    asks.start()
    ids[me] = ask[me]

    for n, copy in enumerate(lat_loads):
        copy.wait()
        latr[...] = dqp[0, n].T.reshape(2, NH, QT, lat_width)
        latq[2 * n : 2 * n + 2] = latr[:, col]

    row_picks(entry, pick_entry, n_ctx, groups * picks * QT)
    key_load.wait()
    q_loads = [
        pltpu.make_async_copy(q_hbm.at[pl.ds(n * pairs, pairs)], dqp.at[n], q_sem.at[n])
        for n in range(2)
    ]
    for copy in q_loads:
        copy.start()
    asks.finish()
    row_picks(ids, pick_own, n_ctx, blocks * QT)

    gathers = [CtxExchange(n_ctx, send, recv, (a_send, a_recv), g) for g in range(2)]
    lat_rows = latq[...].reshape(blocks * QT, lat_width)
    key_rows = keyq[...].reshape(blocks * QT, LANES)
    first = jnp.concatenate([key_rows, lat_rows[:, :256]], axis=1)
    send[:, :, COLS[0]] = nn(pick_own[...], first).astype(bf16).reshape(n_ctx, SLOTS * QT, 384)
    gathers[0].start()
    rest = nn(pick_own[...], lat_rows[:, 256:]).astype(bf16)
    rest = jnp.concatenate([rest, jnp.zeros((slot_rows, WIDTH - LAT.stop), bf16)], axis=1)
    send[:, :, COLS[1]] = rest.reshape(n_ctx, SLOTS * QT, 384)
    gathers[1].start()
    recv[me] = send[me]

    for copy in q_loads:
        copy.wait()

    @pl.loop(0, pairs)
    def _(j):
        one, two = dqp[j // 8, (j % 8) * 2], dqp[j // 8, (j % 8) * 2 + 1]
        qp[0, j] = jnp.concatenate([one[:, :BLOCK], two[:, :BLOCK]], axis=1)
        qp[1, j] = jnp.concatenate([one[:, BLOCK:], two[:, BLOCK:]], axis=1)

    for n in range(4):
        g_loads[n].wait()
        for two in range(2):
            for j in range(2):
                cols = slice((2 * two + j) * LANES, (2 * two + j + 1) * LANES)
                istage[j * key_count : (j + 1) * key_count, :] = stages[n][:, cols].astype(f32)

            @pl.loop(0, heads)
            def _(h):
                for j in range(2):
                    cols = slice((2 * two + j) * LANES, (2 * two + j + 1) * LANES)
                    rows = istage[pl.ds(j * key_count + h, BLOCK // 2, stride=heads), :].astype(bf16)
                    gbuf[n // 2, h, (n % 2) * (BLOCK // 2) : (n % 2 + 1) * (BLOCK // 2), cols] = rows

    istage[...] = iq[...].astype(f32)

    @pl.loop(0, idx_heads)
    def _(h):
        rows = istage[pl.ds(h, groups * BLOCK, stride=idx_heads), :].astype(bf16)
        iqr[0, h] = rows[:BLOCK]
        iqr[1, h] = rows[BLOCK:]

    def head_gathers(sems):
        return [
            [
                HeadGather(
                    comp.at[pl.ds(g * picks, picks), :, COLS[c]], keys.at[g, :, :, :, COLS[c]], sems, (g, c)
                )
                for c in range(2)
            ]
            for g in range(groups)
        ]

    key_gathers = head_gathers((ag_send, ag_recv))

    def order_rows(c):
        rows = tn(pick_entry[...], recv[:, :, COLS[c]].reshape(slot_rows, 384))
        rows = rows.astype(bf16).reshape(groups * picks, QT, 384)
        comp[:, :, COLS[c]] = rows
        for g in range(groups):
            keys[g, :, col, :, COLS[c]] = rows[g * picks : (g + 1) * picks]

    def key_rows_of(g, cols):
        return keys[g, :, :, :, cols].reshape(key_count, cols.stop - cols.start)

    def index_chunk(g, c):
        width = 8 * BLOCK
        rows = iqr[g, 8 * c : 8 * c + 8].reshape(width, LANES)
        v = nt(key_rows_of(g, IDX), rows) * idx_scale
        weight = jnp.concatenate(
            [iw[8 * c + h : 8 * c + h + 1, g * BLOCK : (g + 1) * BLOCK] for h in range(8)], axis=1
        )
        return rows, v, weight

    def query_rows(x):
        flat = x.T
        return flat[:BLOCK] + flat[BLOCK:]

    def index_scores(g):
        total = jnp.zeros((key_count, LANES), f32)
        for c in range(idx_heads // 8):
            _, v, weight = index_chunk(g, c)
            part = v / (1.0 + jnp.exp(-v)) * weight
            for j in range(4):
                total = total + part[:, j * LANES : (j + 1) * LANES]
        ex[g, :, 1] = query_rows(total).reshape(NH, QT, key_count)

    def score_copies(g):
        out = []
        for d in range(1, NH):
            to = lax.rem(col + d, NH)
            out.append(remote(ex.at[g, to], exr.at[g, d - 1], (ex_send, ex_recv), (g, d - 1), (me, to)))
        return out

    def index_softmax(g):
        for copy in score_copies(g):
            copy.wait_recv()
            copy.wait_send()
        total = ex[g, col]
        for d in range(1, NH):
            total = total + exr[g, d - 1]
        target = total[0] * (1.0 / head_total)
        q_pos = col * QT + iota((QT, key_count), 0)
        k_pos = iota((QT, key_count), 1) - (key_count - BLOCK)
        score = jnp.where(k_pos <= q_pos, total[1], -jnp.inf)
        e = jnp.exp(score - jnp.max(score, axis=1, keepdims=True))
        prob = e / jnp.sum(e, axis=1, keepdims=True)
        k_rows = pl.ds(pl.multiple_of(g * BLOCK + col * QT, QT), QT)
        dsb[g, col] = kl[k_rows, 0:1] * (prob - target)
        for copy in d_copies(g, False):
            copy.start()

    def d_copies(g, arrival):
        out = []
        for d in range(1, NH):
            place = lax.rem(col - d + NH, NH) if arrival else col
            to = lax.rem(col + d, NH)
            out.append(
                remote(dsb.at[g, col], dsb.at[g, place], (d_send, d_recv), (g, d - 1), (me, to))
            )
        return out

    def index_backward(g):
        for copy in d_copies(g, True):
            copy.wait_recv()
            copy.wait_send()
        grad_rows = dsb[g].reshape(BLOCK, key_count)
        dst[...] = jnp.concatenate([grad_rows, grad_rows], axis=0).T
        key_side = key_rows_of(g, IDX)
        kt_idx = key_side.T
        for c in range(idx_heads // 8):
            rows, v, weight = index_chunk(g, c)
            sig = 1.0 / (1.0 + jnp.exp(-v))
            wide = jnp.concatenate([dst[...]] * 4, axis=1)
            silu = v * sig
            d_weight = jnp.sum(wide * silu, axis=0, keepdims=True)
            for h in range(8):
                dw[8 * c + h : 8 * c + h + 1, g * BLOCK : (g + 1) * BLOCK] = d_weight[
                    :, h * BLOCK : (h + 1) * BLOCK
                ]
            slope = sig + silu * (1.0 - sig)
            grad = (wide * (weight * idx_scale) * slope).astype(bf16)
            d_rows = nn(kt_idx, grad).T
            for h in range(8):
                istage[pl.ds(g * BLOCK * idx_heads + 8 * c + h, BLOCK, stride=idx_heads), :] = d_rows[
                    h * BLOCK : (h + 1) * BLOCK
                ]
            part = nt(rows.T, grad)
            if c == 0:
                ik_acc[...] = part
            else:
                ik_acc[...] += part
        for j in range(key_count // LANES):
            part = ik_acc[:, j * LANES : (j + 1) * LANES].astype(bf16).T
            ikb[g, 2 * j : 2 * j + 2] = part.reshape(2, NH, QT, LANES)

    def products(n, buf):
        s, dp = buf[0], buf[1]
        g, c = n // (heads // HC), n % (heads // HC)
        queries = jnp.concatenate([qp[g, c * (HC // 2) + j] for j in range(HC // 2)], axis=1)
        s[...] = nn(key_rows_of(g, LAT), queries)
        dp[...] = nt(key_rows_of(g, VAL), gbuf[g, c * HC : (c + 1) * HC].reshape(R, 512))

    def softmax_passes(buf):
        s, dp, ds, low = buf
        steps = key_count // TT
        edge = key_count - BLOCK
        q_pos = iota((BLOCK, R), 1) % BLOCK
        s[edge:, :] = jnp.where(iota((BLOCK, R), 0) <= q_pos, s[edge:, :], -jnp.inf)

        def at(i):
            return pl.ds(pl.multiple_of(i * TT, TT), TT)

        top = lax.fori_loop(
            0, steps,
            lambda i, m: jnp.maximum(m, fold(s[at(i), :], jnp.max)),
            jnp.full((8, R), -jnp.inf, f32),
            unroll=True,
        )
        top = jnp.max(top, axis=0, keepdims=True)

        def exps(i, sums):
            e = jnp.exp2((s[at(i), :] - top) * EXP_SCALE)
            s[at(i), :] = e
            return sums[0] + fold(e, jnp.sum), sums[1] + fold(e * dp[at(i), :], jnp.sum)

        zero = jnp.zeros((8, R), f32)
        total, dot = lax.fori_loop(0, steps, exps, (zero, zero), unroll=True)
        inv = 1.0 / jnp.sum(total, axis=0, keepdims=True)
        delta = jnp.sum(dot, axis=0, keepdims=True) * inv

        def finish(i, carry):
            p = s[at(i), :] * inv
            low[at(i), :] = p.astype(bf16)
            ds[at(i), :] = (p * (dp[at(i), :] - delta) * SCORE_SCALE).astype(bf16)
            part = p[:, :LANES]
            for j in range(1, R // LANES):
                part = part + p[:, j * LANES : (j + 1) * LANES]
            pacc[at(i), :] += part
            return carry

        lax.fori_loop(0, steps, finish, 0, unroll=True)

    def gradients(n, buf):
        ds, low = buf[2][...], buf[3][...]
        g, c = n // (heads // HC), n % (heads // HC)
        d_queries = nn(kt[LAT, :], ds).astype(bf16)
        for j in range(HC // 2):
            dqp[g, c * (HC // 2) + j] = d_queries[:, j * LANES : (j + 1) * LANES]
        queries = jnp.concatenate([qp[g, c * (HC // 2) + j] for j in range(HC // 2)], axis=1)
        acc[:576, :] += nt(queries, ds)
        acc[:512, :] += nt(gbuf[g, c * HC : (c + 1) * HC].reshape(R, 512).T, low)

    def begin(g):
        kt[...] = key_rows_of(g, slice(0, WIDTH)).T
        acc[...] = jnp.zeros_like(acc)
        pacc[...] = jnp.zeros_like(pacc)

    low_half, high_half = pl.ds(0, picks // 2), pl.ds(picks // 2, picks // 2)
    rs = (rs_send, rs_recv)

    def term_copy(g, kind):
        src, dst, to = (
            (ktb.at[g, low_half, far], opp_in.at[g, 0], right),
            (ktb.at[g, high_half, far], opp_in.at[g, 1], left),
            (ktb.at[g, high_half, right], fin.at[g, 1], right),
            (ktb.at[g, low_half, left], fin.at[g, 3], left),
            (merged.at[g, 0], fin.at[g, 0], right),
            (merged.at[g, 1], fin.at[g, 2], left),
        )[kind]
        return remote(src, dst, rs, (g, kind), (me, to))

    def send_terms(g):
        for j in range(key_count // LANES):
            part = acc[:, j * LANES : (j + 1) * LANES].astype(bf16).T
            ktb[g, 2 * j : 2 * j + 2] = part.reshape(2, NH, QT, 640)
        for kind in range(4):
            term_copy(g, kind).start()

    def merge_terms(g):
        half = picks // 2
        term_copy(g, 0).wait_recv()
        merged[g, 0] = (ktb[g, :half, right].astype(f32) + opp_in[g, 0].astype(f32)).astype(bf16)
        term_copy(g, 4).start()
        term_copy(g, 1).wait_recv()
        merged[g, 1] = (ktb[g, half:, left].astype(f32) + opp_in[g, 1].astype(f32)).astype(bf16)
        term_copy(g, 5).start()

    def sum_terms(g):
        for kind in range(2, 6):
            term_copy(g, kind).wait_recv()
        half = picks // 2
        for part, a, b in ((slice(0, half), 0, 3), (slice(half, picks), 1, 2)):
            total = ktb[g, part, col].astype(f32) + fin[g, a].astype(f32) + fin[g, b].astype(f32)
            entries = slice(g * picks + part.start, g * picks + part.stop)
            comp[entries, :, 128:WIDTH] = total.astype(bf16)
        for kind in range(6):
            term_copy(g, kind).wait_send()

    def send_scores(g):
        ex[g, :, 0] = query_rows(pacc[...]).reshape(NH, QT, key_count)
        for copy in score_copies(g):
            copy.start()

    buf_a, buf_b = (s_a, dp_a, ds_a, pl_a), (s_b, dp_b, ds_b, pl_b)

    gathers[0].finish()
    order_rows(0)
    key_gathers[0][0].start()
    gathers[1].finish()
    key_gathers[0][0].forward()
    order_rows(1)
    key_gathers[0][1].start()
    key_gathers[0][0].finish()
    index_scores(0)
    key_gathers[0][1].forward()
    key_gathers[1][0].start()
    key_gathers[1][1].start()
    key_gathers[0][1].finish()

    begin(0)
    products(0, buf_a)
    for it in range(4):
        if it == 1:
            key_gathers[1][0].forward()
            key_gathers[1][1].forward()
        if it == 3:
            merge_terms(0)
            index_softmax(0)
        products(2 * it + 1, buf_b)
        softmax_passes(buf_a)
        gradients(2 * it, buf_a)
        softmax_passes(buf_b)
        if it == 1:
            key_gathers[1][0].finish()
            key_gathers[1][1].finish()
        if it < 3:
            products(2 * it + 2, buf_a)
        gradients(2 * it + 1, buf_b)
        if it % 2 == 1:
            send_terms(it // 2)
            if it == 3:
                index_scores(1)
            send_scores(it // 2)
        if it == 1:
            begin(1)

    index_backward(0)
    index_softmax(1)
    merge_terms(1)
    sum_terms(0)
    index_backward(1)
    ik_copies = []
    for d in range(1, NH):
        to = lax.rem(col + d, NH)
        ik_copies.append(
            remote(ikb.at[:, :, to], ikr.at[d - 1], (ik_send, ik_recv), d - 1, (me, to))
        )
    for copy in ik_copies:
        copy.start()
    sum_terms(1)

    backs = [CtxExchange(n_ctx, send, back, (r_send, r_recv), g) for g in range(2)]
    entry_rows = groups * picks * QT

    def spread(c):
        rows = nn(pick_entry[...], comp[:, :, COLS[c]].reshape(entry_rows, 384))
        send[:, :, COLS[c]] = rows.astype(bf16).reshape(n_ctx, SLOTS * QT, 384)
        backs[c].start()
        back[me, :, COLS[c]] = send[me, :, COLS[c]]

    spread(1)
    for copy in ik_copies:
        copy.wait_recv()
        copy.wait_send()
    idx_sum = ikb[:, :, col].astype(f32)
    for d in range(1, NH):
        idx_sum = idx_sum + ikr[d - 1].astype(f32)
    comp[:, :, IDX] = idx_sum.astype(bf16).reshape(groups * picks, QT, LANES)
    spread(0)

    @pl.loop(0, pairs)
    def _(j):
        one, two = dqp[0, j], dqp[1, j]
        qp[j // 8, (j % 8) * 2] = jnp.concatenate([one[:, :BLOCK], two[:, :BLOCK]], axis=1)
        qp[j // 8, (j % 8) * 2 + 1] = jnp.concatenate([one[:, BLOCK:], two[:, BLOCK:]], axis=1)

    dq_stores = [
        pltpu.make_async_copy(qp.at[n], dq_hbm.at[pl.ds(n * pairs, pairs)], dq_sem.at[n])
        for n in range(2)
    ]
    for copy in dq_stores:
        copy.start()
    diq[...] = istage[...].astype(bf16)

    own_gathers = head_gathers((og_send, og_recv))

    def own_sums(c):
        rows = tn(pick_own[...], back[:, :, COLS[c]].reshape(slot_rows, 384))
        rows = rows.astype(bf16).reshape(blocks, QT, 384)
        comp[:, :, COLS[c]] = rows
        for g in range(groups):
            keys[g, :, col, :, COLS[c]] = rows[g * picks : (g + 1) * picks]
            own_gathers[g][c].start()

    def results(c):
        for n in range(blocks // 2):
            g, b = divmod(2 * n, picks)
            part = keys[g, b : b + 2, :, :, COLS[c]].reshape(LANES, 384)
            place = slice(n * LANES, (n + 1) * LANES)
            if c == 0:
                dkey[place, :] = part[:, IDX]
                dlat[:256, place] = part[:, 128:].T
            else:
                dlat[256:, place] = part.T[:320]

    backs[1].finish()
    own_sums(1)
    backs[0].finish()
    for g in range(groups):
        own_gathers[g][1].forward()
    own_sums(0)
    for g in range(groups):
        own_gathers[g][1].finish()
    results(1)
    for g in range(groups):
        own_gathers[g][0].forward()
    for g in range(groups):
        own_gathers[g][0].finish()
    results(0)
    for copy in dq_stores:
        copy.wait()


VM = pl.BlockSpec(memory_space=pltpu.VMEM)
HB = pl.BlockSpec(memory_space=pl.ANY)
DMA = pltpu.SemaphoreType.DMA


def shards(
    n_ctx, query_latent, d_out, latent, index_query, index_weight, index_key, kl_scale, history, diag_block
):
    q_dev, heads, lat_width = query_latent.shape
    val_width = d_out.shape[2]
    idx_heads, idx_width = index_query.shape[1:]
    groups, hist = history.shape
    picks = hist + 2
    entries = groups * picks
    key_count = picks * BLOCK
    blk_dev = latent.shape[0] // BLOCK
    shape = jax.ShapeDtypeStruct

    sink = jnp.zeros((groups, 1), i32)
    lists = jnp.concatenate([sink, history, diag_block[:, None]], axis=1).reshape(-1)
    owner, local = lists // blk_dev, lists % blk_dev
    order = jnp.arange(entries)
    earlier = (order[None, :] < order[:, None]) & (owner[None, :] == owner[:, None])
    slot = owner * SLOTS + jnp.sum(earlier.astype(i32), axis=1)
    hits = slot[None, :] == jnp.arange(n_ctx * SLOTS)[:, None]

    def slot_table(values):
        ids = jnp.sum(jnp.where(hits, values[None, :] + 1, 0), axis=1) - 1
        ids = jnp.pad(ids.reshape(n_ctx, SLOTS), ((0, 0), (0, 8 - SLOTS)), constant_values=-1)
        return jnp.broadcast_to(ids[:, :, None], (n_ctx, 8, LANES))

    pairs = heads // 2
    chunk = [pltpu.VMEM((key_count, R), t) for t in (f32, f32, bf16, bf16)]
    slots = pltpu.VMEM((n_ctx, SLOTS * QT, WIDTH), bf16)
    d_query, d_lat, d_key, d_iq, d_weight = pl.pallas_call(
        partial(whole_kernel, n_ctx, heads * NH),
        name="sparse_attention_backward",
        in_specs=[VM, VM, HB, HB, HB, HB, VM, VM, VM],
        out_specs=[HB, VM, VM, VM, VM],
        out_shape=[
            shape((heads, lat_width, q_dev), bf16),
            shape((lat_width, blk_dev * BLOCK), bf16),
            shape((blk_dev * BLOCK, idx_width), bf16),
            shape((q_dev * idx_heads, idx_width), bf16),
            shape((idx_heads, q_dev), f32),
        ],
        scratch_shapes=[
            pltpu.VMEM((n_ctx, 8, LANES), i32),
            pltpu.VMEM((2, NH, QT, lat_width), bf16),
            pltpu.VMEM((blk_dev, QT, lat_width), bf16),
            pltpu.VMEM((blk_dev, QT, idx_width), bf16),
            pltpu.VMEM((n_ctx * SLOTS * QT, blk_dev * QT), bf16),
            pltpu.VMEM((n_ctx * SLOTS * QT, entries * QT), bf16),
            slots, slots, slots,
            pltpu.VMEM((entries, QT, WIDTH), bf16),
            pltpu.VMEM((groups, picks, NH, QT, WIDTH), bf16),
            pltpu.VMEM((groups, pairs, lat_width, LANES), bf16),
            pltpu.VMEM((groups, pairs, lat_width, LANES), bf16),
            pltpu.VMEM((groups, heads, BLOCK, val_width), bf16),
            pltpu.VMEM((WIDTH, key_count), bf16),
            pltpu.VMEM((640, key_count), f32),
            pltpu.VMEM((key_count, LANES), f32),
            *chunk, *chunk,
            pltpu.VMEM((q_dev * idx_heads, LANES), f32),
            pltpu.VMEM((groups, idx_heads, BLOCK, LANES), bf16),
            pltpu.VMEM((groups, NH, 2, QT, key_count), f32),
            pltpu.VMEM((groups, NH - 1, 2, QT, key_count), f32),
            pltpu.VMEM((groups, NH, QT, key_count), f32),
            pltpu.VMEM((key_count, LANES), f32),
            pltpu.VMEM((groups, picks, NH, QT, 640), bf16),
            pltpu.VMEM((groups, 2, picks // 2, QT, 640), bf16),
            pltpu.VMEM((groups, 2, picks // 2, QT, 640), bf16),
            pltpu.VMEM((groups, 4, picks // 2, QT, 640), bf16),
            pltpu.VMEM((groups, picks, NH, QT, LANES), bf16),
            pltpu.VMEM((NH - 1, groups, picks, QT, LANES), bf16),
            pltpu.VMEM((idx_width, key_count), f32),
            DMA((blk_dev // 2,)), DMA((1,)), DMA((2,)), DMA((4,)), DMA((2,)),
            DMA((n_ctx,)), DMA((n_ctx,)),
            DMA((2, n_ctx)), DMA((2, n_ctx)), DMA((2, n_ctx)), DMA((2, n_ctx)),
            DMA((groups, 2, 4)), DMA((groups, 2, 4)), DMA((groups, 2, 4)), DMA((groups, 2, 4)),
            DMA((groups, NH - 1)), DMA((groups, NH - 1)), DMA((groups, NH - 1)), DMA((groups, NH - 1)),
            DMA((groups, 6)), DMA((groups, 6)),
            DMA((NH - 1,)), DMA((NH - 1,)),
        ],
        compiler_params=pltpu.CompilerParams(
            collective_id=0, has_side_effects=True, vmem_limit_bytes=63 * 2**20
        ),
    )(
        slot_table(local),
        slot_table(order),
        jnp.transpose(query_latent, (1, 2, 0)),
        d_out.reshape(q_dev * heads, val_width),
        latent.T,
        index_key.reshape(blk_dev, BLOCK, idx_width),
        index_query.reshape(q_dev * idx_heads, idx_width),
        index_weight.T,
        jnp.broadcast_to(kl_scale[:, None], (q_dev, LANES)),
    )
    return (
        jnp.transpose(d_query, (2, 0, 1)),
        d_lat.T,
        d_iq.reshape(q_dev, idx_heads, idx_width),
        d_weight.T,
        d_key,
    )


def solution(mesh):
    in_specs = (
        P("ctx", "head", None),
        P("ctx", "head", None),
        P("ctx", None),
        P("ctx", "head", None),
        P("ctx", "head"),
        P("ctx", None),
        P("ctx"),
        P("ctx", None),
        P("ctx"),
    )
    out_specs = (
        P("ctx", "head", None),
        P("ctx", None),
        P("ctx", "head", None),
        P("ctx", "head"),
        P("ctx", None),
    )
    body = partial(shards, mesh.shape["ctx"])
    return jax.shard_map(body, mesh=mesh, in_specs=in_specs, out_specs=out_specs, check_vma=False)
```

```python
from functools import partial

import jax
import jax.numpy as jnp
from jax import lax
from jax.experimental import pallas as pl
from jax.experimental.pallas import tpu as pltpu
from jax.sharding import PartitionSpec as P

MESH = pl.DeviceIdType.MESH
f32, bf16, i32 = jnp.float32, jnp.bfloat16, jnp.int32

SCORE_SCALE = 192.0 ** (-0.5)
EXP_SCALE = SCORE_SCALE * 1.4426950408889634
BLOCK = 64
SLOTS = 2
LANES = 128
IDX = slice(0, 128)
LAT = slice(128, 704)
VAL = slice(128, 640)
WIDTH = 768
COLS = (slice(0, 384), slice(384, 768))
NH = 4
QT = BLOCK // NH
HC = 8
R = HC * BLOCK
TT = 32


def nn(a, b):
    return jnp.dot(a, b, preferred_element_type=f32)


def nt(a, b):
    return lax.dot_general(a, b, (((1,), (1,)), ((), ())), preferred_element_type=f32)


def tn(a, b):
    return lax.dot_general(a, b, (((0,), (0,)), ((), ())), preferred_element_type=f32)


def iota(shape, dim):
    return lax.broadcasted_iota(i32, shape, dim)


def fold(x, op):
    rows, cols = x.shape
    return op(x.reshape(rows // 8, 8, cols), axis=0)


def row_picks(ids, out, n_ctx, width):
    @pl.loop(0, n_ctx)
    def _(r):
        for s in range(SLOTS):
            row = jnp.broadcast_to(ids[r, s : s + 1, :], (QT, LANES)) * QT + iota((QT, LANES), 0)
            wide = jnp.concatenate([row] * (width // LANES), axis=1)
            hit = jnp.where(wide == iota((QT, width), 1), 1.0, 0.0).astype(bf16)
            out[pl.ds(pl.multiple_of((r * SLOTS + s) * QT, QT), QT), :] = hit


def slot_tables(history, diag, ask, entry, blk_dev):
    groups, hist = history.shape
    picks = hist + 2
    lane = iota((8, LANES), 1)
    owner = jnp.where(lane < groups * picks, 0, -1)
    local = jnp.zeros((8, LANES), i32)
    owners = [jnp.int32(0)] * (groups * picks)
    for g in range(groups):
        for k in range(1, picks):
            block = history[g, k - 1] if k <= hist else diag[g]
            e = g * picks + k
            owners[e] = block // blk_dev
            owner = jnp.where(lane == e, owners[e], owner)
            local = jnp.where(lane == e, block % blk_dev, local)
    slot = owner * SLOTS
    for e, one in enumerate(owners):
        slot = slot + jnp.where(lane > e, 1, 0) * jnp.where(owner == one, 1, 0)
    rows = ask.shape[0] * 8
    place = iota((rows, LANES), 0)
    here = jnp.where(place % 8 < SLOTS, place // 8 * SLOTS + place % 8, -9)
    hit = jnp.broadcast_to(slot[:1], (rows, LANES)) == here
    for values, out in ((local, ask), (lane, entry)):
        wide = jnp.broadcast_to((values[:1] + 1).astype(f32), (rows, LANES))
        found = jnp.sum(jnp.where(hit, wide, 0.0), axis=1, keepdims=True) - 1.0
        out[...] = jnp.broadcast_to(found, (rows, LANES)).astype(i32).reshape(out.shape)


def remote(src, dst, sems, index, to):
    send, recv = sems
    return pltpu.make_async_remote_copy(
        src_ref=src,
        dst_ref=dst,
        send_sem=send.at[index],
        recv_sem=recv.at[index],
        device_id=to,
        device_id_type=MESH,
    )


class CtxExchange:
    def __init__(self, n_ctx, src, dst, sems, group=None):
        self.n, self.src, self.dst, self.sems, self.group = n_ctx, src, dst, sems, group

    def copy(self, d, arrival):
        me, col = lax.axis_index("ctx"), lax.axis_index("head")
        to = lax.rem(me + d, self.n)
        place = lax.rem(me - d + self.n, self.n) if arrival else me
        if self.group is None:
            return remote(self.src.at[to], self.dst.at[place], self.sems, d, (to, col))
        cols = pl.ds(self.group * 384, 384)
        return remote(
            self.src.at[to, :, cols], self.dst.at[place, :, cols], self.sems, (self.group, d), (to, col)
        )

    def start(self):
        @pl.loop(1, self.n)
        def _(d):
            self.copy(d, False).start()

    def finish(self, first=1, last=None):
        @pl.loop(first, last or self.n)
        def _(d):
            copy = self.copy(d, True)
            copy.wait_recv()
            copy.wait_send()


class HeadGather:
    def __init__(self, src, place, sems, index):
        self.src, self.place, self.sems, self.index = src, place, sems, index
        me, col = lax.axis_index("ctx"), lax.axis_index("head")
        self.me, self.col = me, col
        self.right, self.left, self.far = (lax.rem(col + d, NH) for d in (1, 3, 2))

    def copy(self, kind, member):
        to = (self.me, (self.right, self.left)[kind % 2])
        ref = self.place(member)
        if kind < 2:
            return remote(self.src, ref, self.sems, self.index + (kind,), to)
        half = ref.shape[0] // 2
        ref = ref.at[pl.ds((kind - 2) * half, half)]
        return remote(ref, ref, self.sems, self.index + (kind,), to)

    def start(self):
        self.copy(0, self.col).start()
        self.copy(1, self.col).start()

    def forward(self):
        self.copy(0, self.left).wait_recv()
        self.copy(2, self.left).start()
        self.copy(1, self.right).wait_recv()
        self.copy(3, self.right).start()

    def finish(self):
        self.copy(2, self.far).wait_recv()
        self.copy(3, self.far).wait_recv()
        self.copy(0, self.col).wait_send()
        self.copy(1, self.col).wait_send()
        self.copy(2, self.left).wait_send()
        self.copy(3, self.right).wait_send()


class HeadReduce:
    def __init__(self, part, opp, merged, fin, sems, index):
        self.part, self.opp, self.merged, self.fin = part, opp, merged, fin
        self.sems, self.index = sems, index
        me, col = lax.axis_index("ctx"), lax.axis_index("head")
        self.me, self.col = me, col
        self.right, self.left, self.far = (lax.rem(col + d, NH) for d in (1, 3, 2))

    def copy(self, kind):
        to = (self.me, (self.right, self.left, self.right, self.left, self.right, self.left)[kind])
        if kind < 2:
            src, dst = self.part(kind, self.far), self.opp(kind)
        elif kind == 2:
            src, dst = self.part(1, self.right), self.fin(1)
        elif kind == 3:
            src, dst = self.part(0, self.left), self.fin(3)
        else:
            src, dst = self.merged(kind - 4), self.fin(2 * (kind - 4))
        return remote(src, dst, self.sems, self.index + (kind,), to)

    def start(self):
        for kind in range(4):
            self.copy(kind).start()

    def merge(self):
        for half, member in ((0, self.right), (1, self.left)):
            self.copy(half).wait_recv()
            total = self.part(half, member)[...].astype(f32) + self.opp(half)[...].astype(f32)
            out = self.merged(half)
            out[...] = total.astype(out.dtype)
            self.copy(4 + half).start()

    def finish(self):
        for kind in range(2, 6):
            self.copy(kind).wait_recv()
        for kind in range(6):
            self.copy(kind).wait_send()

    def total(self, half):
        a, b = ((0, 3), (1, 2))[half]
        own = self.part(half, self.col)[...].astype(f32)
        return own + self.fin(a)[...].astype(f32) + self.fin(b)[...].astype(f32)


def greet(n_ctx):
    me, col = lax.axis_index("ctx"), lax.axis_index("head")
    barrier = pltpu.get_barrier_semaphore()

    @pl.loop(1, n_ctx)
    def _(d):
        pl.semaphore_signal(
            barrier, inc=1, device_id=(lax.rem(me + d, n_ctx), col), device_id_type=MESH
        )

    for d in range(1, NH):
        pl.semaphore_signal(barrier, inc=1, device_id=(me, lax.rem(col + d, NH)), device_id_type=MESH)
    pl.semaphore_wait(barrier, n_ctx + NH - 2)


def whole_kernel(
    n_ctx, head_total,
    history, diag, q_hbm, g_hbm, lat_hbm, key_hbm, iq, iw, kl_row,
    dq_hbm, dlat, dkey, diq, dw,
    ask, entry, kl, ids, latr, latq, keyq, pick_own, pick_entry, send, recv, back, comp, keys,
    qp, dqp, gbuf, kt, acc, pacc, s_a, dp_a, ds_a, pl_a, s_b, dp_b, ds_b, pl_b,
    istage, iqr, ex, ex_opp, ex_merged, ex_fin, dsb, dst, ktb, opp_in, merged, fin,
    ikb, ik_opp, ik_merged, ik_fin, ik_acc,
    lat_sem, key_sem, q_sem, g_sem, dq_sem,
    ask_send, ask_recv, a_send, a_recv, r_send, r_recv, ag_send, ag_recv, og_send, og_recv,
    ex_send, ex_recv, d_send, d_recv, rs_send, rs_recv, ik_send, ik_recv,
):
    me, col = lax.axis_index("ctx"), lax.axis_index("head")
    right, left, far = (lax.rem(col + d, NH) for d in (1, 3, 2))
    blocks = latq.shape[0]
    lat_width = latq.shape[2]
    groups, picks = keys.shape[0], keys.shape[1]
    key_count = picks * BLOCK
    pairs = qp.shape[1]
    heads = 2 * pairs
    idx_heads = iw.shape[0]
    idx_scale = LANES ** (-0.5)
    slot_rows = n_ctx * SLOTS * QT

    lat_loads = [
        pltpu.make_async_copy(
            lat_hbm.at[:, pl.ds(n * LANES, LANES)], dqp.at[0, n], lat_sem.at[n]
        )
        for n in range(blocks // 2)
    ]
    mine = pl.ds(pl.multiple_of(col * QT, QT), QT)
    key_load = pltpu.make_async_copy(key_hbm.at[:, mine], keyq, key_sem.at[0])
    stages = (ds_a, pl_a, ds_b, pl_b)
    g_loads = [
        pltpu.make_async_copy(
            g_hbm.at[pl.ds(n * key_count, key_count)], stages[n], g_sem.at[n]
        )
        for n in range(4)
    ]
    for copy in lat_loads + [key_load] + g_loads:
        copy.start()
    slot_tables(history, diag, ask, entry, blocks)
    kl[...] = jnp.broadcast_to(kl_row[...], (LANES, LANES)).T
    greet(n_ctx)
    asks = CtxExchange(n_ctx, ask, ids, (ask_send, ask_recv))
    asks.start()
    ids[me] = ask[me]

    for n, copy in enumerate(lat_loads):
        copy.wait()
        latr[...] = dqp[0, n].T.reshape(2, NH, QT, lat_width)
        latq[2 * n : 2 * n + 2] = latr[:, col]

    row_picks(entry, pick_entry, n_ctx, groups * picks * QT)
    key_load.wait()
    q_loads = [
        pltpu.make_async_copy(q_hbm.at[pl.ds(n * pairs, pairs)], dqp.at[n], q_sem.at[n])
        for n in range(2)
    ]
    for copy in q_loads:
        copy.start()
    asks.finish()
    row_picks(ids, pick_own, n_ctx, blocks * QT)

    gathers = [CtxExchange(n_ctx, send, recv, (a_send, a_recv), g) for g in range(2)]
    lat_rows = latq[...].reshape(blocks * QT, lat_width)
    key_rows = keyq[...].reshape(blocks * QT, LANES)
    first = jnp.concatenate([key_rows, lat_rows[:, :256]], axis=1)
    send[:, :, COLS[0]] = nn(pick_own[...], first).astype(bf16).reshape(n_ctx, SLOTS * QT, 384)
    gathers[0].start()
    rest = nn(pick_own[...], lat_rows[:, 256:]).astype(bf16)
    rest = jnp.concatenate([rest, jnp.zeros((slot_rows, WIDTH - LAT.stop), bf16)], axis=1)
    send[:, :, COLS[1]] = rest.reshape(n_ctx, SLOTS * QT, 384)
    gathers[1].start()
    recv[me] = send[me]

    for copy in q_loads:
        copy.wait()

    @pl.loop(0, pairs)
    def _(j):
        one, two = dqp[j // 8, (j % 8) * 2], dqp[j // 8, (j % 8) * 2 + 1]
        qp[0, j] = jnp.concatenate([one[:, :BLOCK], two[:, :BLOCK]], axis=1)
        qp[1, j] = jnp.concatenate([one[:, BLOCK:], two[:, BLOCK:]], axis=1)

    for n in range(4):
        g_loads[n].wait()
        for two in range(2):
            for j in range(2):
                cols = slice((2 * two + j) * LANES, (2 * two + j + 1) * LANES)
                istage[j * key_count : (j + 1) * key_count, :] = stages[n][:, cols].astype(f32)

            @pl.loop(0, heads)
            def _(h):
                for j in range(2):
                    cols = slice((2 * two + j) * LANES, (2 * two + j + 1) * LANES)
                    rows = istage[pl.ds(j * key_count + h, BLOCK // 2, stride=heads), :].astype(bf16)
                    gbuf[n // 2, h, (n % 2) * (BLOCK // 2) : (n % 2 + 1) * (BLOCK // 2), cols] = rows

    istage[...] = iq[...].astype(f32)

    @pl.loop(0, idx_heads)
    def _(h):
        rows = istage[pl.ds(h, groups * BLOCK, stride=idx_heads), :].astype(bf16)
        iqr[0, h] = rows[:BLOCK]
        iqr[1, h] = rows[BLOCK:]

    def head_gathers(sems):
        return [
            [
                HeadGather(
                    comp.at[pl.ds(g * picks, picks), :, COLS[c]],
                    lambda m, g=g, c=c: keys.at[g, :, m, :, COLS[c]],
                    sems,
                    (g, c),
                )
                for c in range(2)
            ]
            for g in range(groups)
        ]

    key_gathers = head_gathers((ag_send, ag_recv))

    def order_rows(c):
        rows = tn(pick_entry[...], recv[:, :, COLS[c]].reshape(slot_rows, 384))
        rows = rows.astype(bf16).reshape(groups * picks, QT, 384)
        comp[:, :, COLS[c]] = rows
        for g in range(groups):
            keys[g, :, col, :, COLS[c]] = rows[g * picks : (g + 1) * picks]

    def key_rows_of(g, cols):
        return keys[g, :, :, :, cols].reshape(key_count, cols.stop - cols.start)

    def index_chunk(g, c):
        width = 8 * BLOCK
        rows = iqr[g, 8 * c : 8 * c + 8].reshape(width, LANES)
        v = nt(key_rows_of(g, IDX), rows) * idx_scale
        weight = jnp.concatenate(
            [iw[8 * c + h : 8 * c + h + 1, g * BLOCK : (g + 1) * BLOCK] for h in range(8)], axis=1
        )
        return rows, v, weight

    def query_rows(x):
        flat = x.T
        return flat[:BLOCK] + flat[BLOCK:]

    def index_scores(g):
        total = jnp.zeros((key_count, LANES), f32)
        for c in range(idx_heads // 8):
            _, v, weight = index_chunk(g, c)
            part = v / (1.0 + jnp.exp(-v)) * weight
            for j in range(4):
                total = total + part[:, j * LANES : (j + 1) * LANES]
        ex[g, 1] = query_rows(total).reshape(NH, QT, key_count)

    def row_sums(g, kind):
        return HeadReduce(
            lambda half, m: ex.at[g, kind, m, pl.ds(half * 8, 8)],
            lambda i: ex_opp.at[g, kind, i],
            lambda i: ex_merged.at[g, kind, i],
            lambda i: ex_fin.at[g, kind, i],
            (ex_send, ex_recv),
            (g, kind),
        )

    probs = [row_sums(g, 0) for g in range(groups)]
    scores = [row_sums(g, 1) for g in range(groups)]
    d_rows = [
        HeadGather(dsb.at[g, col], lambda m, g=g: dsb.at[g, m], (d_send, d_recv), (g,)) for g in range(groups)
    ]

    def index_softmax(g):
        probs[g].finish()
        scores[g].finish()
        target = jnp.concatenate([probs[g].total(0), probs[g].total(1)], axis=0) * (1.0 / head_total)
        score = jnp.concatenate([scores[g].total(0), scores[g].total(1)], axis=0)
        q_pos = col * QT + iota((QT, key_count), 0)
        k_pos = iota((QT, key_count), 1) - (key_count - BLOCK)
        score = jnp.where(k_pos <= q_pos, score, -jnp.inf)
        e = jnp.exp(score - jnp.max(score, axis=1, keepdims=True))
        prob = e / jnp.sum(e, axis=1, keepdims=True)
        k_rows = pl.ds(pl.multiple_of(g * BLOCK + col * QT, QT), QT)
        dsb[g, col] = kl[k_rows, 0:1] * (prob - target)
        d_rows[g].start()

    def block_terms(terms, opp, merged, fin, sems, index, g, cols):
        half_picks = picks // 2
        return HeadReduce(
            lambda half, m: terms.at[g, pl.ds(half * half_picks, half_picks), m, :, cols],
            lambda i: opp.at[g, i, :, :, cols],
            lambda i: merged.at[g, i, :, :, cols],
            lambda i: fin.at[g, i, :, :, cols],
            sems,
            index,
        )

    every = slice(0, LANES)
    idx_terms = [
        block_terms(ikb, ik_opp, ik_merged, ik_fin, (ik_send, ik_recv), (g,), g, every) for g in range(groups)
    ]
    lat_cols = (slice(0, 256), slice(256, 640))
    lat_terms = [
        [
            block_terms(ktb, opp_in, merged, fin, (rs_send, rs_recv), (g, c), g, lat_cols[c])
            for c in range(2)
        ]
        for g in range(groups)
    ]

    def index_backward(g):
        d_rows[g].finish()
        grad_rows = dsb[g].reshape(BLOCK, key_count)
        dst[...] = jnp.concatenate([grad_rows, grad_rows], axis=0).T
        key_side = key_rows_of(g, IDX)
        kt_idx = key_side.T
        for c in range(idx_heads // 8):
            rows, v, weight = index_chunk(g, c)
            sig = 1.0 / (1.0 + jnp.exp(-v))
            wide = jnp.concatenate([dst[...]] * 4, axis=1)
            silu = v * sig
            d_weight = jnp.sum(wide * silu, axis=0, keepdims=True)
            for h in range(8):
                dw[8 * c + h : 8 * c + h + 1, g * BLOCK : (g + 1) * BLOCK] = d_weight[
                    :, h * BLOCK : (h + 1) * BLOCK
                ]
            slope = sig + silu * (1.0 - sig)
            grad = (wide * (weight * idx_scale) * slope).astype(bf16)
            iq_grad = nn(kt_idx, grad).T
            for h in range(8):
                istage[pl.ds(g * BLOCK * idx_heads + 8 * c + h, BLOCK, stride=idx_heads), :] = iq_grad[
                    h * BLOCK : (h + 1) * BLOCK
                ]
            part = nt(rows.T, grad)
            if c == 0:
                ik_acc[...] = part
            else:
                ik_acc[...] += part
        for j in range(key_count // LANES):
            part = ik_acc[:, j * LANES : (j + 1) * LANES].astype(bf16).T
            ikb[g, 2 * j : 2 * j + 2] = part.reshape(2, NH, QT, LANES)
        idx_terms[g].start()

    def products(n, buf):
        s, dp = buf[0], buf[1]
        g, c = n // (heads // HC), n % (heads // HC)
        queries = jnp.concatenate([qp[g, c * (HC // 2) + j] for j in range(HC // 2)], axis=1)
        s[...] = nn(key_rows_of(g, LAT), queries)
        dp[...] = nt(key_rows_of(g, VAL), gbuf[g, c * HC : (c + 1) * HC].reshape(R, 512))

    def softmax_passes(buf):
        s, dp, ds, low = buf
        steps = key_count // TT
        edge = key_count - BLOCK
        q_pos = iota((BLOCK, R), 1) % BLOCK
        s[edge:, :] = jnp.where(iota((BLOCK, R), 0) <= q_pos, s[edge:, :], -jnp.inf)

        def at(i):
            return pl.ds(pl.multiple_of(i * TT, TT), TT)

        top = lax.fori_loop(
            0, steps,
            lambda i, m: jnp.maximum(m, fold(s[at(i), :], jnp.max)),
            jnp.full((8, R), -jnp.inf, f32),
            unroll=True,
        )
        top = jnp.max(top, axis=0, keepdims=True)

        def exps(i, sums):
            e = jnp.exp2((s[at(i), :] - top) * EXP_SCALE)
            s[at(i), :] = e
            return sums[0] + fold(e, jnp.sum), sums[1] + fold(e * dp[at(i), :], jnp.sum)

        zero = jnp.zeros((8, R), f32)
        total, dot = lax.fori_loop(0, steps, exps, (zero, zero), unroll=True)
        inv = 1.0 / jnp.sum(total, axis=0, keepdims=True)
        delta = jnp.sum(dot, axis=0, keepdims=True) * inv

        def finish(i, carry):
            p = s[at(i), :] * inv
            low[at(i), :] = p.astype(bf16)
            ds[at(i), :] = (p * (dp[at(i), :] - delta) * SCORE_SCALE).astype(bf16)
            part = p[:, :LANES]
            for j in range(1, R // LANES):
                part = part + p[:, j * LANES : (j + 1) * LANES]
            pacc[at(i), :] += part
            return carry

        lax.fori_loop(0, steps, finish, 0, unroll=True)

    def gradients(n, buf):
        ds, low = buf[2][...], buf[3][...]
        g, c = n // (heads // HC), n % (heads // HC)
        d_queries = nn(kt[LAT, :], ds).astype(bf16)
        for j in range(HC // 2):
            dqp[g, c * (HC // 2) + j] = d_queries[:, j * LANES : (j + 1) * LANES]
        queries = jnp.concatenate([qp[g, c * (HC // 2) + j] for j in range(HC // 2)], axis=1)
        acc[:576, :] += nt(queries, ds)
        acc[:512, :] += nt(gbuf[g, c * HC : (c + 1) * HC].reshape(R, 512).T, low)

    def begin(g):
        kt[...] = key_rows_of(g, slice(0, WIDTH)).T
        acc[...] = jnp.zeros_like(acc)
        pacc[...] = jnp.zeros_like(pacc)

    def send_terms(g):
        for j in range(key_count // LANES):
            part = acc[:, j * LANES : (j + 1) * LANES].astype(bf16).T
            ktb[g, 2 * j : 2 * j + 2] = part.reshape(2, NH, QT, 640)
        lat_terms[g][1].start()
        lat_terms[g][0].start()

    def sum_terms(reduce, g, cols):
        reduce.finish()
        half = picks // 2
        for i in range(2):
            comp[g * picks + i * half : g * picks + (i + 1) * half, :, cols] = reduce.total(i).astype(bf16)

    def send_probs(g):
        ex[g, 0] = query_rows(pacc[...]).reshape(NH, QT, key_count)
        probs[g].start()

    buf_a, buf_b = (s_a, dp_a, ds_a, pl_a), (s_b, dp_b, ds_b, pl_b)

    half_ctx = n_ctx // 2
    gathers[0].finish()
    order_rows(0)
    key_gathers[0][0].start()
    gathers[1].finish(1, half_ctx)
    key_gathers[0][0].forward()
    gathers[1].finish(half_ctx)
    order_rows(1)
    key_gathers[0][1].start()
    key_gathers[0][0].finish()
    index_scores(0)
    key_gathers[0][1].forward()
    key_gathers[1][0].start()
    key_gathers[1][1].start()
    scores[0].start()
    key_gathers[0][1].finish()

    begin(0)
    products(0, buf_a)
    for it in range(4):
        if it == 1:
            key_gathers[1][0].forward()
            key_gathers[1][1].forward()
            scores[0].merge()
        if it == 3:
            for c in (1, 0):
                lat_terms[0][c].merge()
            probs[0].merge()
            scores[1].merge()
        products(2 * it + 1, buf_b)
        softmax_passes(buf_a)
        gradients(2 * it, buf_a)
        if it == 3:
            index_softmax(0)
        softmax_passes(buf_b)
        if it == 1:
            key_gathers[1][0].finish()
            key_gathers[1][1].finish()
        if it < 3:
            products(2 * it + 2, buf_a)
        if it == 3:
            d_rows[0].forward()
        gradients(2 * it + 1, buf_b)
        if it % 2 == 1:
            send_probs(it // 2)
            send_terms(it // 2)
        if it == 1:
            begin(1)
            index_scores(1)
            scores[1].start()

    backs = [CtxExchange(n_ctx, send, back, (r_send, r_recv), g) for g in range(2)]
    entry_rows = groups * picks * QT

    def spread(c):
        rows = nn(pick_entry[...], comp[:, :, COLS[c]].reshape(entry_rows, 384))
        send[:, :, COLS[c]] = rows.astype(bf16).reshape(n_ctx, SLOTS * QT, 384)
        backs[c].start()
        back[me, :, COLS[c]] = send[me, :, COLS[c]]

    probs[1].merge()
    sum_terms(lat_terms[0][1], 0, COLS[1])
    lat_terms[1][1].merge()
    index_softmax(1)
    lat_terms[1][0].merge()
    sum_terms(lat_terms[1][1], 1, COLS[1])
    spread(1)
    d_rows[1].forward()
    index_backward(0)
    index_backward(1)
    idx_terms[0].merge()
    for g in range(groups):
        sum_terms(lat_terms[g][0], g, slice(128, 384))
    idx_terms[1].merge()
    for g in range(groups):
        sum_terms(idx_terms[g], g, IDX)
    spread(0)

    @pl.loop(0, pairs)
    def _(j):
        one, two = dqp[0, j], dqp[1, j]
        qp[j // 8, (j % 8) * 2] = jnp.concatenate([one[:, :BLOCK], two[:, :BLOCK]], axis=1)
        qp[j // 8, (j % 8) * 2 + 1] = jnp.concatenate([one[:, BLOCK:], two[:, BLOCK:]], axis=1)

    dq_stores = [
        pltpu.make_async_copy(qp.at[n], dq_hbm.at[pl.ds(n * pairs, pairs)], dq_sem.at[n])
        for n in range(2)
    ]
    for copy in dq_stores:
        copy.start()
    diq[...] = istage[...].astype(bf16)

    own_gathers = head_gathers((og_send, og_recv))

    def own_sums(c):
        rows = tn(pick_own[...], back[:, :, COLS[c]].reshape(slot_rows, 384))
        rows = rows.astype(bf16).reshape(blocks, QT, 384)
        comp[:, :, COLS[c]] = rows
        for g in range(groups):
            keys[g, :, col, :, COLS[c]] = rows[g * picks : (g + 1) * picks]
            own_gathers[g][c].start()

    def results(c):
        for n in range(blocks // 2):
            g, b = divmod(2 * n, picks)
            part = keys[g, b : b + 2, :, :, COLS[c]].reshape(LANES, 384)
            place = slice(n * LANES, (n + 1) * LANES)
            if c == 0:
                dkey[place, :] = part[:, IDX]
                dlat[:256, place] = part[:, 128:].T
            else:
                dlat[256:, place] = part.T[:320]

    backs[1].finish()
    own_sums(1)
    backs[0].finish(1, half_ctx)
    for g in range(groups):
        own_gathers[g][1].forward()
    backs[0].finish(half_ctx)
    own_sums(0)
    for g in range(groups):
        own_gathers[g][1].finish()
    results(1)
    for g in range(groups):
        own_gathers[g][0].forward()
    for g in range(groups):
        own_gathers[g][0].finish()
    results(0)
    for copy in dq_stores:
        copy.wait()


VM = pl.BlockSpec(memory_space=pltpu.VMEM)
HB = pl.BlockSpec(memory_space=pl.ANY)
SM = pl.BlockSpec(memory_space=pltpu.SMEM)
DMA = pltpu.SemaphoreType.DMA


def shards(
    n_ctx, query_latent, d_out, latent, index_query, index_weight, index_key, kl_scale, history, diag_block
):
    q_dev, heads, lat_width = query_latent.shape
    val_width = d_out.shape[2]
    idx_heads, idx_width = index_query.shape[1:]
    groups, hist = history.shape
    picks = hist + 2
    entries = groups * picks
    key_count = picks * BLOCK
    blk_dev = latent.shape[0] // BLOCK
    shape = jax.ShapeDtypeStruct

    pairs = heads // 2
    chunk = [pltpu.VMEM((key_count, R), t) for t in (f32, f32, bf16, bf16)]
    slots = pltpu.VMEM((n_ctx, SLOTS * QT, WIDTH), bf16)
    d_query, d_lat, d_key, d_iq, d_weight = pl.pallas_call(
        partial(whole_kernel, n_ctx, heads * NH),
        name="sparse_attention_backward",
        in_specs=[SM, SM, HB, HB, HB, HB, VM, VM, VM],
        out_specs=[HB, VM, VM, VM, VM],
        out_shape=[
            shape((heads, lat_width, q_dev), bf16),
            shape((lat_width, blk_dev * BLOCK), bf16),
            shape((blk_dev * BLOCK, idx_width), bf16),
            shape((q_dev * idx_heads, idx_width), bf16),
            shape((idx_heads, q_dev), f32),
        ],
        scratch_shapes=[
            pltpu.VMEM((n_ctx, 8, LANES), i32),
            pltpu.VMEM((n_ctx, 8, LANES), i32),
            pltpu.VMEM((q_dev, LANES), f32),
            pltpu.VMEM((n_ctx, 8, LANES), i32),
            pltpu.VMEM((2, NH, QT, lat_width), bf16),
            pltpu.VMEM((blk_dev, QT, lat_width), bf16),
            pltpu.VMEM((blk_dev, QT, idx_width), bf16),
            pltpu.VMEM((n_ctx * SLOTS * QT, blk_dev * QT), bf16),
            pltpu.VMEM((n_ctx * SLOTS * QT, entries * QT), bf16),
            slots, slots, slots,
            pltpu.VMEM((entries, QT, WIDTH), bf16),
            pltpu.VMEM((groups, picks, NH, QT, WIDTH), bf16),
            pltpu.VMEM((groups, pairs, lat_width, LANES), bf16),
            pltpu.VMEM((groups, pairs, lat_width, LANES), bf16),
            pltpu.VMEM((groups, heads, BLOCK, val_width), bf16),
            pltpu.VMEM((WIDTH, key_count), bf16),
            pltpu.VMEM((640, key_count), f32),
            pltpu.VMEM((key_count, LANES), f32),
            *chunk, *chunk,
            pltpu.VMEM((q_dev * idx_heads, LANES), f32),
            pltpu.VMEM((groups, idx_heads, BLOCK, LANES), bf16),
            pltpu.VMEM((groups, 2, NH, QT, key_count), f32),
            pltpu.VMEM((groups, 2, 2, QT // 2, key_count), f32),
            pltpu.VMEM((groups, 2, 2, QT // 2, key_count), f32),
            pltpu.VMEM((groups, 2, 4, QT // 2, key_count), f32),
            pltpu.VMEM((groups, NH, QT, key_count), f32),
            pltpu.VMEM((key_count, LANES), f32),
            pltpu.VMEM((groups, picks, NH, QT, 640), bf16),
            pltpu.VMEM((groups, 2, picks // 2, QT, 640), bf16),
            pltpu.VMEM((groups, 2, picks // 2, QT, 640), bf16),
            pltpu.VMEM((groups, 4, picks // 2, QT, 640), bf16),
            pltpu.VMEM((groups, picks, NH, QT, LANES), bf16),
            pltpu.VMEM((groups, 2, picks // 2, QT, LANES), bf16),
            pltpu.VMEM((groups, 2, picks // 2, QT, LANES), bf16),
            pltpu.VMEM((groups, 4, picks // 2, QT, LANES), bf16),
            pltpu.VMEM((idx_width, key_count), f32),
            DMA((blk_dev // 2,)), DMA((1,)), DMA((2,)), DMA((4,)), DMA((2,)),
            DMA((n_ctx,)), DMA((n_ctx,)),
            DMA((2, n_ctx)), DMA((2, n_ctx)), DMA((2, n_ctx)), DMA((2, n_ctx)),
            DMA((groups, 2, 4)), DMA((groups, 2, 4)), DMA((groups, 2, 4)), DMA((groups, 2, 4)),
            DMA((groups, 2, 6)), DMA((groups, 2, 6)),
            DMA((groups, 4)), DMA((groups, 4)),
            DMA((groups, 2, 6)), DMA((groups, 2, 6)),
            DMA((groups, 6)), DMA((groups, 6)),
        ],
        compiler_params=pltpu.CompilerParams(
            collective_id=0, has_side_effects=True, vmem_limit_bytes=63 * 2**20
        ),
    )(
        history,
        diag_block,
        jnp.transpose(query_latent, (1, 2, 0)),
        d_out.reshape(q_dev * heads, val_width),
        latent.T,
        index_key.reshape(blk_dev, BLOCK, idx_width),
        index_query.reshape(q_dev * idx_heads, idx_width),
        index_weight.T,
        kl_scale.reshape(1, q_dev),
    )
    return (
        jnp.transpose(d_query, (2, 0, 1)),
        d_lat.T,
        d_iq.reshape(q_dev, idx_heads, idx_width),
        d_weight.T,
        d_key,
    )


def solution(mesh):
    in_specs = (
        P("ctx", "head", None),
        P("ctx", "head", None),
        P("ctx", None),
        P("ctx", "head", None),
        P("ctx", "head"),
        P("ctx", None),
        P("ctx"),
        P("ctx", None),
        P("ctx"),
    )
    out_specs = (
        P("ctx", "head", None),
        P("ctx", None),
        P("ctx", "head", None),
        P("ctx", "head"),
        P("ctx", None),
    )
    body = partial(shards, mesh.shape["ctx"])
    return jax.shard_map(body, mesh=mesh, in_specs=in_specs, out_specs=out_specs, check_vma=False)
```

```python
from functools import partial

import jax
import jax.numpy as jnp
from jax import lax
from jax.experimental import pallas as pl
from jax.experimental.pallas import tpu as pltpu
from jax.sharding import PartitionSpec as P

MESH = pl.DeviceIdType.MESH
f32, bf16, i32 = jnp.float32, jnp.bfloat16, jnp.int32

SCORE_SCALE = 192.0 ** (-0.5)
EXP_SCALE = SCORE_SCALE * 1.4426950408889634
BLOCK = 64
SLOTS = 2
LANES = 128
IDX = slice(0, 128)
LAT = slice(128, 704)
VAL = slice(128, 640)
WIDTH = 768
COLS = (slice(0, 384), slice(384, 768))
KEY_COLS = (slice(0, 384), slice(384, 768))
NH = 4
QT = BLOCK // NH
HC = 8
R = HC * BLOCK
TT = 32


def nn(a, b):
    return jnp.dot(a, b, preferred_element_type=f32)


def nt(a, b):
    return lax.dot_general(a, b, (((1,), (1,)), ((), ())), preferred_element_type=f32)


def tn(a, b):
    return lax.dot_general(a, b, (((0,), (0,)), ((), ())), preferred_element_type=f32)


def iota(shape, dim):
    return lax.broadcasted_iota(i32, shape, dim)


def fold(x, op):
    rows, cols = x.shape
    return op(x.reshape(rows // 8, 8, cols), axis=0)


def row_picks(ids, out, n_ctx, width):
    @pl.loop(0, n_ctx)
    def _(r):
        for s in range(SLOTS):
            row = jnp.broadcast_to(ids[r, s : s + 1, :], (QT, LANES)) * QT + iota((QT, LANES), 0)
            wide = jnp.concatenate([row] * (width // LANES), axis=1)
            hit = jnp.where(wide == iota((QT, width), 1), 1.0, 0.0).astype(bf16)
            out[pl.ds(pl.multiple_of((r * SLOTS + s) * QT, QT), QT), :] = hit


def slot_tables(history, diag, ask, entry, blk_dev):
    groups, hist = history.shape
    picks = hist + 2
    lane = iota((8, LANES), 1)
    owner = jnp.where(lane < groups * picks, 0, -1)
    local = jnp.zeros((8, LANES), i32)
    owners = [jnp.int32(0)] * (groups * picks)
    for g in range(groups):
        for k in range(1, picks):
            block = history[g, k - 1] if k <= hist else diag[g]
            e = g * picks + k
            owners[e] = block // blk_dev
            owner = jnp.where(lane == e, owners[e], owner)
            local = jnp.where(lane == e, block % blk_dev, local)
    slot = owner * SLOTS
    for e, one in enumerate(owners):
        slot = slot + jnp.where(lane > e, 1, 0) * jnp.where(owner == one, 1, 0)
    rows = ask.shape[0] * 8
    place = iota((rows, LANES), 0)
    here = jnp.where(place % 8 < SLOTS, place // 8 * SLOTS + place % 8, -9)
    hit = jnp.broadcast_to(slot[:1], (rows, LANES)) == here
    for values, out in ((local, ask), (lane, entry)):
        wide = jnp.broadcast_to((values[:1] + 1).astype(f32), (rows, LANES))
        found = jnp.sum(jnp.where(hit, wide, 0.0), axis=1, keepdims=True) - 1.0
        out[...] = jnp.broadcast_to(found, (rows, LANES)).astype(i32).reshape(out.shape)


def remote(src, dst, sems, index, to):
    send, recv = sems
    return pltpu.make_async_remote_copy(
        src_ref=src,
        dst_ref=dst,
        send_sem=send.at[index],
        recv_sem=recv.at[index],
        device_id=to,
        device_id_type=MESH,
    )


class CtxExchange:
    def __init__(self, n_ctx, src, dst, sems, group=None, cols=None):
        self.n, self.src, self.dst, self.sems, self.group, self.cols = n_ctx, src, dst, sems, group, cols

    def copy(self, d, arrival):
        me, col = lax.axis_index("ctx"), lax.axis_index("head")
        to = lax.rem(me + d, self.n)
        place = lax.rem(me - d + self.n, self.n) if arrival else me
        if self.group is None:
            return remote(self.src.at[to], self.dst.at[place], self.sems, d, (to, col))
        cols = self.cols
        return remote(
            self.src.at[to, :, cols], self.dst.at[place, :, cols], self.sems, (self.group, d), (to, col)
        )

    def start(self):
        @pl.loop(1, self.n)
        def _(d):
            self.copy(d, False).start()

    def finish(self, first=1, last=None):
        @pl.loop(first, last or self.n)
        def _(d):
            copy = self.copy(d, True)
            copy.wait_recv()
            copy.wait_send()


class HeadGather:
    def __init__(self, src, place, sems, index):
        self.src, self.place, self.sems, self.index = src, place, sems, index
        me, col = lax.axis_index("ctx"), lax.axis_index("head")
        self.me, self.col = me, col
        self.right, self.left, self.far = (lax.rem(col + d, NH) for d in (1, 3, 2))

    def copy(self, kind, member):
        to = (self.me, (self.right, self.left)[kind % 2])
        ref = self.place(member)
        if kind < 2:
            return remote(self.src, ref, self.sems, self.index + (kind,), to)
        half = ref.shape[0] // 2
        ref = ref.at[pl.ds((kind - 2) * half, half)]
        return remote(ref, ref, self.sems, self.index + (kind,), to)

    def start(self):
        self.copy(0, self.col).start()
        self.copy(1, self.col).start()

    def forward(self):
        self.copy(0, self.left).wait_recv()
        self.copy(2, self.left).start()
        self.copy(1, self.right).wait_recv()
        self.copy(3, self.right).start()

    def finish(self):
        self.copy(2, self.far).wait_recv()
        self.copy(3, self.far).wait_recv()
        self.copy(0, self.col).wait_send()
        self.copy(1, self.col).wait_send()
        self.copy(2, self.left).wait_send()
        self.copy(3, self.right).wait_send()


class HeadReduce:
    def __init__(self, part, opp, merged, fin, sems, index):
        self.part, self.opp, self.merged, self.fin = part, opp, merged, fin
        self.sems, self.index = sems, index
        me, col = lax.axis_index("ctx"), lax.axis_index("head")
        self.me, self.col = me, col
        self.right, self.left, self.far = (lax.rem(col + d, NH) for d in (1, 3, 2))

    def copy(self, kind):
        to = (self.me, (self.right, self.left, self.right, self.left, self.right, self.left)[kind])
        if kind < 2:
            src, dst = self.part(kind, self.far), self.opp(kind)
        elif kind == 2:
            src, dst = self.part(1, self.right), self.fin(1)
        elif kind == 3:
            src, dst = self.part(0, self.left), self.fin(3)
        else:
            src, dst = self.merged(kind - 4), self.fin(2 * (kind - 4))
        return remote(src, dst, self.sems, self.index + (kind,), to)

    def start(self):
        for kind in range(4):
            self.copy(kind).start()

    def merge(self):
        for half, member in ((0, self.right), (1, self.left)):
            self.copy(half).wait_recv()
            total = self.part(half, member)[...].astype(f32) + self.opp(half)[...].astype(f32)
            out = self.merged(half)
            out[...] = total.astype(out.dtype)
            self.copy(4 + half).start()

    def finish(self):
        for kind in range(2, 6):
            self.copy(kind).wait_recv()
        for kind in range(6):
            self.copy(kind).wait_send()

    def total(self, half):
        a, b = ((0, 3), (1, 2))[half]
        own = self.part(half, self.col)[...].astype(f32)
        return own + self.fin(a)[...].astype(f32) + self.fin(b)[...].astype(f32)


def greet(n_ctx):
    me, col = lax.axis_index("ctx"), lax.axis_index("head")
    barrier = pltpu.get_barrier_semaphore()

    @pl.loop(1, n_ctx)
    def _(d):
        pl.semaphore_signal(
            barrier, inc=1, device_id=(lax.rem(me + d, n_ctx), col), device_id_type=MESH
        )

    for d in range(1, NH):
        pl.semaphore_signal(barrier, inc=1, device_id=(me, lax.rem(col + d, NH)), device_id_type=MESH)
    pl.semaphore_wait(barrier, n_ctx + NH - 2)


def whole_kernel(
    n_ctx, head_total,
    history, diag, q_hbm, g_hbm, lat_hbm, key_hbm, iq, iw, kl_row,
    dq_hbm, dlat, dkey, diq, dw,
    ask, entry, kl, ids, latr, latq, keyq, pick_own, pick_entry, send, recv, back, comp, keys,
    qp, dqp, gbuf, kt, acc, pacc, s_a, dp_a, ds_a, pl_a, s_b, dp_b, ds_b, pl_b,
    istage, iqr, ex, ex_opp, ex_merged, ex_fin, dsb, dst, ktb, opp_in, merged, fin,
    ikb, ik_opp, ik_merged, ik_fin, ik_acc,
    lat_sem, key_sem, q_sem, g_sem, dq_sem,
    ask_send, ask_recv, a_send, a_recv, r_send, r_recv, ag_send, ag_recv, og_send, og_recv,
    ex_send, ex_recv, d_send, d_recv, rs_send, rs_recv, ik_send, ik_recv,
):
    me, col = lax.axis_index("ctx"), lax.axis_index("head")
    right, left, far = (lax.rem(col + d, NH) for d in (1, 3, 2))
    blocks = latq.shape[0]
    lat_width = latq.shape[2]
    groups, picks = keys.shape[0], keys.shape[1]
    key_count = picks * BLOCK
    pairs = qp.shape[1]
    heads = 2 * pairs
    idx_heads = iw.shape[0]
    idx_scale = LANES ** (-0.5)
    slot_rows = n_ctx * SLOTS * QT

    lat_loads = [
        pltpu.make_async_copy(
            lat_hbm.at[:, pl.ds(n * LANES, LANES)], dqp.at[0, n], lat_sem.at[n]
        )
        for n in range(blocks // 2)
    ]
    mine = pl.ds(pl.multiple_of(col * QT, QT), QT)
    key_load = pltpu.make_async_copy(key_hbm.at[:, mine], keyq, key_sem.at[0])
    stages = (ds_a, pl_a, ds_b, pl_b)
    g_loads = [
        pltpu.make_async_copy(
            g_hbm.at[pl.ds(n * key_count, key_count)], stages[n], g_sem.at[n]
        )
        for n in range(4)
    ]
    for copy in lat_loads + [key_load] + g_loads:
        copy.start()
    slot_tables(history, diag, ask, entry, blocks)
    kl[...] = jnp.broadcast_to(kl_row[...], (LANES, LANES)).T
    greet(n_ctx)
    asks = CtxExchange(n_ctx, ask, ids, (ask_send, ask_recv))
    asks.start()
    ids[me] = ask[me]

    for n, copy in enumerate(lat_loads):
        copy.wait()
        latr[...] = dqp[0, n].T.reshape(2, NH, QT, lat_width)
        latq[2 * n : 2 * n + 2] = latr[:, col]

    row_picks(entry, pick_entry, n_ctx, groups * picks * QT)
    key_load.wait()
    q_loads = [
        pltpu.make_async_copy(q_hbm.at[pl.ds(n * pairs, pairs)], dqp.at[n], q_sem.at[n])
        for n in range(2)
    ]
    for copy in q_loads:
        copy.start()
    asks.finish()
    row_picks(ids, pick_own, n_ctx, blocks * QT)

    gathers = [CtxExchange(n_ctx, send, recv, (a_send, a_recv), c, KEY_COLS[c]) for c in range(2)]
    lat_rows = latq[...].reshape(blocks * QT, lat_width)
    key_rows = keyq[...].reshape(blocks * QT, LANES)
    split = KEY_COLS[0].stop
    first = jnp.concatenate([key_rows, lat_rows[:, : split - LAT.start]], axis=1)
    first = nn(pick_own[...], first).astype(bf16)
    send[:, :, KEY_COLS[0]] = first.reshape(n_ctx, SLOTS * QT, split)
    gathers[0].start()
    pad = jnp.zeros((blocks * QT, WIDTH - LAT.stop), bf16)
    rest = jnp.concatenate([lat_rows[:, split - LAT.start :], pad], axis=1)
    rest = nn(pick_own[...], rest).astype(bf16)
    send[:, :, KEY_COLS[1]] = rest.reshape(n_ctx, SLOTS * QT, WIDTH - split)
    recv[me] = send[me]

    for copy in q_loads:
        copy.wait()

    @pl.loop(0, pairs)
    def _(j):
        one, two = dqp[j // 8, (j % 8) * 2], dqp[j // 8, (j % 8) * 2 + 1]
        qp[0, j] = jnp.concatenate([one[:, :BLOCK], two[:, :BLOCK]], axis=1)
        qp[1, j] = jnp.concatenate([one[:, BLOCK:], two[:, BLOCK:]], axis=1)

    for n in range(4):
        g_loads[n].wait()
        for two in range(2):
            for j in range(2):
                cols = slice((2 * two + j) * LANES, (2 * two + j + 1) * LANES)
                istage[j * key_count : (j + 1) * key_count, :] = stages[n][:, cols].astype(f32)

            @pl.loop(0, heads)
            def _(h):
                for j in range(2):
                    cols = slice((2 * two + j) * LANES, (2 * two + j + 1) * LANES)
                    rows = istage[pl.ds(j * key_count + h, BLOCK // 2, stride=heads), :].astype(bf16)
                    gbuf[n // 2, h, (n % 2) * (BLOCK // 2) : (n % 2 + 1) * (BLOCK // 2), cols] = rows

    istage[...] = iq[...].astype(f32)

    @pl.loop(0, idx_heads)
    def _(h):
        rows = istage[pl.ds(h, groups * BLOCK, stride=idx_heads), :].astype(bf16)
        iqr[0, h] = rows[:BLOCK]
        iqr[1, h] = rows[BLOCK:]

    def head_gathers(sems, groups_of_cols):
        return [
            [
                HeadGather(
                    comp.at[pl.ds(g * picks, picks), :, cols],
                    lambda m, g=g, cols=cols: keys.at[g, :, m, :, cols],
                    sems,
                    (g, c),
                )
                for c, cols in enumerate(groups_of_cols)
            ]
            for g in range(groups)
        ]

    key_gathers = head_gathers((ag_send, ag_recv), KEY_COLS)

    def order_rows(c):
        cols = KEY_COLS[c]
        rows = tn(pick_entry[...], recv[:, :, cols].reshape(slot_rows, cols.stop - cols.start))
        rows = rows.astype(bf16).reshape(groups * picks, QT, cols.stop - cols.start)
        comp[:, :, cols] = rows
        for g in range(groups):
            keys[g, :, col, :, cols] = rows[g * picks : (g + 1) * picks]

    def key_rows_of(g, cols):
        return keys[g, :, :, :, cols].reshape(key_count, cols.stop - cols.start)

    def index_chunk(g, c):
        width = 8 * BLOCK
        rows = iqr[g, 8 * c : 8 * c + 8].reshape(width, LANES)
        v = nt(key_rows_of(g, IDX), rows) * idx_scale
        weight = jnp.concatenate(
            [iw[8 * c + h : 8 * c + h + 1, g * BLOCK : (g + 1) * BLOCK] for h in range(8)], axis=1
        )
        return rows, v, weight

    def query_rows(x):
        flat = x.T
        return flat[:BLOCK] + flat[BLOCK:]

    def index_scores(g):
        total = jnp.zeros((key_count, LANES), f32)
        for c in range(idx_heads // 8):
            _, v, weight = index_chunk(g, c)
            part = v / (1.0 + jnp.exp(-v)) * weight
            for j in range(4):
                total = total + part[:, j * LANES : (j + 1) * LANES]
        ex[g, 1] = query_rows(total).reshape(NH, QT, key_count)

    def row_sums(g, kind):
        return HeadReduce(
            lambda half, m: ex.at[g, kind, m, pl.ds(half * 8, 8)],
            lambda i: ex_opp.at[g, kind, i],
            lambda i: ex_merged.at[g, kind, i],
            lambda i: ex_fin.at[g, kind, i],
            (ex_send, ex_recv),
            (g, kind),
        )

    probs = [row_sums(g, 0) for g in range(groups)]
    scores = [row_sums(g, 1) for g in range(groups)]
    d_rows = [
        HeadGather(dsb.at[g, col], lambda m, g=g: dsb.at[g, m], (d_send, d_recv), (g,)) for g in range(groups)
    ]

    def index_softmax(g):
        probs[g].finish()
        scores[g].finish()
        target = jnp.concatenate([probs[g].total(0), probs[g].total(1)], axis=0) * (1.0 / head_total)
        score = jnp.concatenate([scores[g].total(0), scores[g].total(1)], axis=0)
        q_pos = col * QT + iota((QT, key_count), 0)
        k_pos = iota((QT, key_count), 1) - (key_count - BLOCK)
        score = jnp.where(k_pos <= q_pos, score, -jnp.inf)
        e = jnp.exp(score - jnp.max(score, axis=1, keepdims=True))
        prob = e / jnp.sum(e, axis=1, keepdims=True)
        k_rows = pl.ds(pl.multiple_of(g * BLOCK + col * QT, QT), QT)
        dsb[g, col] = kl[k_rows, 0:1] * (prob - target)
        d_rows[g].start()

    def block_terms(terms, opp, merged, fin, sems, index, g, cols):
        half_picks = picks // 2
        return HeadReduce(
            lambda half, m: terms.at[g, pl.ds(half * half_picks, half_picks), m, :, cols],
            lambda i: opp.at[g, i, :, :, cols],
            lambda i: merged.at[g, i, :, :, cols],
            lambda i: fin.at[g, i, :, :, cols],
            sems,
            index,
        )

    every = slice(0, LANES)
    idx_terms = [
        block_terms(ikb, ik_opp, ik_merged, ik_fin, (ik_send, ik_recv), (g,), g, every) for g in range(groups)
    ]
    lat_cols = (slice(0, 256), slice(256, 640))
    lat_terms = [
        [
            block_terms(ktb, opp_in, merged, fin, (rs_send, rs_recv), (g, c), g, lat_cols[c])
            for c in range(2)
        ]
        for g in range(groups)
    ]

    def index_backward(g):
        d_rows[g].finish()
        grad_rows = dsb[g].reshape(BLOCK, key_count)
        dst[...] = jnp.concatenate([grad_rows, grad_rows], axis=0).T
        key_side = key_rows_of(g, IDX)
        kt_idx = key_side.T
        for c in range(idx_heads // 8):
            rows, v, weight = index_chunk(g, c)
            sig = 1.0 / (1.0 + jnp.exp(-v))
            wide = jnp.concatenate([dst[...]] * 4, axis=1)
            silu = v * sig
            d_weight = jnp.sum(wide * silu, axis=0, keepdims=True)
            for h in range(8):
                dw[8 * c + h : 8 * c + h + 1, g * BLOCK : (g + 1) * BLOCK] = d_weight[
                    :, h * BLOCK : (h + 1) * BLOCK
                ]
            slope = sig + silu * (1.0 - sig)
            grad = (wide * (weight * idx_scale) * slope).astype(bf16)
            iq_grad = nn(kt_idx, grad).T
            for h in range(8):
                istage[pl.ds(g * BLOCK * idx_heads + 8 * c + h, BLOCK, stride=idx_heads), :] = iq_grad[
                    h * BLOCK : (h + 1) * BLOCK
                ]
            part = nt(rows.T, grad)
            if c == 0:
                ik_acc[...] = part
            else:
                ik_acc[...] += part
        for j in range(key_count // LANES):
            part = ik_acc[:, j * LANES : (j + 1) * LANES].astype(bf16).T
            ikb[g, 2 * j : 2 * j + 2] = part.reshape(2, NH, QT, LANES)

    def products(n, buf):
        s, dp = buf[0], buf[1]
        g, c = n // (heads // HC), n % (heads // HC)
        queries = jnp.concatenate([qp[g, c * (HC // 2) + j] for j in range(HC // 2)], axis=1)
        s[...] = nn(key_rows_of(g, LAT), queries)
        dp[...] = nt(key_rows_of(g, VAL), gbuf[g, c * HC : (c + 1) * HC].reshape(R, 512))

    def softmax_passes(buf):
        s, dp, ds, low = buf
        steps = key_count // TT
        edge = key_count - BLOCK
        q_pos = iota((BLOCK, R), 1) % BLOCK
        s[edge:, :] = jnp.where(iota((BLOCK, R), 0) <= q_pos, s[edge:, :], -jnp.inf)

        def at(i):
            return pl.ds(pl.multiple_of(i * TT, TT), TT)

        top = lax.fori_loop(
            0, steps,
            lambda i, m: jnp.maximum(m, fold(s[at(i), :], jnp.max)),
            jnp.full((8, R), -jnp.inf, f32),
            unroll=True,
        )
        top = jnp.max(top, axis=0, keepdims=True)

        def exps(i, sums):
            e = jnp.exp2((s[at(i), :] - top) * EXP_SCALE)
            s[at(i), :] = e
            return sums[0] + fold(e, jnp.sum), sums[1] + fold(e * dp[at(i), :], jnp.sum)

        zero = jnp.zeros((8, R), f32)
        total, dot = lax.fori_loop(0, steps, exps, (zero, zero), unroll=True)
        inv = 1.0 / jnp.sum(total, axis=0, keepdims=True)
        delta = jnp.sum(dot, axis=0, keepdims=True) * inv

        def finish(i, carry):
            p = s[at(i), :] * inv
            low[at(i), :] = p.astype(bf16)
            ds[at(i), :] = (p * (dp[at(i), :] - delta) * SCORE_SCALE).astype(bf16)
            part = p[:, :LANES]
            for j in range(1, R // LANES):
                part = part + p[:, j * LANES : (j + 1) * LANES]
            pacc[at(i), :] += part
            return carry

        lax.fori_loop(0, steps, finish, 0, unroll=True)

    def gradients(n, buf):
        ds, low = buf[2][...], buf[3][...]
        g, c = n // (heads // HC), n % (heads // HC)
        d_queries = nn(kt[LAT, :], ds).astype(bf16)
        for j in range(HC // 2):
            dqp[g, c * (HC // 2) + j] = d_queries[:, j * LANES : (j + 1) * LANES]
        queries = jnp.concatenate([qp[g, c * (HC // 2) + j] for j in range(HC // 2)], axis=1)
        acc[:576, :] += nt(queries, ds)
        acc[:512, :] += nt(gbuf[g, c * HC : (c + 1) * HC].reshape(R, 512).T, low)

    def begin(g):
        kt[...] = key_rows_of(g, slice(0, WIDTH)).T
        acc[...] = jnp.zeros_like(acc)
        pacc[...] = jnp.zeros_like(pacc)

    def send_terms(g):
        for j in range(key_count // LANES):
            part = acc[:, j * LANES : (j + 1) * LANES].astype(bf16).T
            ktb[g, 2 * j : 2 * j + 2] = part.reshape(2, NH, QT, 640)
        lat_terms[g][1].start()

    def sum_terms(reduce, g, cols):
        reduce.finish()
        half = picks // 2
        for i in range(2):
            comp[g * picks + i * half : g * picks + (i + 1) * half, :, cols] = reduce.total(i).astype(bf16)

    def send_probs(g):
        ex[g, 0] = query_rows(pacc[...]).reshape(NH, QT, key_count)
        probs[g].start()

    buf_a, buf_b = (s_a, dp_a, ds_a, pl_a), (s_b, dp_b, ds_b, pl_b)

    half_ctx = n_ctx // 2
    gathers[0].finish(1, half_ctx)
    gathers[1].start()
    gathers[0].finish(half_ctx)
    order_rows(0)
    key_gathers[0][0].start()
    gathers[1].finish(1, half_ctx)
    key_gathers[0][0].forward()
    gathers[1].finish(half_ctx)
    order_rows(1)
    key_gathers[0][1].start()
    key_gathers[0][0].finish()
    index_scores(0)
    key_gathers[0][1].forward()
    key_gathers[1][0].start()
    key_gathers[1][1].start()
    scores[0].start()
    key_gathers[0][1].finish()

    begin(0)
    products(0, buf_a)
    for it in range(4):
        if it == 1:
            key_gathers[1][0].forward()
            key_gathers[1][1].forward()
            scores[0].merge()
        if it == 3:
            probs[0].merge()
            scores[1].merge()
            for c in (1, 0):
                lat_terms[0][c].merge()
        products(2 * it + 1, buf_b)
        softmax_passes(buf_a)
        gradients(2 * it, buf_a)
        if it == 3:
            index_softmax(0)
        softmax_passes(buf_b)
        if it == 1:
            key_gathers[1][0].finish()
            key_gathers[1][1].finish()
        if it < 3:
            products(2 * it + 2, buf_a)
        if it == 3:
            d_rows[0].forward()
        gradients(2 * it + 1, buf_b)
        if it % 2 == 1:
            send_probs(it // 2)
            send_terms(it // 2)
        if it == 1:
            lat_terms[0][0].start()
            begin(1)
            index_scores(1)
            scores[1].start()

    backs = [CtxExchange(n_ctx, send, back, (r_send, r_recv), c, COLS[c]) for c in range(2)]
    entry_rows = groups * picks * QT

    def spread(c):
        rows = nn(pick_entry[...], comp[:, :, COLS[c]].reshape(entry_rows, 384))
        send[:, :, COLS[c]] = rows.astype(bf16).reshape(n_ctx, SLOTS * QT, 384)
        backs[c].start()
        back[me, :, COLS[c]] = send[me, :, COLS[c]]

    own_gathers = head_gathers((og_send, og_recv), COLS)

    def own_sums(c):
        rows = tn(pick_own[...], back[:, :, COLS[c]].reshape(slot_rows, 384))
        rows = rows.astype(bf16).reshape(blocks, QT, 384)
        comp[:, :, COLS[c]] = rows
        for g in range(groups):
            keys[g, :, col, :, COLS[c]] = rows[g * picks : (g + 1) * picks]
            own_gathers[g][c].start()

    def results(c):
        for n in range(blocks // 2):
            g, b = divmod(2 * n, picks)
            part = keys[g, b : b + 2, :, :, COLS[c]].reshape(LANES, 384)
            place = slice(n * LANES, (n + 1) * LANES)
            if c == 0:
                dkey[place, :] = part[:, IDX]
                dlat[:256, place] = part[:, 128:].T
            else:
                dlat[256:, place] = part.T[:320]

    sum_terms(lat_terms[0][1], 0, COLS[1])
    sum_terms(lat_terms[0][0], 0, slice(128, 384))
    probs[1].merge()
    index_backward(0)
    lat_terms[1][1].merge()
    index_softmax(1)
    lat_terms[1][0].start()
    idx_terms[0].start()
    sum_terms(lat_terms[1][1], 1, COLS[1])
    spread(1)
    d_rows[1].forward()
    lat_terms[1][0].merge()
    idx_terms[0].merge()
    index_backward(1)
    idx_terms[1].start()
    sum_terms(lat_terms[1][0], 1, slice(128, 384))
    sum_terms(idx_terms[0], 0, IDX)
    idx_terms[1].merge()
    backs[1].finish()
    own_sums(1)
    sum_terms(idx_terms[1], 1, IDX)
    spread(0)

    @pl.loop(0, pairs)
    def _(j):
        one, two = dqp[0, j], dqp[1, j]
        qp[j // 8, (j % 8) * 2] = jnp.concatenate([one[:, :BLOCK], two[:, :BLOCK]], axis=1)
        qp[j // 8, (j % 8) * 2 + 1] = jnp.concatenate([one[:, BLOCK:], two[:, BLOCK:]], axis=1)

    dq_stores = [
        pltpu.make_async_copy(qp.at[n], dq_hbm.at[pl.ds(n * pairs, pairs)], dq_sem.at[n])
        for n in range(2)
    ]
    for copy in dq_stores:
        copy.start()
    diq[...] = istage[...].astype(bf16)

    backs[0].finish(1, half_ctx)
    for g in range(groups):
        own_gathers[g][1].forward()
    backs[0].finish(half_ctx)
    own_sums(0)
    for g in range(groups):
        own_gathers[g][1].finish()
    results(1)
    for g in range(groups):
        own_gathers[g][0].forward()
    for g in range(groups):
        own_gathers[g][0].finish()
    results(0)
    for copy in dq_stores:
        copy.wait()


def settle_kernel(*refs):
    count = len(refs) // 2
    sems = refs[-1]
    copies = []
    for n, (src, dst) in enumerate(zip(refs[:count], refs[count:-1])):
        parts = 4 if src.shape[0] % 4 == 0 and n == 0 else 1
        size = src.shape[0] // parts
        for part in range(parts):
            rows = pl.ds(part * size, size)
            copies.append(pltpu.make_async_copy(src.at[rows], dst.at[rows], sems.at[len(copies)]))
    for copy in copies:
        copy.start()
    for copy in copies:
        copy.wait()


VM = pl.BlockSpec(memory_space=pltpu.VMEM)
HB = pl.BlockSpec(memory_space=pl.ANY)
SM = pl.BlockSpec(memory_space=pltpu.SMEM)
DMA = pltpu.SemaphoreType.DMA


def shards(
    n_ctx, query_latent, d_out, latent, index_query, index_weight, index_key, kl_scale, history, diag_block
):
    q_dev, heads, lat_width = query_latent.shape
    val_width = d_out.shape[2]
    idx_heads, idx_width = index_query.shape[1:]
    groups, hist = history.shape
    picks = hist + 2
    entries = groups * picks
    key_count = picks * BLOCK
    blk_dev = latent.shape[0] // BLOCK
    shape = jax.ShapeDtypeStruct

    pairs = heads // 2
    chunk = [pltpu.VMEM((key_count, R), t) for t in (f32, f32, bf16, bf16)]
    slots = pltpu.VMEM((n_ctx, SLOTS * QT, WIDTH), bf16)
    results = pl.pallas_call(
        partial(whole_kernel, n_ctx, heads * NH),
        name="sparse_attention_backward",
        in_specs=[SM, SM, HB, HB, HB, HB, VM, VM, VM],
        out_specs=[HB, VM, VM, VM, VM],
        out_shape=[
            shape((heads, lat_width, q_dev), bf16),
            shape((lat_width, blk_dev * BLOCK), bf16),
            shape((blk_dev * BLOCK, idx_width), bf16),
            shape((q_dev * idx_heads, idx_width), bf16),
            shape((idx_heads, q_dev), f32),
        ],
        scratch_shapes=[
            pltpu.VMEM((n_ctx, 8, LANES), i32),
            pltpu.VMEM((n_ctx, 8, LANES), i32),
            pltpu.VMEM((q_dev, LANES), f32),
            pltpu.VMEM((n_ctx, 8, LANES), i32),
            pltpu.VMEM((2, NH, QT, lat_width), bf16),
            pltpu.VMEM((blk_dev, QT, lat_width), bf16),
            pltpu.VMEM((blk_dev, QT, idx_width), bf16),
            pltpu.VMEM((n_ctx * SLOTS * QT, blk_dev * QT), bf16),
            pltpu.VMEM((n_ctx * SLOTS * QT, entries * QT), bf16),
            slots, slots, slots,
            pltpu.VMEM((entries, QT, WIDTH), bf16),
            pltpu.VMEM((groups, picks, NH, QT, WIDTH), bf16),
            pltpu.VMEM((groups, pairs, lat_width, LANES), bf16),
            pltpu.VMEM((groups, pairs, lat_width, LANES), bf16),
            pltpu.VMEM((groups, heads, BLOCK, val_width), bf16),
            pltpu.VMEM((WIDTH, key_count), bf16),
            pltpu.VMEM((640, key_count), f32),
            pltpu.VMEM((key_count, LANES), f32),
            *chunk, *chunk,
            pltpu.VMEM((q_dev * idx_heads, LANES), f32),
            pltpu.VMEM((groups, idx_heads, BLOCK, LANES), bf16),
            pltpu.VMEM((groups, 2, NH, QT, key_count), f32),
            pltpu.VMEM((groups, 2, 2, QT // 2, key_count), f32),
            pltpu.VMEM((groups, 2, 2, QT // 2, key_count), f32),
            pltpu.VMEM((groups, 2, 4, QT // 2, key_count), f32),
            pltpu.VMEM((groups, NH, QT, key_count), f32),
            pltpu.VMEM((key_count, LANES), f32),
            pltpu.VMEM((groups, picks, NH, QT, 640), bf16),
            pltpu.VMEM((groups, 2, picks // 2, QT, 640), bf16),
            pltpu.VMEM((groups, 2, picks // 2, QT, 640), bf16),
            pltpu.VMEM((groups, 4, picks // 2, QT, 640), bf16),
            pltpu.VMEM((groups, picks, NH, QT, LANES), bf16),
            pltpu.VMEM((groups, 2, picks // 2, QT, LANES), bf16),
            pltpu.VMEM((groups, 2, picks // 2, QT, LANES), bf16),
            pltpu.VMEM((groups, 4, picks // 2, QT, LANES), bf16),
            pltpu.VMEM((idx_width, key_count), f32),
            DMA((blk_dev // 2,)), DMA((1,)), DMA((2,)), DMA((4,)), DMA((2,)),
            DMA((n_ctx,)), DMA((n_ctx,)),
            DMA((2, n_ctx)), DMA((2, n_ctx)), DMA((2, n_ctx)), DMA((2, n_ctx)),
            DMA((groups, 2, 4)), DMA((groups, 2, 4)), DMA((groups, 2, 4)), DMA((groups, 2, 4)),
            DMA((groups, 2, 6)), DMA((groups, 2, 6)),
            DMA((groups, 4)), DMA((groups, 4)),
            DMA((groups, 2, 6)), DMA((groups, 2, 6)),
            DMA((groups, 6)), DMA((groups, 6)),
        ],
        compiler_params=pltpu.CompilerParams(
            collective_id=0, has_side_effects=True, vmem_limit_bytes=63 * 2**20
        ),
    )(
        history,
        diag_block,
        jnp.transpose(query_latent, (1, 2, 0)),
        d_out.reshape(q_dev * heads, val_width),
        latent.T,
        index_key.reshape(blk_dev, BLOCK, idx_width),
        index_query.reshape(q_dev * idx_heads, idx_width),
        index_weight.T,
        kl_scale.reshape(1, q_dev),
    )
    d_query, d_lat, d_key, d_iq, d_weight = pl.pallas_call(
        settle_kernel,
        name="settle_results",
        in_specs=[HB] * 5,
        out_specs=[HB] * 5,
        out_shape=[shape(x.shape, x.dtype) for x in results],
        scratch_shapes=[DMA((8,))],
    )(*results)
    return (
        jnp.transpose(d_query, (2, 0, 1)),
        d_lat.T,
        d_iq.reshape(q_dev, idx_heads, idx_width),
        d_weight.T,
        d_key,
    )


def solution(mesh):
    in_specs = (
        P("ctx", "head", None),
        P("ctx", "head", None),
        P("ctx", None),
        P("ctx", "head", None),
        P("ctx", "head"),
        P("ctx", None),
        P("ctx"),
        P("ctx", None),
        P("ctx"),
    )
    out_specs = (
        P("ctx", "head", None),
        P("ctx", None),
        P("ctx", "head", None),
        P("ctx", "head"),
        P("ctx", None),
    )
    body = partial(shards, mesh.shape["ctx"])
    return jax.shard_map(body, mesh=mesh, in_specs=in_specs, out_specs=out_specs, check_vma=False)
```

```python
from functools import partial

import jax
import jax.numpy as jnp
from jax import lax
from jax.experimental import pallas as pl
from jax.experimental.pallas import tpu as pltpu
from jax.sharding import PartitionSpec as P

MESH = pl.DeviceIdType.MESH
f32, bf16, i32 = jnp.float32, jnp.bfloat16, jnp.int32

SCORE_SCALE = 192.0 ** (-0.5)
EXP_SCALE = SCORE_SCALE * 1.4426950408889634
BLOCK = 64
SLOTS = 2
LANES = 128
IDX = slice(0, 128)
LAT = slice(128, 704)
VAL = slice(128, 640)
WIDTH = 768
COLS = (slice(0, 256), slice(256, 512), slice(512, 768))
KEY_COLS = (slice(0, 384), slice(384, 768))
NH = 4
QT = BLOCK // NH
HC = 8
R = HC * BLOCK
TT = 32


def nn(a, b):
    return jnp.dot(a, b, preferred_element_type=f32)


def nt(a, b):
    return lax.dot_general(a, b, (((1,), (1,)), ((), ())), preferred_element_type=f32)


def tn(a, b):
    return lax.dot_general(a, b, (((0,), (0,)), ((), ())), preferred_element_type=f32)


def iota(shape, dim):
    return lax.broadcasted_iota(i32, shape, dim)


def fold(x, op):
    rows, cols = x.shape
    return op(x.reshape(rows // 8, 8, cols), axis=0)


def row_picks(ids, out, n_ctx, width):
    @pl.loop(0, n_ctx)
    def _(r):
        for s in range(SLOTS):
            row = jnp.broadcast_to(ids[r, s : s + 1, :], (QT, LANES)) * QT + iota((QT, LANES), 0)
            wide = jnp.concatenate([row] * (width // LANES), axis=1)
            hit = jnp.where(wide == iota((QT, width), 1), 1.0, 0.0).astype(bf16)
            out[pl.ds(pl.multiple_of((r * SLOTS + s) * QT, QT), QT), :] = hit


def slot_tables(history, diag, ask, entry, blk_dev):
    groups, hist = history.shape
    picks = hist + 2
    lane = iota((8, LANES), 1)
    owner = jnp.where(lane < groups * picks, 0, -1)
    local = jnp.zeros((8, LANES), i32)
    owners = [jnp.int32(0)] * (groups * picks)
    for g in range(groups):
        for k in range(1, picks):
            block = history[g, k - 1] if k <= hist else diag[g]
            e = g * picks + k
            owners[e] = block // blk_dev
            owner = jnp.where(lane == e, owners[e], owner)
            local = jnp.where(lane == e, block % blk_dev, local)
    slot = owner * SLOTS
    for e, one in enumerate(owners):
        slot = slot + jnp.where(lane > e, 1, 0) * jnp.where(owner == one, 1, 0)
    rows = ask.shape[0] * 8
    place = iota((rows, LANES), 0)
    here = jnp.where(place % 8 < SLOTS, place // 8 * SLOTS + place % 8, -9)
    hit = jnp.broadcast_to(slot[:1], (rows, LANES)) == here
    for values, out in ((local, ask), (lane, entry)):
        wide = jnp.broadcast_to((values[:1] + 1).astype(f32), (rows, LANES))
        found = jnp.sum(jnp.where(hit, wide, 0.0), axis=1, keepdims=True) - 1.0
        out[...] = jnp.broadcast_to(found, (rows, LANES)).astype(i32).reshape(out.shape)


def remote(src, dst, sems, index, to):
    send, recv = sems
    return pltpu.make_async_remote_copy(
        src_ref=src,
        dst_ref=dst,
        send_sem=send.at[index],
        recv_sem=recv.at[index],
        device_id=to,
        device_id_type=MESH,
    )


class CtxExchange:
    def __init__(self, n_ctx, src, dst, sems, group=None, cols=None):
        self.n, self.src, self.dst, self.sems, self.group, self.cols = n_ctx, src, dst, sems, group, cols

    def copy(self, d, arrival):
        me, col = lax.axis_index("ctx"), lax.axis_index("head")
        to = lax.rem(me + d, self.n)
        place = lax.rem(me - d + self.n, self.n) if arrival else me
        if self.group is None:
            return remote(self.src.at[to], self.dst.at[place], self.sems, d, (to, col))
        cols = self.cols
        return remote(
            self.src.at[to, :, cols], self.dst.at[place, :, cols], self.sems, (self.group, d), (to, col)
        )

    def start(self):
        @pl.loop(1, self.n)
        def _(d):
            self.copy(d, False).start()

    def finish(self, first=1, last=None):
        @pl.loop(first, last or self.n)
        def _(d):
            copy = self.copy(d, True)
            copy.wait_recv()
            copy.wait_send()


class HeadGather:
    def __init__(self, src, place, sems, index):
        self.src, self.place, self.sems, self.index = src, place, sems, index
        me, col = lax.axis_index("ctx"), lax.axis_index("head")
        self.me, self.col = me, col
        self.right, self.left, self.far = (lax.rem(col + d, NH) for d in (1, 3, 2))

    def copy(self, kind, member):
        to = (self.me, (self.right, self.left)[kind % 2])
        ref = self.place(member)
        if kind < 2:
            return remote(self.src, ref, self.sems, self.index + (kind,), to)
        half = ref.shape[0] // 2
        ref = ref.at[pl.ds((kind - 2) * half, half)]
        return remote(ref, ref, self.sems, self.index + (kind,), to)

    def start(self):
        self.copy(0, self.col).start()
        self.copy(1, self.col).start()

    def forward(self):
        self.copy(0, self.left).wait_recv()
        self.copy(2, self.left).start()
        self.copy(1, self.right).wait_recv()
        self.copy(3, self.right).start()

    def finish(self):
        self.copy(2, self.far).wait_recv()
        self.copy(3, self.far).wait_recv()
        self.copy(0, self.col).wait_send()
        self.copy(1, self.col).wait_send()
        self.copy(2, self.left).wait_send()
        self.copy(3, self.right).wait_send()


class HeadReduce:
    def __init__(self, part, opp, merged, fin, sems, index):
        self.part, self.opp, self.merged, self.fin = part, opp, merged, fin
        self.sems, self.index = sems, index
        me, col = lax.axis_index("ctx"), lax.axis_index("head")
        self.me, self.col = me, col
        self.right, self.left, self.far = (lax.rem(col + d, NH) for d in (1, 3, 2))

    def copy(self, kind):
        to = (self.me, (self.right, self.left, self.right, self.left, self.right, self.left)[kind])
        if kind < 2:
            src, dst = self.part(kind, self.far), self.opp(kind)
        elif kind == 2:
            src, dst = self.part(1, self.right), self.fin(1)
        elif kind == 3:
            src, dst = self.part(0, self.left), self.fin(3)
        else:
            src, dst = self.merged(kind - 4), self.fin(2 * (kind - 4))
        return remote(src, dst, self.sems, self.index + (kind,), to)

    def start(self):
        for kind in range(4):
            self.copy(kind).start()

    def merge(self):
        for half, member in ((0, self.right), (1, self.left)):
            self.copy(half).wait_recv()
            total = self.part(half, member)[...].astype(f32) + self.opp(half)[...].astype(f32)
            out = self.merged(half)
            out[...] = total.astype(out.dtype)
            self.copy(4 + half).start()

    def finish(self):
        for kind in range(2, 6):
            self.copy(kind).wait_recv()
        for kind in range(6):
            self.copy(kind).wait_send()

    def total(self, half):
        a, b = ((0, 3), (1, 2))[half]
        own = self.part(half, self.col)[...].astype(f32)
        return own + self.fin(a)[...].astype(f32) + self.fin(b)[...].astype(f32)


def greet(n_ctx):
    me, col = lax.axis_index("ctx"), lax.axis_index("head")
    barrier = pltpu.get_barrier_semaphore()

    @pl.loop(1, n_ctx)
    def _(d):
        pl.semaphore_signal(
            barrier, inc=1, device_id=(lax.rem(me + d, n_ctx), col), device_id_type=MESH
        )

    for d in range(1, NH):
        pl.semaphore_signal(barrier, inc=1, device_id=(me, lax.rem(col + d, NH)), device_id_type=MESH)
    pl.semaphore_wait(barrier, n_ctx + NH - 2)


def whole_kernel(
    n_ctx, head_total,
    history, diag, q_hbm, g_hbm, lat_hbm, key_hbm, iq, iw, kl_row,
    dq_hbm, dlat, dkey, diq, dw,
    ask, entry, kl, ids, latr, latq, keyq, pick_own, pick_entry, send, recv, back, comp, keys,
    qp, dqp, gbuf, kt, acc, pacc, s_a, dp_a, ds_a, pl_a, s_b, dp_b, ds_b, pl_b,
    istage, iqr, ex, ex_opp, ex_merged, ex_fin, dsb, dst, ktb, opp_in, merged, fin,
    ikb, ik_opp, ik_merged, ik_fin, ik_acc,
    lat_sem, key_sem, q_sem, g_sem, dq_sem,
    ask_send, ask_recv, a_send, a_recv, r_send, r_recv, ag_send, ag_recv, og_send, og_recv,
    ex_send, ex_recv, d_send, d_recv, rs_send, rs_recv, ik_send, ik_recv,
):
    me, col = lax.axis_index("ctx"), lax.axis_index("head")
    right, left, far = (lax.rem(col + d, NH) for d in (1, 3, 2))
    blocks = latq.shape[0]
    lat_width = latq.shape[2]
    groups, picks = keys.shape[0], keys.shape[1]
    key_count = picks * BLOCK
    pairs = qp.shape[1]
    heads = 2 * pairs
    idx_heads = iw.shape[0]
    idx_scale = LANES ** (-0.5)
    slot_rows = n_ctx * SLOTS * QT

    lat_loads = [
        pltpu.make_async_copy(
            lat_hbm.at[:, pl.ds(n * LANES, LANES)], dqp.at[0, n], lat_sem.at[n]
        )
        for n in range(blocks // 2)
    ]
    mine = pl.ds(pl.multiple_of(col * QT, QT), QT)
    key_load = pltpu.make_async_copy(key_hbm.at[:, mine], keyq, key_sem.at[0])
    stages = (ds_a, pl_a, ds_b, pl_b)
    g_loads = [
        pltpu.make_async_copy(
            g_hbm.at[pl.ds(n * key_count, key_count)], stages[n], g_sem.at[n]
        )
        for n in range(4)
    ]
    for copy in lat_loads + [key_load] + g_loads:
        copy.start()
    slot_tables(history, diag, ask, entry, blocks)
    kl[...] = jnp.broadcast_to(kl_row[...], (LANES, LANES)).T
    greet(n_ctx)
    asks = CtxExchange(n_ctx, ask, ids, (ask_send, ask_recv))
    asks.start()
    ids[me] = ask[me]

    for n, copy in enumerate(lat_loads):
        copy.wait()
        latr[...] = dqp[0, n].T.reshape(2, NH, QT, lat_width)
        latq[2 * n : 2 * n + 2] = latr[:, col]

    row_picks(entry, pick_entry, n_ctx, groups * picks * QT)
    key_load.wait()
    q_loads = [
        pltpu.make_async_copy(q_hbm.at[pl.ds(n * pairs, pairs)], dqp.at[n], q_sem.at[n])
        for n in range(2)
    ]
    for copy in q_loads:
        copy.start()
    asks.finish()
    row_picks(ids, pick_own, n_ctx, blocks * QT)

    gathers = [CtxExchange(n_ctx, send, recv, (a_send, a_recv), c, KEY_COLS[c]) for c in range(2)]
    lat_rows = latq[...].reshape(blocks * QT, lat_width)
    key_rows = keyq[...].reshape(blocks * QT, LANES)
    split = KEY_COLS[0].stop
    first = jnp.concatenate([key_rows, lat_rows[:, : split - LAT.start]], axis=1)
    first = nn(pick_own[...], first).astype(bf16)
    send[:, :, KEY_COLS[0]] = first.reshape(n_ctx, SLOTS * QT, split)
    gathers[0].start()
    pad = jnp.zeros((blocks * QT, WIDTH - LAT.stop), bf16)
    rest = jnp.concatenate([lat_rows[:, split - LAT.start :], pad], axis=1)
    rest = nn(pick_own[...], rest).astype(bf16)
    send[:, :, KEY_COLS[1]] = rest.reshape(n_ctx, SLOTS * QT, WIDTH - split)
    recv[me] = send[me]

    for copy in q_loads:
        copy.wait()

    @pl.loop(0, pairs)
    def _(j):
        one, two = dqp[j // 8, (j % 8) * 2], dqp[j // 8, (j % 8) * 2 + 1]
        qp[0, j] = jnp.concatenate([one[:, :BLOCK], two[:, :BLOCK]], axis=1)
        qp[1, j] = jnp.concatenate([one[:, BLOCK:], two[:, BLOCK:]], axis=1)

    for n in range(4):
        g_loads[n].wait()
        for two in range(2):
            for j in range(2):
                cols = slice((2 * two + j) * LANES, (2 * two + j + 1) * LANES)
                istage[j * key_count : (j + 1) * key_count, :] = stages[n][:, cols].astype(f32)

            @pl.loop(0, heads)
            def _(h):
                for j in range(2):
                    cols = slice((2 * two + j) * LANES, (2 * two + j + 1) * LANES)
                    rows = istage[pl.ds(j * key_count + h, BLOCK // 2, stride=heads), :].astype(bf16)
                    gbuf[n // 2, h, (n % 2) * (BLOCK // 2) : (n % 2 + 1) * (BLOCK // 2), cols] = rows

    istage[...] = iq[...].astype(f32)

    @pl.loop(0, idx_heads)
    def _(h):
        rows = istage[pl.ds(h, groups * BLOCK, stride=idx_heads), :].astype(bf16)
        iqr[0, h] = rows[:BLOCK]
        iqr[1, h] = rows[BLOCK:]

    def head_gathers(sems, groups_of_cols):
        return [
            [
                HeadGather(
                    comp.at[pl.ds(g * picks, picks), :, cols],
                    lambda m, g=g, cols=cols: keys.at[g, :, m, :, cols],
                    sems,
                    (g, c),
                )
                for c, cols in enumerate(groups_of_cols)
            ]
            for g in range(groups)
        ]

    key_gathers = head_gathers((ag_send, ag_recv), KEY_COLS)

    def order_rows(c):
        cols = KEY_COLS[c]
        rows = tn(pick_entry[...], recv[:, :, cols].reshape(slot_rows, cols.stop - cols.start))
        rows = rows.astype(bf16).reshape(groups * picks, QT, cols.stop - cols.start)
        comp[:, :, cols] = rows
        for g in range(groups):
            keys[g, :, col, :, cols] = rows[g * picks : (g + 1) * picks]

    def key_rows_of(g, cols):
        return keys[g, :, :, :, cols].reshape(key_count, cols.stop - cols.start)

    def index_chunk(g, c):
        width = 8 * BLOCK
        rows = iqr[g, 8 * c : 8 * c + 8].reshape(width, LANES)
        v = nt(key_rows_of(g, IDX), rows) * idx_scale
        weight = jnp.concatenate(
            [iw[8 * c + h : 8 * c + h + 1, g * BLOCK : (g + 1) * BLOCK] for h in range(8)], axis=1
        )
        return rows, v, weight

    def query_rows(x):
        flat = x.T
        return flat[:BLOCK] + flat[BLOCK:]

    def index_scores(g):
        total = jnp.zeros((key_count, LANES), f32)
        for c in range(idx_heads // 8):
            _, v, weight = index_chunk(g, c)
            part = v / (1.0 + jnp.exp(-v)) * weight
            for j in range(4):
                total = total + part[:, j * LANES : (j + 1) * LANES]
        ex[g, 1] = query_rows(total).reshape(NH, QT, key_count)

    def row_sums(g, kind):
        return HeadReduce(
            lambda half, m: ex.at[g, kind, m, pl.ds(half * 8, 8)],
            lambda i: ex_opp.at[g, kind, i],
            lambda i: ex_merged.at[g, kind, i],
            lambda i: ex_fin.at[g, kind, i],
            (ex_send, ex_recv),
            (g, kind),
        )

    probs = [row_sums(g, 0) for g in range(groups)]
    scores = [row_sums(g, 1) for g in range(groups)]
    d_rows = [
        HeadGather(dsb.at[g, col], lambda m, g=g: dsb.at[g, m], (d_send, d_recv), (g,)) for g in range(groups)
    ]

    def index_softmax(g):
        probs[g].finish()
        scores[g].finish()
        target = jnp.concatenate([probs[g].total(0), probs[g].total(1)], axis=0) * (1.0 / head_total)
        score = jnp.concatenate([scores[g].total(0), scores[g].total(1)], axis=0)
        q_pos = col * QT + iota((QT, key_count), 0)
        k_pos = iota((QT, key_count), 1) - (key_count - BLOCK)
        score = jnp.where(k_pos <= q_pos, score, -jnp.inf)
        e = jnp.exp(score - jnp.max(score, axis=1, keepdims=True))
        prob = e / jnp.sum(e, axis=1, keepdims=True)
        k_rows = pl.ds(pl.multiple_of(g * BLOCK + col * QT, QT), QT)
        dsb[g, col] = kl[k_rows, 0:1] * (prob - target)
        d_rows[g].start()

    def block_terms(terms, opp, merged, fin, sems, index, g, cols):
        half_picks = picks // 2
        return HeadReduce(
            lambda half, m: terms.at[g, pl.ds(half * half_picks, half_picks), m, :, cols],
            lambda i: opp.at[g, i, :, :, cols],
            lambda i: merged.at[g, i, :, :, cols],
            lambda i: fin.at[g, i, :, :, cols],
            sems,
            index,
        )

    every = slice(0, LANES)
    idx_terms = [
        block_terms(ikb, ik_opp, ik_merged, ik_fin, (ik_send, ik_recv), (g,), g, every) for g in range(groups)
    ]
    lat_cols = (slice(0, 128), slice(128, 384), slice(384, 640))
    lat_place = [slice(LAT.start + x.start, LAT.start + x.stop) for x in lat_cols]
    lat_terms = [
        [
            block_terms(ktb, opp_in, merged, fin, (rs_send, rs_recv), (g, c), g, lat_cols[c])
            for c in range(3)
        ]
        for g in range(groups)
    ]

    def index_backward(g):
        d_rows[g].finish()
        grad_rows = dsb[g].reshape(BLOCK, key_count)
        dst[...] = jnp.concatenate([grad_rows, grad_rows], axis=0).T
        key_side = key_rows_of(g, IDX)
        kt_idx = key_side.T
        for c in range(idx_heads // 8):
            rows, v, weight = index_chunk(g, c)
            sig = 1.0 / (1.0 + jnp.exp(-v))
            wide = jnp.concatenate([dst[...]] * 4, axis=1)
            silu = v * sig
            d_weight = jnp.sum(wide * silu, axis=0, keepdims=True)
            for h in range(8):
                dw[8 * c + h : 8 * c + h + 1, g * BLOCK : (g + 1) * BLOCK] = d_weight[
                    :, h * BLOCK : (h + 1) * BLOCK
                ]
            slope = sig + silu * (1.0 - sig)
            grad = (wide * (weight * idx_scale) * slope).astype(bf16)
            iq_grad = nn(kt_idx, grad).T
            for h in range(8):
                istage[pl.ds(g * BLOCK * idx_heads + 8 * c + h, BLOCK, stride=idx_heads), :] = iq_grad[
                    h * BLOCK : (h + 1) * BLOCK
                ]
            part = nt(rows.T, grad)
            if c == 0:
                ik_acc[...] = part
            else:
                ik_acc[...] += part
        for j in range(key_count // LANES):
            part = ik_acc[:, j * LANES : (j + 1) * LANES].astype(bf16).T
            ikb[g, 2 * j : 2 * j + 2] = part.reshape(2, NH, QT, LANES)

    def products(n, buf):
        s, dp = buf[0], buf[1]
        g, c = n // (heads // HC), n % (heads // HC)
        queries = jnp.concatenate([qp[g, c * (HC // 2) + j] for j in range(HC // 2)], axis=1)
        s[...] = nn(key_rows_of(g, LAT), queries)
        dp[...] = nt(key_rows_of(g, VAL), gbuf[g, c * HC : (c + 1) * HC].reshape(R, 512))

    def softmax_passes(buf):
        s, dp, ds, low = buf
        steps = key_count // TT
        edge = key_count - BLOCK
        q_pos = iota((BLOCK, R), 1) % BLOCK
        s[edge:, :] = jnp.where(iota((BLOCK, R), 0) <= q_pos, s[edge:, :], -jnp.inf)

        def at(i):
            return pl.ds(pl.multiple_of(i * TT, TT), TT)

        top = lax.fori_loop(
            0, steps,
            lambda i, m: jnp.maximum(m, fold(s[at(i), :], jnp.max)),
            jnp.full((8, R), -jnp.inf, f32),
            unroll=True,
        )
        top = jnp.max(top, axis=0, keepdims=True)

        def exps(i, sums):
            e = jnp.exp2((s[at(i), :] - top) * EXP_SCALE)
            s[at(i), :] = e
            return sums[0] + fold(e, jnp.sum), sums[1] + fold(e * dp[at(i), :], jnp.sum)

        zero = jnp.zeros((8, R), f32)
        total, dot = lax.fori_loop(0, steps, exps, (zero, zero), unroll=True)
        inv = 1.0 / jnp.sum(total, axis=0, keepdims=True)
        delta = jnp.sum(dot, axis=0, keepdims=True) * inv

        def finish(i, carry):
            p = s[at(i), :] * inv
            low[at(i), :] = p.astype(bf16)
            ds[at(i), :] = (p * (dp[at(i), :] - delta) * SCORE_SCALE).astype(bf16)
            part = p[:, :LANES]
            for j in range(1, R // LANES):
                part = part + p[:, j * LANES : (j + 1) * LANES]
            pacc[at(i), :] += part
            return carry

        lax.fori_loop(0, steps, finish, 0, unroll=True)

    def gradients(n, buf):
        ds, low = buf[2][...], buf[3][...]
        g, c = n // (heads // HC), n % (heads // HC)
        d_queries = nn(kt[LAT, :], ds).astype(bf16)
        for j in range(HC // 2):
            dqp[g, c * (HC // 2) + j] = d_queries[:, j * LANES : (j + 1) * LANES]
        queries = jnp.concatenate([qp[g, c * (HC // 2) + j] for j in range(HC // 2)], axis=1)
        acc[:576, :] += nt(queries, ds)
        acc[:512, :] += nt(gbuf[g, c * HC : (c + 1) * HC].reshape(R, 512).T, low)

    def begin(g):
        kt[...] = key_rows_of(g, slice(0, WIDTH)).T
        acc[...] = jnp.zeros_like(acc)
        pacc[...] = jnp.zeros_like(pacc)

    def send_terms(g):
        for j in range(key_count // LANES):
            part = acc[:, j * LANES : (j + 1) * LANES].astype(bf16).T
            ktb[g, 2 * j : 2 * j + 2] = part.reshape(2, NH, QT, 640)
        lat_terms[g][2].start()

    def sum_terms(reduce, g, cols):
        reduce.finish()
        half = picks // 2
        for i in range(2):
            comp[g * picks + i * half : g * picks + (i + 1) * half, :, cols] = reduce.total(i).astype(bf16)

    def send_probs(g):
        ex[g, 0] = query_rows(pacc[...]).reshape(NH, QT, key_count)
        probs[g].start()

    buf_a, buf_b = (s_a, dp_a, ds_a, pl_a), (s_b, dp_b, ds_b, pl_b)

    half_ctx = n_ctx // 2
    gathers[0].finish(1, half_ctx)
    gathers[1].start()
    gathers[0].finish(half_ctx)
    order_rows(0)
    key_gathers[0][0].start()
    gathers[1].finish(1, half_ctx)
    key_gathers[0][0].forward()
    gathers[1].finish(half_ctx)
    order_rows(1)
    key_gathers[0][1].start()
    key_gathers[0][0].finish()
    index_scores(0)
    key_gathers[0][1].forward()
    key_gathers[1][0].start()
    key_gathers[1][1].start()
    scores[0].start()
    key_gathers[0][1].finish()

    begin(0)
    products(0, buf_a)
    for it in range(4):
        if it == 1:
            key_gathers[1][0].forward()
            key_gathers[1][1].forward()
            scores[0].merge()
        if it == 3:
            probs[0].merge()
            scores[1].merge()
            for c in (2, 1, 0):
                lat_terms[0][c].merge()
        products(2 * it + 1, buf_b)
        softmax_passes(buf_a)
        gradients(2 * it, buf_a)
        if it == 3:
            index_softmax(0)
        softmax_passes(buf_b)
        if it == 1:
            key_gathers[1][0].finish()
            key_gathers[1][1].finish()
        if it < 3:
            products(2 * it + 2, buf_a)
        if it == 3:
            d_rows[0].forward()
        gradients(2 * it + 1, buf_b)
        if it % 2 == 1:
            send_probs(it // 2)
            send_terms(it // 2)
        if it == 1:
            lat_terms[0][1].start()
            lat_terms[0][0].start()
            begin(1)
            index_scores(1)
            scores[1].start()

    backs = [CtxExchange(n_ctx, send, back, (r_send, r_recv), c, COLS[c]) for c in range(3)]
    entry_rows = groups * picks * QT

    def spread(c):
        rows = nn(pick_entry[...], comp[:, :, COLS[c]].reshape(entry_rows, 256))
        send[:, :, COLS[c]] = rows.astype(bf16).reshape(n_ctx, SLOTS * QT, 256)
        backs[c].start()
        back[me, :, COLS[c]] = send[me, :, COLS[c]]

    own_gathers = head_gathers((og_send, og_recv), COLS)

    def own_sums(c):
        rows = tn(pick_own[...], back[:, :, COLS[c]].reshape(slot_rows, 256))
        rows = rows.astype(bf16).reshape(blocks, QT, 256)
        comp[:, :, COLS[c]] = rows
        for g in range(groups):
            keys[g, :, col, :, COLS[c]] = rows[g * picks : (g + 1) * picks]
            own_gathers[g][c].start()

    def results(c):
        for n in range(blocks // 2):
            g, b = divmod(2 * n, picks)
            part = keys[g, b : b + 2, :, :, COLS[c]].reshape(LANES, 256)
            place = slice(n * LANES, (n + 1) * LANES)
            if c == 0:
                dkey[place, :] = part[:, IDX]
                dlat[:128, place] = part[:, 128:].T
            elif c == 1:
                dlat[128:384, place] = part.T
            else:
                dlat[384:, place] = part.T[: lat_width - 384]

    for c in (2, 1, 0):
        sum_terms(lat_terms[0][c], 0, lat_place[c])
    probs[1].merge()
    index_backward(0)
    lat_terms[1][2].merge()
    lat_terms[1][1].start()
    index_softmax(1)
    sum_terms(lat_terms[1][2], 1, lat_place[2])
    spread(2)
    lat_terms[1][1].merge()
    lat_terms[1][0].start()
    idx_terms[0].start()
    d_rows[1].forward()
    sum_terms(lat_terms[1][1], 1, lat_place[1])
    spread(1)
    lat_terms[1][0].merge()
    idx_terms[0].merge()
    index_backward(1)
    idx_terms[1].start()
    sum_terms(lat_terms[1][0], 1, lat_place[0])
    sum_terms(idx_terms[0], 0, IDX)
    idx_terms[1].merge()
    backs[2].finish()
    own_sums(2)
    sum_terms(idx_terms[1], 1, IDX)
    spread(0)

    @pl.loop(0, pairs)
    def _(j):
        one, two = dqp[0, j], dqp[1, j]
        qp[j // 8, (j % 8) * 2] = jnp.concatenate([one[:, :BLOCK], two[:, :BLOCK]], axis=1)
        qp[j // 8, (j % 8) * 2 + 1] = jnp.concatenate([one[:, BLOCK:], two[:, BLOCK:]], axis=1)

    dq_stores = [
        pltpu.make_async_copy(qp.at[n], dq_hbm.at[pl.ds(n * pairs, pairs)], dq_sem.at[n])
        for n in range(2)
    ]
    for copy in dq_stores:
        copy.start()
    diq[...] = istage[...].astype(bf16)

    def all_blocks(step, c):
        for g in range(groups):
            getattr(own_gathers[g][c], step)()

    all_blocks("forward", 2)
    backs[1].finish()
    own_sums(1)
    all_blocks("finish", 2)
    results(2)
    all_blocks("forward", 1)
    backs[0].finish()
    own_sums(0)
    all_blocks("finish", 1)
    results(1)
    all_blocks("forward", 0)
    all_blocks("finish", 0)
    results(0)
    for copy in dq_stores:
        copy.wait()


SETTLE_PARTS = (8, 4, 1, 1, 1)


def settle_kernel(*refs):
    count = len(SETTLE_PARTS)
    srcs, dsts, bufs = refs[:count], refs[count : 2 * count], refs[2 * count : 3 * count]
    in_sem, out_sem = refs[3 * count :]
    ins, outs = [], []
    for src, dst, buf, parts in zip(srcs, dsts, bufs, SETTLE_PARTS):
        size = src.shape[0] // parts
        for part in range(parts):
            rows = pl.ds(part * size, size)
            n = len(ins)
            ins.append(pltpu.make_async_copy(src.at[rows], buf.at[rows], in_sem.at[n]))
            outs.append(pltpu.make_async_copy(buf.at[rows], dst.at[rows], out_sem.at[n]))
    for copy in ins:
        copy.start()
    for copy, after in zip(ins, outs):
        copy.wait()
        after.start()
    for copy in outs:
        copy.wait()


VM = pl.BlockSpec(memory_space=pltpu.VMEM)
HB = pl.BlockSpec(memory_space=pl.ANY)
SM = pl.BlockSpec(memory_space=pltpu.SMEM)
DMA = pltpu.SemaphoreType.DMA


def shards(
    n_ctx, query_latent, d_out, latent, index_query, index_weight, index_key, kl_scale, history, diag_block
):
    q_dev, heads, lat_width = query_latent.shape
    val_width = d_out.shape[2]
    idx_heads, idx_width = index_query.shape[1:]
    groups, hist = history.shape
    picks = hist + 2
    entries = groups * picks
    key_count = picks * BLOCK
    blk_dev = latent.shape[0] // BLOCK
    shape = jax.ShapeDtypeStruct

    pairs = heads // 2
    chunk = [pltpu.VMEM((key_count, R), t) for t in (f32, f32, bf16, bf16)]
    slots = pltpu.VMEM((n_ctx, SLOTS * QT, WIDTH), bf16)
    results = pl.pallas_call(
        partial(whole_kernel, n_ctx, heads * NH),
        name="sparse_attention_backward",
        in_specs=[SM, SM, HB, HB, HB, HB, VM, VM, VM],
        out_specs=[HB, VM, VM, VM, VM],
        out_shape=[
            shape((heads, lat_width, q_dev), bf16),
            shape((lat_width, blk_dev * BLOCK), bf16),
            shape((blk_dev * BLOCK, idx_width), bf16),
            shape((q_dev * idx_heads, idx_width), bf16),
            shape((idx_heads, q_dev), f32),
        ],
        scratch_shapes=[
            pltpu.VMEM((n_ctx, 8, LANES), i32),
            pltpu.VMEM((n_ctx, 8, LANES), i32),
            pltpu.VMEM((q_dev, LANES), f32),
            pltpu.VMEM((n_ctx, 8, LANES), i32),
            pltpu.VMEM((2, NH, QT, lat_width), bf16),
            pltpu.VMEM((blk_dev, QT, lat_width), bf16),
            pltpu.VMEM((blk_dev, QT, idx_width), bf16),
            pltpu.VMEM((n_ctx * SLOTS * QT, blk_dev * QT), bf16),
            pltpu.VMEM((n_ctx * SLOTS * QT, entries * QT), bf16),
            slots, slots, slots,
            pltpu.VMEM((entries, QT, WIDTH), bf16),
            pltpu.VMEM((groups, picks, NH, QT, WIDTH), bf16),
            pltpu.VMEM((groups, pairs, lat_width, LANES), bf16),
            pltpu.VMEM((groups, pairs, lat_width, LANES), bf16),
            pltpu.VMEM((groups, heads, BLOCK, val_width), bf16),
            pltpu.VMEM((WIDTH, key_count), bf16),
            pltpu.VMEM((640, key_count), f32),
            pltpu.VMEM((key_count, LANES), f32),
            *chunk, *chunk,
            pltpu.VMEM((q_dev * idx_heads, LANES), f32),
            pltpu.VMEM((groups, idx_heads, BLOCK, LANES), bf16),
            pltpu.VMEM((groups, 2, NH, QT, key_count), f32),
            pltpu.VMEM((groups, 2, 2, QT // 2, key_count), f32),
            pltpu.VMEM((groups, 2, 2, QT // 2, key_count), f32),
            pltpu.VMEM((groups, 2, 4, QT // 2, key_count), f32),
            pltpu.VMEM((groups, NH, QT, key_count), f32),
            pltpu.VMEM((key_count, LANES), f32),
            pltpu.VMEM((groups, picks, NH, QT, 640), bf16),
            pltpu.VMEM((groups, 2, picks // 2, QT, 640), bf16),
            pltpu.VMEM((groups, 2, picks // 2, QT, 640), bf16),
            pltpu.VMEM((groups, 4, picks // 2, QT, 640), bf16),
            pltpu.VMEM((groups, picks, NH, QT, LANES), bf16),
            pltpu.VMEM((groups, 2, picks // 2, QT, LANES), bf16),
            pltpu.VMEM((groups, 2, picks // 2, QT, LANES), bf16),
            pltpu.VMEM((groups, 4, picks // 2, QT, LANES), bf16),
            pltpu.VMEM((idx_width, key_count), f32),
            DMA((blk_dev // 2,)), DMA((1,)), DMA((2,)), DMA((4,)), DMA((2,)),
            DMA((n_ctx,)), DMA((n_ctx,)),
            DMA((2, n_ctx)), DMA((2, n_ctx)), DMA((3, n_ctx)), DMA((3, n_ctx)),
            DMA((groups, 2, 4)), DMA((groups, 2, 4)), DMA((groups, 3, 4)), DMA((groups, 3, 4)),
            DMA((groups, 2, 6)), DMA((groups, 2, 6)),
            DMA((groups, 4)), DMA((groups, 4)),
            DMA((groups, 3, 6)), DMA((groups, 3, 6)),
            DMA((groups, 6)), DMA((groups, 6)),
        ],
        compiler_params=pltpu.CompilerParams(
            collective_id=0, has_side_effects=True, vmem_limit_bytes=63 * 2**20
        ),
    )(
        history,
        diag_block,
        jnp.transpose(query_latent, (1, 2, 0)),
        d_out.reshape(q_dev * heads, val_width),
        latent.T,
        index_key.reshape(blk_dev, BLOCK, idx_width),
        index_query.reshape(q_dev * idx_heads, idx_width),
        index_weight.T,
        kl_scale.reshape(1, q_dev),
    )
    d_query, d_lat, d_key, d_iq, d_weight = pl.pallas_call(
        settle_kernel,
        name="settle_results",
        in_specs=[HB] * 5,
        out_specs=[HB] * 5,
        out_shape=[shape(x.shape, x.dtype) for x in results],
        scratch_shapes=[pltpu.VMEM(x.shape, x.dtype) for x in results] + [DMA((sum(SETTLE_PARTS),))] * 2,
        compiler_params=pltpu.CompilerParams(vmem_limit_bytes=63 * 2**20),
    )(*results)
    return (
        jnp.transpose(d_query, (2, 0, 1)),
        d_lat.T,
        d_iq.reshape(q_dev, idx_heads, idx_width),
        d_weight.T,
        d_key,
    )


def solution(mesh):
    in_specs = (
        P("ctx", "head", None),
        P("ctx", "head", None),
        P("ctx", None),
        P("ctx", "head", None),
        P("ctx", "head"),
        P("ctx", None),
        P("ctx"),
        P("ctx", None),
        P("ctx"),
    )
    out_specs = (
        P("ctx", "head", None),
        P("ctx", None),
        P("ctx", "head", None),
        P("ctx", "head"),
        P("ctx", None),
    )
    body = partial(shards, mesh.shape["ctx"])
    return jax.shard_map(body, mesh=mesh, in_specs=in_specs, out_specs=out_specs, check_vma=False)
```

```python
from functools import partial

import jax
import jax.numpy as jnp
from jax import lax
from jax.experimental import pallas as pl
from jax.experimental.pallas import tpu as pltpu
from jax.sharding import PartitionSpec as P

MESH = pl.DeviceIdType.MESH
f32, bf16, i32 = jnp.float32, jnp.bfloat16, jnp.int32

SCORE_SCALE = 192.0 ** (-0.5)
EXP_SCALE = SCORE_SCALE * 1.4426950408889634
BLOCK = 64
SLOTS = 2
LANES = 128
IDX = slice(0, 128)
LAT = slice(128, 704)
VAL = slice(128, 640)
WIDTH = 768
COLS = (slice(0, 256), slice(256, 512), slice(512, 768))
KEY_COLS = (slice(0, 384), slice(384, 768))
NH = 4
QT = BLOCK // NH
HC = 8
R = HC * BLOCK
TT = 32


def nn(a, b):
    return jnp.dot(a, b, preferred_element_type=f32)


def nt(a, b):
    return lax.dot_general(a, b, (((1,), (1,)), ((), ())), preferred_element_type=f32)


def tn(a, b):
    return lax.dot_general(a, b, (((0,), (0,)), ((), ())), preferred_element_type=f32)


def iota(shape, dim):
    return lax.broadcasted_iota(i32, shape, dim)


def fold(x, op):
    rows, cols = x.shape
    return op(x.reshape(rows // 8, 8, cols), axis=0)


def row_picks(ids, out, n_ctx, width):
    @pl.loop(0, n_ctx)
    def _(r):
        for s in range(SLOTS):
            row = jnp.broadcast_to(ids[r, s : s + 1, :], (QT, LANES)) * QT + iota((QT, LANES), 0)
            wide = jnp.concatenate([row] * (width // LANES), axis=1)
            hit = jnp.where(wide == iota((QT, width), 1), 1.0, 0.0).astype(bf16)
            out[pl.ds(pl.multiple_of((r * SLOTS + s) * QT, QT), QT), :] = hit


def slot_tables(history, diag, ask, entry, blk_dev):
    groups, hist = history.shape
    picks = hist + 2
    lane = iota((8, LANES), 1)
    owner = jnp.where(lane < groups * picks, 0, -1)
    local = jnp.zeros((8, LANES), i32)
    owners = [jnp.int32(0)] * (groups * picks)
    for g in range(groups):
        for k in range(1, picks):
            block = history[g, k - 1] if k <= hist else diag[g]
            e = g * picks + k
            owners[e] = block // blk_dev
            owner = jnp.where(lane == e, owners[e], owner)
            local = jnp.where(lane == e, block % blk_dev, local)
    slot = owner * SLOTS
    for e, one in enumerate(owners):
        slot = slot + jnp.where(lane > e, 1, 0) * jnp.where(owner == one, 1, 0)
    rows = ask.shape[0] * 8
    place = iota((rows, LANES), 0)
    here = jnp.where(place % 8 < SLOTS, place // 8 * SLOTS + place % 8, -9)
    hit = jnp.broadcast_to(slot[:1], (rows, LANES)) == here
    for values, out in ((local, ask), (lane, entry)):
        wide = jnp.broadcast_to((values[:1] + 1).astype(f32), (rows, LANES))
        found = jnp.sum(jnp.where(hit, wide, 0.0), axis=1, keepdims=True) - 1.0
        out[...] = jnp.broadcast_to(found, (rows, LANES)).astype(i32).reshape(out.shape)


def remote(src, dst, sems, index, to):
    send, recv = sems
    return pltpu.make_async_remote_copy(
        src_ref=src,
        dst_ref=dst,
        send_sem=send.at[index],
        recv_sem=recv.at[index],
        device_id=to,
        device_id_type=MESH,
    )


class CtxExchange:
    def __init__(self, n_ctx, src, dst, sems, group=None, cols=None):
        self.n, self.src, self.dst, self.sems, self.group, self.cols = n_ctx, src, dst, sems, group, cols

    def copy(self, d, arrival):
        me, col = lax.axis_index("ctx"), lax.axis_index("head")
        to = lax.rem(me + d, self.n)
        place = lax.rem(me - d + self.n, self.n) if arrival else me
        if self.group is None:
            return remote(self.src.at[to], self.dst.at[place], self.sems, d, (to, col))
        cols = self.cols
        return remote(
            self.src.at[to, :, cols], self.dst.at[place, :, cols], self.sems, (self.group, d), (to, col)
        )

    def start(self):
        @pl.loop(1, self.n)
        def _(d):
            self.copy(d, False).start()

    def finish(self, first=1, last=None):
        @pl.loop(first, last or self.n)
        def _(d):
            copy = self.copy(d, True)
            copy.wait_recv()
            copy.wait_send()


class HeadGather:
    def __init__(self, src, place, sems, index):
        self.src, self.place, self.sems, self.index = src, place, sems, index
        me, col = lax.axis_index("ctx"), lax.axis_index("head")
        self.me, self.col = me, col
        self.right, self.left, self.far = (lax.rem(col + d, NH) for d in (1, 3, 2))

    def copy(self, kind, member):
        to = (self.me, (self.right, self.left)[kind % 2])
        ref = self.place(member)
        if kind < 2:
            return remote(self.src, ref, self.sems, self.index + (kind,), to)
        half = ref.shape[0] // 2
        ref = ref.at[pl.ds((kind - 2) * half, half)]
        return remote(ref, ref, self.sems, self.index + (kind,), to)

    def start(self):
        self.copy(0, self.col).start()
        self.copy(1, self.col).start()

    def forward(self):
        self.copy(0, self.left).wait_recv()
        self.copy(2, self.left).start()
        self.copy(1, self.right).wait_recv()
        self.copy(3, self.right).start()

    def finish(self):
        self.copy(2, self.far).wait_recv()
        self.copy(3, self.far).wait_recv()
        self.copy(0, self.col).wait_send()
        self.copy(1, self.col).wait_send()
        self.copy(2, self.left).wait_send()
        self.copy(3, self.right).wait_send()


class HeadReduce:
    def __init__(self, part, opp, merged, fin, sems, index):
        self.part, self.opp, self.merged, self.fin = part, opp, merged, fin
        self.sems, self.index = sems, index
        me, col = lax.axis_index("ctx"), lax.axis_index("head")
        self.me, self.col = me, col
        self.right, self.left, self.far = (lax.rem(col + d, NH) for d in (1, 3, 2))

    def copy(self, kind):
        to = (self.me, (self.right, self.left, self.right, self.left, self.right, self.left)[kind])
        if kind < 2:
            src, dst = self.part(kind, self.far), self.opp(kind)
        elif kind == 2:
            src, dst = self.part(1, self.right), self.fin(1)
        elif kind == 3:
            src, dst = self.part(0, self.left), self.fin(3)
        else:
            src, dst = self.merged(kind - 4), self.fin(2 * (kind - 4))
        return remote(src, dst, self.sems, self.index + (kind,), to)

    def start(self):
        for kind in range(4):
            self.copy(kind).start()

    def merge(self):
        for half, member in ((0, self.right), (1, self.left)):
            self.copy(half).wait_recv()
            total = self.part(half, member)[...].astype(f32) + self.opp(half)[...].astype(f32)
            out = self.merged(half)
            out[...] = total.astype(out.dtype)
            self.copy(4 + half).start()

    def finish(self):
        for kind in range(2, 6):
            self.copy(kind).wait_recv()
        for kind in range(6):
            self.copy(kind).wait_send()

    def total(self, half):
        a, b = ((0, 3), (1, 2))[half]
        own = self.part(half, self.col)[...].astype(f32)
        return own + self.fin(a)[...].astype(f32) + self.fin(b)[...].astype(f32)


def greet(n_ctx):
    me, col = lax.axis_index("ctx"), lax.axis_index("head")
    barrier = pltpu.get_barrier_semaphore()

    @pl.loop(1, n_ctx)
    def _(d):
        pl.semaphore_signal(
            barrier, inc=1, device_id=(lax.rem(me + d, n_ctx), col), device_id_type=MESH
        )

    for d in range(1, NH):
        pl.semaphore_signal(barrier, inc=1, device_id=(me, lax.rem(col + d, NH)), device_id_type=MESH)
    pl.semaphore_wait(barrier, n_ctx + NH - 2)


def whole_kernel(
    n_ctx, head_total,
    history, diag, q_hbm, g_hbm, lat_hbm, key_hbm, iq, iw, kl_row,
    dq_hbm, dlat, dkey, diq, dw,
    ask, entry, kl, ids, latr, latq, keyq, pick_own, pick_entry, send, recv, back, comp, keys,
    qp, dqp, gbuf, kt, acc, pacc, s_a, dp_a, ds_a, pl_a, s_b, dp_b, ds_b, pl_b,
    istage, iqr, ex, ex_opp, ex_merged, ex_fin, dsb, dst, ktb, opp_in, merged, fin,
    ikb, ik_opp, ik_merged, ik_fin, ik_acc,
    lat_sem, key_sem, q_sem, g_sem, dq_sem,
    ask_send, ask_recv, a_send, a_recv, r_send, r_recv, ag_send, ag_recv, og_send, og_recv,
    ex_send, ex_recv, d_send, d_recv, rs_send, rs_recv, ik_send, ik_recv,
):
    me, col = lax.axis_index("ctx"), lax.axis_index("head")
    right, left, far = (lax.rem(col + d, NH) for d in (1, 3, 2))
    blocks = latq.shape[0]
    lat_width = latq.shape[2]
    groups, picks = keys.shape[0], keys.shape[1]
    key_count = picks * BLOCK
    pairs = qp.shape[1]
    heads = 2 * pairs
    idx_heads = iw.shape[0]
    idx_scale = LANES ** (-0.5)
    slot_rows = n_ctx * SLOTS * QT

    lat_loads = [
        pltpu.make_async_copy(
            lat_hbm.at[:, pl.ds(n * LANES, LANES)], dqp.at[0, n], lat_sem.at[n]
        )
        for n in range(blocks // 2)
    ]
    mine = pl.ds(pl.multiple_of(col * QT, QT), QT)
    key_load = pltpu.make_async_copy(key_hbm.at[:, mine], keyq, key_sem.at[0])
    stages = (ds_a, pl_a, ds_b, pl_b)
    g_loads = [
        pltpu.make_async_copy(
            g_hbm.at[pl.ds(n * key_count, key_count)], stages[n], g_sem.at[n]
        )
        for n in range(4)
    ]
    for copy in lat_loads + [key_load] + g_loads:
        copy.start()
    slot_tables(history, diag, ask, entry, blocks)
    kl[...] = jnp.broadcast_to(kl_row[...], (LANES, LANES)).T
    greet(n_ctx)
    asks = CtxExchange(n_ctx, ask, ids, (ask_send, ask_recv))
    asks.start()
    ids[me] = ask[me]

    for n, copy in enumerate(lat_loads):
        copy.wait()
        latr[...] = dqp[0, n].T.reshape(2, NH, QT, lat_width)
        latq[2 * n : 2 * n + 2] = latr[:, col]

    row_picks(entry, pick_entry, n_ctx, groups * picks * QT)
    key_load.wait()
    q_loads = [
        pltpu.make_async_copy(q_hbm.at[pl.ds(n * pairs, pairs)], dqp.at[n], q_sem.at[n])
        for n in range(2)
    ]
    for copy in q_loads:
        copy.start()
    asks.finish()
    row_picks(ids, pick_own, n_ctx, blocks * QT)

    gathers = [CtxExchange(n_ctx, send, recv, (a_send, a_recv), c, KEY_COLS[c]) for c in range(2)]
    lat_rows = latq[...].reshape(blocks * QT, lat_width)
    key_rows = keyq[...].reshape(blocks * QT, LANES)
    split = KEY_COLS[0].stop
    first = jnp.concatenate([key_rows, lat_rows[:, : split - LAT.start]], axis=1)
    first = nn(pick_own[...], first).astype(bf16)
    send[:, :, KEY_COLS[0]] = first.reshape(n_ctx, SLOTS * QT, split)
    gathers[0].start()
    pad = jnp.zeros((blocks * QT, WIDTH - LAT.stop), bf16)
    rest = jnp.concatenate([lat_rows[:, split - LAT.start :], pad], axis=1)
    rest = nn(pick_own[...], rest).astype(bf16)
    send[:, :, KEY_COLS[1]] = rest.reshape(n_ctx, SLOTS * QT, WIDTH - split)
    recv[me] = send[me]

    for copy in q_loads:
        copy.wait()

    @pl.loop(0, pairs)
    def _(j):
        one, two = dqp[j // 8, (j % 8) * 2], dqp[j // 8, (j % 8) * 2 + 1]
        qp[0, j] = jnp.concatenate([one[:, :BLOCK], two[:, :BLOCK]], axis=1)
        qp[1, j] = jnp.concatenate([one[:, BLOCK:], two[:, BLOCK:]], axis=1)

    for n in range(4):
        g_loads[n].wait()
        for two in range(2):
            for j in range(2):
                cols = slice((2 * two + j) * LANES, (2 * two + j + 1) * LANES)
                istage[j * key_count : (j + 1) * key_count, :] = stages[n][:, cols].astype(f32)

            @pl.loop(0, heads)
            def _(h):
                for j in range(2):
                    cols = slice((2 * two + j) * LANES, (2 * two + j + 1) * LANES)
                    rows = istage[pl.ds(j * key_count + h, BLOCK // 2, stride=heads), :].astype(bf16)
                    gbuf[n // 2, h, (n % 2) * (BLOCK // 2) : (n % 2 + 1) * (BLOCK // 2), cols] = rows

    istage[...] = iq[...].astype(f32)

    @pl.loop(0, idx_heads)
    def _(h):
        rows = istage[pl.ds(h, groups * BLOCK, stride=idx_heads), :].astype(bf16)
        iqr[0, h] = rows[:BLOCK]
        iqr[1, h] = rows[BLOCK:]

    def head_gathers(sems, groups_of_cols):
        return [
            [
                HeadGather(
                    comp.at[pl.ds(g * picks, picks), :, cols],
                    lambda m, g=g, cols=cols: keys.at[g, :, m, :, cols],
                    sems,
                    (g, c),
                )
                for c, cols in enumerate(groups_of_cols)
            ]
            for g in range(groups)
        ]

    key_gathers = head_gathers((ag_send, ag_recv), KEY_COLS)

    def order_rows(c):
        cols = KEY_COLS[c]
        rows = tn(pick_entry[...], recv[:, :, cols].reshape(slot_rows, cols.stop - cols.start))
        rows = rows.astype(bf16).reshape(groups * picks, QT, cols.stop - cols.start)
        comp[:, :, cols] = rows
        for g in range(groups):
            keys[g, :, col, :, cols] = rows[g * picks : (g + 1) * picks]

    def key_rows_of(g, cols):
        return keys[g, :, :, :, cols].reshape(key_count, cols.stop - cols.start)

    def index_chunk(g, c):
        width = 8 * BLOCK
        rows = iqr[g, 8 * c : 8 * c + 8].reshape(width, LANES)
        v = nt(key_rows_of(g, IDX), rows) * idx_scale
        weight = jnp.concatenate(
            [iw[8 * c + h : 8 * c + h + 1, g * BLOCK : (g + 1) * BLOCK] for h in range(8)], axis=1
        )
        return rows, v, weight

    def query_rows(x):
        flat = x.T
        return flat[:BLOCK] + flat[BLOCK:]

    def index_scores(g):
        total = jnp.zeros((key_count, LANES), f32)
        for c in range(idx_heads // 8):
            _, v, weight = index_chunk(g, c)
            part = v / (1.0 + jnp.exp(-v)) * weight
            for j in range(4):
                total = total + part[:, j * LANES : (j + 1) * LANES]
        ex[g, 1] = query_rows(total).reshape(NH, QT, key_count)

    def row_sums(g, kind):
        return HeadReduce(
            lambda half, m: ex.at[g, kind, m, pl.ds(half * 8, 8)],
            lambda i: ex_opp.at[g, kind, i],
            lambda i: ex_merged.at[g, kind, i],
            lambda i: ex_fin.at[g, kind, i],
            (ex_send, ex_recv),
            (g, kind),
        )

    probs = [row_sums(g, 0) for g in range(groups)]
    scores = [row_sums(g, 1) for g in range(groups)]
    d_rows = [
        HeadGather(dsb.at[g, col], lambda m, g=g: dsb.at[g, m], (d_send, d_recv), (g,)) for g in range(groups)
    ]

    def index_softmax(g):
        probs[g].finish()
        scores[g].finish()
        target = jnp.concatenate([probs[g].total(0), probs[g].total(1)], axis=0) * (1.0 / head_total)
        score = jnp.concatenate([scores[g].total(0), scores[g].total(1)], axis=0)
        q_pos = col * QT + iota((QT, key_count), 0)
        k_pos = iota((QT, key_count), 1) - (key_count - BLOCK)
        score = jnp.where(k_pos <= q_pos, score, -jnp.inf)
        e = jnp.exp(score - jnp.max(score, axis=1, keepdims=True))
        prob = e / jnp.sum(e, axis=1, keepdims=True)
        k_rows = pl.ds(pl.multiple_of(g * BLOCK + col * QT, QT), QT)
        dsb[g, col] = kl[k_rows, 0:1] * (prob - target)
        d_rows[g].start()

    def block_terms(terms, opp, merged, fin, sems, index, g, cols):
        half_picks = picks // 2
        return HeadReduce(
            lambda half, m: terms.at[g, pl.ds(half * half_picks, half_picks), m, :, cols],
            lambda i: opp.at[g, i, :, :, cols],
            lambda i: merged.at[g, i, :, :, cols],
            lambda i: fin.at[g, i, :, :, cols],
            sems,
            index,
        )

    every = slice(0, LANES)
    idx_terms = [
        block_terms(ikb, ik_opp, ik_merged, ik_fin, (ik_send, ik_recv), (g,), g, every) for g in range(groups)
    ]
    lat_cols = (slice(0, 128), slice(128, 384), slice(384, 640))
    lat_place = [slice(LAT.start + x.start, LAT.start + x.stop) for x in lat_cols]
    lat_terms = [
        [
            block_terms(ktb, opp_in, merged, fin, (rs_send, rs_recv), (g, c), g, lat_cols[c])
            for c in range(3)
        ]
        for g in range(groups)
    ]

    def index_backward(g):
        d_rows[g].finish()
        grad_rows = dsb[g].reshape(BLOCK, key_count)
        dst[...] = jnp.concatenate([grad_rows, grad_rows], axis=0).T
        key_side = key_rows_of(g, IDX)
        kt_idx = key_side.T
        for c in range(idx_heads // 8):
            rows, v, weight = index_chunk(g, c)
            sig = 1.0 / (1.0 + jnp.exp(-v))
            wide = jnp.concatenate([dst[...]] * 4, axis=1)
            silu = v * sig
            d_weight = jnp.sum(wide * silu, axis=0, keepdims=True)
            for h in range(8):
                dw[8 * c + h : 8 * c + h + 1, g * BLOCK : (g + 1) * BLOCK] = d_weight[
                    :, h * BLOCK : (h + 1) * BLOCK
                ]
            slope = sig + silu * (1.0 - sig)
            grad = (wide * (weight * idx_scale) * slope).astype(bf16)
            iq_grad = nn(kt_idx, grad).T
            for h in range(8):
                istage[pl.ds(g * BLOCK * idx_heads + 8 * c + h, BLOCK, stride=idx_heads), :] = iq_grad[
                    h * BLOCK : (h + 1) * BLOCK
                ]
            part = nt(rows.T, grad)
            if c == 0:
                ik_acc[...] = part
            else:
                ik_acc[...] += part
        for j in range(key_count // LANES):
            part = ik_acc[:, j * LANES : (j + 1) * LANES].astype(bf16).T
            ikb[g, 2 * j : 2 * j + 2] = part.reshape(2, NH, QT, LANES)

    def products(n, buf):
        s, dp = buf[0], buf[1]
        g, c = n // (heads // HC), n % (heads // HC)
        queries = jnp.concatenate([qp[g, c * (HC // 2) + j] for j in range(HC // 2)], axis=1)
        s[...] = nn(key_rows_of(g, LAT), queries)
        dp[...] = nt(key_rows_of(g, VAL), gbuf[g, c * HC : (c + 1) * HC].reshape(R, 512))

    def softmax_passes(buf):
        s, dp, ds, low = buf
        steps = key_count // TT
        edge = key_count - BLOCK
        q_pos = iota((BLOCK, R), 1) % BLOCK
        s[edge:, :] = jnp.where(iota((BLOCK, R), 0) <= q_pos, s[edge:, :], -jnp.inf)

        def at(i):
            return pl.ds(pl.multiple_of(i * TT, TT), TT)

        top = lax.fori_loop(
            0, steps,
            lambda i, m: jnp.maximum(m, fold(s[at(i), :], jnp.max)),
            jnp.full((8, R), -jnp.inf, f32),
            unroll=True,
        )
        top = jnp.max(top, axis=0, keepdims=True)

        def exps(i, sums):
            e = jnp.exp2((s[at(i), :] - top) * EXP_SCALE)
            s[at(i), :] = e
            return sums[0] + fold(e, jnp.sum), sums[1] + fold(e * dp[at(i), :], jnp.sum)

        zero = jnp.zeros((8, R), f32)
        total, dot = lax.fori_loop(0, steps, exps, (zero, zero), unroll=True)
        inv = 1.0 / jnp.sum(total, axis=0, keepdims=True)
        delta = jnp.sum(dot, axis=0, keepdims=True) * inv

        def finish(i, carry):
            p = s[at(i), :] * inv
            low[at(i), :] = p.astype(bf16)
            ds[at(i), :] = (p * (dp[at(i), :] - delta) * SCORE_SCALE).astype(bf16)
            part = p[:, :LANES]
            for j in range(1, R // LANES):
                part = part + p[:, j * LANES : (j + 1) * LANES]
            pacc[at(i), :] += part
            return carry

        lax.fori_loop(0, steps, finish, 0, unroll=True)

    def gradients(n, buf):
        ds, low = buf[2][...], buf[3][...]
        g, c = n // (heads // HC), n % (heads // HC)
        d_queries = nn(kt[LAT, :], ds).astype(bf16)
        for j in range(HC // 2):
            dqp[g, c * (HC // 2) + j] = d_queries[:, j * LANES : (j + 1) * LANES]
        queries = jnp.concatenate([qp[g, c * (HC // 2) + j] for j in range(HC // 2)], axis=1)
        acc[:576, :] += nt(queries, ds)
        acc[:512, :] += nt(gbuf[g, c * HC : (c + 1) * HC].reshape(R, 512).T, low)

    def begin(g):
        kt[...] = key_rows_of(g, slice(0, WIDTH)).T
        acc[...] = jnp.zeros_like(acc)
        pacc[...] = jnp.zeros_like(pacc)

    def send_terms(g):
        for j in range(key_count // LANES):
            part = acc[:, j * LANES : (j + 1) * LANES].astype(bf16).T
            ktb[g, 2 * j : 2 * j + 2] = part.reshape(2, NH, QT, 640)
        lat_terms[g][2].start()

    def sum_terms(reduce, g, cols):
        reduce.finish()
        half = picks // 2
        for i in range(2):
            comp[g * picks + i * half : g * picks + (i + 1) * half, :, cols] = reduce.total(i).astype(bf16)

    def send_probs(g):
        ex[g, 0] = query_rows(pacc[...]).reshape(NH, QT, key_count)
        probs[g].start()

    buf_a, buf_b = (s_a, dp_a, ds_a, pl_a), (s_b, dp_b, ds_b, pl_b)

    half_ctx = n_ctx // 2
    gathers[0].finish(1, half_ctx)
    gathers[1].start()
    gathers[0].finish(half_ctx)
    order_rows(0)
    key_gathers[0][0].start()
    gathers[1].finish(1, half_ctx)
    key_gathers[0][0].forward()
    gathers[1].finish(half_ctx)
    order_rows(1)
    key_gathers[0][1].start()
    key_gathers[0][0].finish()
    index_scores(0)
    key_gathers[0][1].forward()
    key_gathers[1][0].start()
    key_gathers[1][1].start()
    scores[0].start()
    key_gathers[0][1].finish()

    begin(0)
    products(0, buf_a)
    for it in range(4):
        if it == 1:
            key_gathers[1][0].forward()
            key_gathers[1][1].forward()
            scores[0].merge()
        if it == 3:
            probs[0].merge()
            scores[1].merge()
            for c in (2, 1, 0):
                lat_terms[0][c].merge()
        products(2 * it + 1, buf_b)
        softmax_passes(buf_a)
        gradients(2 * it, buf_a)
        if it == 3:
            index_softmax(0)
        softmax_passes(buf_b)
        if it == 1:
            key_gathers[1][0].finish()
            key_gathers[1][1].finish()
        if it < 3:
            products(2 * it + 2, buf_a)
        if it == 3:
            d_rows[0].forward()
        gradients(2 * it + 1, buf_b)
        if it % 2 == 1:
            send_probs(it // 2)
            send_terms(it // 2)
        if it == 1:
            lat_terms[0][1].start()
            lat_terms[0][0].start()
            begin(1)
            index_scores(1)
            scores[1].start()

    backs = [CtxExchange(n_ctx, send, back, (r_send, r_recv), c, COLS[c]) for c in range(3)]
    entry_rows = groups * picks * QT

    def spread(c):
        rows = nn(pick_entry[...], comp[:, :, COLS[c]].reshape(entry_rows, 256))
        send[:, :, COLS[c]] = rows.astype(bf16).reshape(n_ctx, SLOTS * QT, 256)
        backs[c].start()
        back[me, :, COLS[c]] = send[me, :, COLS[c]]

    own_gathers = head_gathers((og_send, og_recv), COLS)

    def own_sums(c):
        rows = tn(pick_own[...], back[:, :, COLS[c]].reshape(slot_rows, 256))
        rows = rows.astype(bf16).reshape(blocks, QT, 256)
        comp[:, :, COLS[c]] = rows
        for g in range(groups):
            keys[g, :, col, :, COLS[c]] = rows[g * picks : (g + 1) * picks]
            own_gathers[g][c].start()

    def results(c):
        for n in range(blocks // 2):
            g, b = divmod(2 * n, picks)
            part = keys[g, b : b + 2, :, :, COLS[c]].reshape(LANES, 256)
            place = slice(n * LANES, (n + 1) * LANES)
            if c == 0:
                dkey[place, :] = part[:, IDX]
                dlat[:128, place] = part[:, 128:].T
            elif c == 1:
                dlat[128:384, place] = part.T
            else:
                dlat[384:, place] = part.T[: lat_width - 384]

    for c in (2, 1, 0):
        sum_terms(lat_terms[0][c], 0, lat_place[c])
    probs[1].merge()
    index_backward(0)
    lat_terms[1][2].merge()
    lat_terms[1][1].start()
    index_softmax(1)
    sum_terms(lat_terms[1][2], 1, lat_place[2])
    spread(2)
    lat_terms[1][1].merge()
    lat_terms[1][0].start()
    idx_terms[0].start()
    d_rows[1].forward()
    sum_terms(lat_terms[1][1], 1, lat_place[1])
    spread(1)
    lat_terms[1][0].merge()
    idx_terms[0].merge()
    index_backward(1)
    idx_terms[1].start()
    backs[2].finish()
    own_sums(2)
    sum_terms(lat_terms[1][0], 1, lat_place[0])
    sum_terms(idx_terms[0], 0, IDX)
    idx_terms[1].merge()
    sum_terms(idx_terms[1], 1, IDX)
    spread(0)

    @pl.loop(0, pairs)
    def _(j):
        one, two = dqp[0, j], dqp[1, j]
        qp[j // 8, (j % 8) * 2] = jnp.concatenate([one[:, :BLOCK], two[:, :BLOCK]], axis=1)
        qp[j // 8, (j % 8) * 2 + 1] = jnp.concatenate([one[:, BLOCK:], two[:, BLOCK:]], axis=1)

    dq_stores = [
        pltpu.make_async_copy(qp.at[n], dq_hbm.at[pl.ds(n * pairs, pairs)], dq_sem.at[n])
        for n in range(2)
    ]
    for copy in dq_stores:
        copy.start()
    diq[...] = istage[...].astype(bf16)

    def all_blocks(step, c):
        for g in range(groups):
            getattr(own_gathers[g][c], step)()

    all_blocks("forward", 2)
    backs[1].finish()
    own_sums(1)
    all_blocks("finish", 2)
    results(2)
    all_blocks("forward", 1)
    backs[0].finish()
    own_sums(0)
    all_blocks("finish", 1)
    results(1)
    all_blocks("forward", 0)
    all_blocks("finish", 0)
    results(0)
    for copy in dq_stores:
        copy.wait()


SETTLE_PARTS = (8, 4, 1, 1, 1)


def settle_kernel(*refs):
    count = len(SETTLE_PARTS)
    srcs, dsts, bufs = refs[:count], refs[count : 2 * count], refs[2 * count : 3 * count]
    in_sem, out_sem = refs[3 * count :]
    ins, outs = [], []
    for src, dst, buf, parts in zip(srcs, dsts, bufs, SETTLE_PARTS):
        size = src.shape[0] // parts
        for part in range(parts):
            rows = pl.ds(part * size, size)
            n = len(ins)
            ins.append(pltpu.make_async_copy(src.at[rows], buf.at[rows], in_sem.at[n]))
            outs.append(pltpu.make_async_copy(buf.at[rows], dst.at[rows], out_sem.at[n]))
    for copy in ins:
        copy.start()
    for copy, after in zip(ins, outs):
        copy.wait()
        after.start()
    for copy in outs:
        copy.wait()


VM = pl.BlockSpec(memory_space=pltpu.VMEM)
HB = pl.BlockSpec(memory_space=pl.ANY)
SM = pl.BlockSpec(memory_space=pltpu.SMEM)
DMA = pltpu.SemaphoreType.DMA


def shards(
    n_ctx, query_latent, d_out, latent, index_query, index_weight, index_key, kl_scale, history, diag_block
):
    q_dev, heads, lat_width = query_latent.shape
    val_width = d_out.shape[2]
    idx_heads, idx_width = index_query.shape[1:]
    groups, hist = history.shape
    picks = hist + 2
    entries = groups * picks
    key_count = picks * BLOCK
    blk_dev = latent.shape[0] // BLOCK
    shape = jax.ShapeDtypeStruct

    pairs = heads // 2
    chunk = [pltpu.VMEM((key_count, R), t) for t in (f32, f32, bf16, bf16)]
    slots = pltpu.VMEM((n_ctx, SLOTS * QT, WIDTH), bf16)
    results = pl.pallas_call(
        partial(whole_kernel, n_ctx, heads * NH),
        name="sparse_attention_backward",
        in_specs=[SM, SM, HB, HB, HB, HB, VM, VM, VM],
        out_specs=[HB, VM, VM, VM, VM],
        out_shape=[
            shape((heads, lat_width, q_dev), bf16),
            shape((lat_width, blk_dev * BLOCK), bf16),
            shape((blk_dev * BLOCK, idx_width), bf16),
            shape((q_dev * idx_heads, idx_width), bf16),
            shape((idx_heads, q_dev), f32),
        ],
        scratch_shapes=[
            pltpu.VMEM((n_ctx, 8, LANES), i32),
            pltpu.VMEM((n_ctx, 8, LANES), i32),
            pltpu.VMEM((q_dev, LANES), f32),
            pltpu.VMEM((n_ctx, 8, LANES), i32),
            pltpu.VMEM((2, NH, QT, lat_width), bf16),
            pltpu.VMEM((blk_dev, QT, lat_width), bf16),
            pltpu.VMEM((blk_dev, QT, idx_width), bf16),
            pltpu.VMEM((n_ctx * SLOTS * QT, blk_dev * QT), bf16),
            pltpu.VMEM((n_ctx * SLOTS * QT, entries * QT), bf16),
            slots, slots, slots,
            pltpu.VMEM((entries, QT, WIDTH), bf16),
            pltpu.VMEM((groups, picks, NH, QT, WIDTH), bf16),
            pltpu.VMEM((groups, pairs, lat_width, LANES), bf16),
            pltpu.VMEM((groups, pairs, lat_width, LANES), bf16),
            pltpu.VMEM((groups, heads, BLOCK, val_width), bf16),
            pltpu.VMEM((WIDTH, key_count), bf16),
            pltpu.VMEM((640, key_count), f32),
            pltpu.VMEM((key_count, LANES), f32),
            *chunk, *chunk,
            pltpu.VMEM((q_dev * idx_heads, LANES), f32),
            pltpu.VMEM((groups, idx_heads, BLOCK, LANES), bf16),
            pltpu.VMEM((groups, 2, NH, QT, key_count), f32),
            pltpu.VMEM((groups, 2, 2, QT // 2, key_count), f32),
            pltpu.VMEM((groups, 2, 2, QT // 2, key_count), f32),
            pltpu.VMEM((groups, 2, 4, QT // 2, key_count), f32),
            pltpu.VMEM((groups, NH, QT, key_count), f32),
            pltpu.VMEM((key_count, LANES), f32),
            pltpu.VMEM((groups, picks, NH, QT, 640), bf16),
            pltpu.VMEM((groups, 2, picks // 2, QT, 640), bf16),
            pltpu.VMEM((groups, 2, picks // 2, QT, 640), bf16),
            pltpu.VMEM((groups, 4, picks // 2, QT, 640), bf16),
            pltpu.VMEM((groups, picks, NH, QT, LANES), bf16),
            pltpu.VMEM((groups, 2, picks // 2, QT, LANES), bf16),
            pltpu.VMEM((groups, 2, picks // 2, QT, LANES), bf16),
            pltpu.VMEM((groups, 4, picks // 2, QT, LANES), bf16),
            pltpu.VMEM((idx_width, key_count), f32),
            DMA((blk_dev // 2,)), DMA((1,)), DMA((2,)), DMA((4,)), DMA((2,)),
            DMA((n_ctx,)), DMA((n_ctx,)),
            DMA((2, n_ctx)), DMA((2, n_ctx)), DMA((3, n_ctx)), DMA((3, n_ctx)),
            DMA((groups, 2, 4)), DMA((groups, 2, 4)), DMA((groups, 3, 4)), DMA((groups, 3, 4)),
            DMA((groups, 2, 6)), DMA((groups, 2, 6)),
            DMA((groups, 4)), DMA((groups, 4)),
            DMA((groups, 3, 6)), DMA((groups, 3, 6)),
            DMA((groups, 6)), DMA((groups, 6)),
        ],
        compiler_params=pltpu.CompilerParams(
            collective_id=0, has_side_effects=True, vmem_limit_bytes=63 * 2**20
        ),
    )(
        history,
        diag_block,
        jnp.transpose(query_latent, (1, 2, 0)),
        d_out.reshape(q_dev * heads, val_width),
        latent.T,
        index_key.reshape(blk_dev, BLOCK, idx_width),
        index_query.reshape(q_dev * idx_heads, idx_width),
        index_weight.T,
        kl_scale.reshape(1, q_dev),
    )
    d_query, d_lat, d_key, d_iq, d_weight = pl.pallas_call(
        settle_kernel,
        name="settle_results",
        in_specs=[HB] * 5,
        out_specs=[HB] * 5,
        out_shape=[shape(x.shape, x.dtype) for x in results],
        scratch_shapes=[pltpu.VMEM(x.shape, x.dtype) for x in results] + [DMA((sum(SETTLE_PARTS),))] * 2,
        compiler_params=pltpu.CompilerParams(vmem_limit_bytes=63 * 2**20),
    )(*results)
    return (
        jnp.transpose(d_query, (2, 0, 1)),
        d_lat.T,
        d_iq.reshape(q_dev, idx_heads, idx_width),
        d_weight.T,
        d_key,
    )


def solution(mesh):
    in_specs = (
        P("ctx", "head", None),
        P("ctx", "head", None),
        P("ctx", None),
        P("ctx", "head", None),
        P("ctx", "head"),
        P("ctx", None),
        P("ctx"),
        P("ctx", None),
        P("ctx"),
    )
    out_specs = (
        P("ctx", "head", None),
        P("ctx", None),
        P("ctx", "head", None),
        P("ctx", "head"),
        P("ctx", None),
    )
    body = partial(shards, mesh.shape["ctx"])
    return jax.shard_map(body, mesh=mesh, in_specs=in_specs, out_specs=out_specs, check_vma=False)
```
